32 devices in a mesh: blk: 8 (over y, x, core), group: 4 (over z).
Axes of the slice: x: 2, y: 2, z: 4, core: 2. Of those that a mesh axis runs over, the one named last changes fastest.
Arguments:
- tokens: bfloat16 [20, 2048, 512], P('group', 'blk'), may hold values from -6 to 6
- cotangent: bfloat16 [20, 2048, 512], P('group', 'blk')
- lengths: int32 [20], P('group'), may hold values from 128 to 2048, as said below
- ln_params: float32 [4, 512], replicated
- attn_master: float32 [4, 512, 512], P(None, 'blk', 'group')
- attn_first: float32 [4, 512, 512], P(None, 'blk', 'group')
- attn_second: float32 [4, 512, 512], P(None, 'blk', 'group')
- up_master: float32 [512, 2048], P('blk', 'group'), may hold values from -0.25 to 0.25
- up_first: float32 [512, 2048], P('blk', 'group'), may hold values from -768 to 768
- up_second: float32 [512, 2048], P('blk', 'group'), may hold values from 14745.6 to 58982.4
- down_master: float32 [2048, 512], P('blk', 'group'), may hold values from -0.125 to 0.125
- down_first: float32 [2048, 512], P('blk', 'group'), may hold values from -1536 to 1536
- down_second: float32 [2048, 512], P('blk', 'group'), may hold values from 58982.4 to 235929.6
- ln_first: float32 [4, 512], replicated, may hold values from -4096 to 4096
- ln_second: float32 [4, 512], replicated, may hold values from 552960 to 2211840
Outputs:
- block_out: bfloat16 [20, 2048, 512], P('group', 'blk')
- input_grad: float32 [20, 2048, 512], P('group', 'blk')
- attn_moment1: float32 [4, 512, 512], P(None, 'blk', 'group')
- attn_moment2: float32 [4, 512, 512], P(None, 'blk', 'group')
- attn_new: float32 [4, 512, 512], P(None, 'blk', 'group')
- attn_copy: bfloat16 [4, 512, 512], P(None, 'blk', 'group')
- up_moment1: float32 [512, 2048], P('blk', 'group')
- up_moment2: float32 [512, 2048], P('blk', 'group')
- up_new: float32 [512, 2048], P('blk', 'group')
- up_copy: bfloat16 [512, 2048], P('blk', 'group')
- down_moment1: float32 [2048, 512], P('blk', 'group')
- down_moment2: float32 [2048, 512], P('blk', 'group')
- down_new: float32 [2048, 512], P('blk', 'group')
- down_copy: bfloat16 [2048, 512], P('blk', 'group')
- ln_moment1: float32 [4, 512], replicated
- ln_moment2: float32 [4, 512], replicated
- ln_new: float32 [4, 512], replicated
- norms: float32 [2, 6], replicated
The draws below stay inside these ranges and needn't reach their ends.
Inputs may be any that keep to these rules, and one draw needn't show every extreme that they name: `lengths`: in each group of 5 consecutive sequences one, drawn from the seed, has all 2048 positions valid.
All inputs are finite; a program needn't handle non-finite values.
Results may differ from the reference program's by a relative error of at most 0.024.
Values may be sent and summed in bfloat16 or wider, within the bound.
No kernel may reach another device: no remote copies, remote signals or barrier semaphores. Data moves between devices by JAX's collectives and lax.ppermute only.
A program may use at most 192 MiB of HBM per device.

```python
import math
import jax
import jax.numpy as jnp
from jax import lax

D = 512
HEADS = 8
FF = 2048
SPAN = 128
STEP = 5
SEQ_DEV = 5
LENGTH = 2048
SEQS = 20
TOKENS_ALL = 40960


def draw_cotangent(key, part):
    key = jax.random.fold_in(key, 3)
    ramp = jnp.arange(D, dtype=jnp.float32) / (D - 1)
    noise = jax.random.normal(key, (SEQS, LENGTH, D), jnp.float32)
    slope = 1.0 + 2.0 * ramp
    return (noise * slope).astype(jnp.bfloat16)


def draw_lengths(key, part):
    key = jax.random.fold_in(key, 5)
    key_one, key_two = jax.random.split(key)
    drawn = jax.random.randint(key_one, (SEQS,), SPAN, LENGTH + 1)
    chosen = jax.random.randint(key_two, (SEQS // SEQ_DEV,), 0, SEQ_DEV)
    whole = (jnp.arange(SEQ_DEV, dtype=jnp.int32)[None, :] == chosen[:, None]).reshape(SEQS)
    return jnp.where(whole, LENGTH, drawn).astype(jnp.int32)


def draw_ln_params(key, part):
    key = jax.random.fold_in(key, 7)
    key_one, key_two = jax.random.split(key)
    ramp = jnp.arange(D, dtype=jnp.float32) / (D - 1)
    gains = (0.5 + ramp)[None] * jax.random.uniform(key_one, (2, D), jnp.float32, 0.8, 1.25)
    biases = 0.3 * jax.random.normal(key_two, (2, D), jnp.float32)
    return jnp.stack([gains[0], biases[0], gains[1], biases[1]])


def draw_attn_master(key, part):
    key = jax.random.fold_in(key, 11)
    slabs = jnp.array([1.0, 1.0, 1.0, 8.0], jnp.float32)[:, None, None] / math.sqrt(D)
    noise = jax.random.normal(key, (4, D, D), jnp.float32)
    return noise * slabs


def draw_attn_first(key, part):
    key = jax.random.fold_in(key, 13)
    slabs = jnp.array([0.8, 0.8, 3.2, 0.4], jnp.float32)[:, None, None] * math.sqrt(TOKENS_ALL)
    noise = jax.random.normal(key, (4, D, D), jnp.float32)
    return noise * slabs


def draw_attn_second(key, part):
    key = jax.random.fold_in(key, 17)
    slabs = jnp.array([0.625, 0.625, 10.0, 0.156], jnp.float32)[:, None, None] * TOKENS_ALL
    factor = jnp.exp(jax.random.uniform(key, (4, D, D), jnp.float32, 0.0, math.log(4.0)))
    return factor * slabs


def steps_of(rng, shape, pieces, least, largest):
    factor_of = 1.0
    for axis_at, blocks in pieces:
        draws = jax.random.uniform(jax.random.fold_in(jax.random.fold_in(rng, 6), axis_at), (blocks,), jnp.float32, least / len(pieces), largest / len(pieces))
        factor_of = factor_of * jnp.repeat(jnp.exp(draws), shape[axis_at] // blocks).reshape((-1,) + (1,) * (len(shape) - 1 - axis_at))
    return factor_of


def normal_values(rng, shape, width, most, pieces=(), held_as=jnp.bfloat16):
    loudness = steps_of(rng, shape, pieces, -0.22, 0.18) if pieces else 1.0
    entries = jax.random.normal(rng, shape, jnp.float32) * width * loudness
    return jnp.minimum(jnp.maximum(entries, -most), most).astype(held_as)


def setup_inputs(seed: int = 0) -> dict:
    seeds = jax.random.split(jax.random.key(seed), 16)
    return {
        "tokens": normal_values(seeds[0], (SEQS, LENGTH, D), 1.0, 6.0, ((0, 4), (1, 8))),
        "cotangent": draw_cotangent(jax.random.fold_in(seeds[15], 71), 0),
        "lengths": draw_lengths(jax.random.fold_in(seeds[15], 71), 0),
        "ln_params": draw_ln_params(jax.random.fold_in(seeds[15], 71), 0),
        "attn_master": draw_attn_master(jax.random.fold_in(seeds[15], 71), 0),
        "attn_first": draw_attn_first(jax.random.fold_in(seeds[15], 71), 0),
        "attn_second": draw_attn_second(jax.random.fold_in(seeds[15], 71), 0),
        "up_master": normal_values(seeds[7], (D, FF), D ** -0.5, 0.25, ((0, 8), (1, 4)), jnp.float32),
        "up_first": normal_values(seeds[8], (D, FF), (0.6 * TOKENS_ALL ** 0.5), 768.0, ((0, 8), (1, 4)), jnp.float32),
        "up_second": jnp.clip(jnp.exp(math.log(58982.4) - 1.3862944 * jax.random.uniform(seeds[9], (D, FF), jnp.float32) ** steps_of(seeds[9], (D, FF), ((0, 8), (1, 4)), -0.2, 0.2)), 14745.6, 58982.4),
        "down_master": normal_values(seeds[10], (FF, D), FF ** -0.5, 0.125, ((0, 8), (1, 4)), jnp.float32),
        "down_first": normal_values(seeds[11], (FF, D), (1.2 * TOKENS_ALL ** 0.5), 1536.0, ((0, 8), (1, 4)), jnp.float32),
        "down_second": jnp.clip(jnp.exp(math.log(235929.6) - 1.3862944 * jax.random.uniform(seeds[12], (FF, D), jnp.float32) ** steps_of(seeds[12], (FF, D), ((0, 8), (1, 4)), -0.2, 0.2)), 58982.4, 235929.6),
        "ln_first": normal_values(seeds[13], (4, D), (3.7 * TOKENS_ALL ** 0.5), 4096.0, (), jnp.float32),
        "ln_second": jnp.clip(jnp.exp(jax.random.uniform(seeds[14], (4, D), jnp.float32, math.log(552960.0), math.log(2211840))), 552960.0, 2211840),
    }


masked_value = -1e+30

@jax.custom_vjp
def low(v):
    return lax.optimization_barrier(v.astype(jnp.bfloat16)).astype(jnp.float32)

@jax.custom_vjp
def low_back(v):
    return v

def low_keep(v):
    return (low(v), None)

def low_pass(kept, grad):
    return (grad,)

def back_keep(v):
    return (v, None)

def back_low(kept, grad):
    return (low(grad),)
low.defvjp(low_keep, low_pass)
low_back.defvjp(back_keep, back_low)

def layer_norm(values, gain, bias):
    center = values - lax.optimization_barrier(jnp.mean(values, -1, keepdims=True))
    spread = lax.optimization_barrier(jnp.mean(center * center, -1, keepdims=True))
    return center * lax.rsqrt(spread + 1e-05) * gain + bias

def mix_sequence(values, length, attn_weight, up_weight, down_weight, norm_params):
    highest = lax.Precision.HIGHEST
    model_width = values.shape[1]
    head_width = model_width // HEADS
    span_count = LENGTH // SPAN
    factor = head_width ** (-0.5)
    attn_low = low(attn_weight)
    up_low = low(up_weight)
    down_low = low(down_weight)
    normed_in = low(layer_norm(values, norm_params[0], norm_params[1]))

    def project(matrix):
        return low_back(low(jnp.dot(normed_in, matrix, precision=highest)))
    query_rows = project(attn_low[0])
    key_rows = project(attn_low[1])
    value_rows = project(attn_low[2])
    positions = jnp.arange(LENGTH, dtype=jnp.int32)
    valid_span = (positions < length).astype(jnp.float32).reshape(span_count, SPAN)
    counts = lax.optimization_barrier(jnp.sum(valid_span, 1))
    denom = jnp.maximum(counts, 1.0)[:, None]
    key_sum = low(lax.optimization_barrier(jnp.sum(key_rows.reshape(span_count, SPAN, model_width) * valid_span[:, :, None], 1)) / denom)
    value_sum = low(lax.optimization_barrier(jnp.sum(value_rows.reshape(span_count, SPAN, model_width) * valid_span[:, :, None], 1)) / denom)
    query_spans = query_rows.reshape(span_count, SPAN, HEADS, head_width)
    key_spans = key_rows.reshape(span_count, SPAN, HEADS, head_width)
    value_spans = value_rows.reshape(span_count, SPAN, HEADS, head_width)
    local = jnp.einsum('sqhe,skhe->shqk', query_spans, key_spans, precision=highest) * factor
    inner = jnp.arange(SPAN, dtype=jnp.int32)
    local_mask = (inner[None, :] <= inner[:, None])[None, None] & (valid_span[:, None, None, :] > 0.0)
    local = low_back(jnp.where(local_mask, local, masked_value))
    query_heads = query_rows.reshape(LENGTH, HEADS, head_width)
    key_heads = key_sum.reshape(span_count, HEADS, head_width)
    value_heads = value_sum.reshape(span_count, HEADS, head_width)
    summary = jnp.einsum('qhe,nhe->hqn', query_heads, key_heads, precision=highest) * factor
    span_index = jnp.arange(span_count, dtype=jnp.int32)
    summary_mask = (positions[:, None] // SPAN > span_index[None, :]) & (counts[None, :] > 0.0)
    summary = low_back(jnp.where(summary_mask[None], summary, masked_value))
    local_rows = jnp.transpose(local, (1, 0, 2, 3)).reshape(HEADS, LENGTH, SPAN)
    joint = jnp.concatenate([local_rows, summary], -1)
    top = lax.optimization_barrier(jnp.max(joint, -1, keepdims=True))
    log_total = top + jnp.log(lax.optimization_barrier(jnp.sum(jnp.exp(joint - top), -1, keepdims=True)))
    probs = low(jnp.exp(joint - log_total))
    probs_local = probs[:, :, :SPAN].reshape(HEADS, span_count, SPAN, SPAN)
    probs_summary = probs[:, :, SPAN:]
    mixed = jnp.einsum('hsqk,skhe->sqhe', probs_local, value_spans, precision=highest).reshape(LENGTH, model_width)
    mixed = mixed + jnp.einsum('hqn,nhe->qhe', probs_summary, value_heads, precision=highest).reshape(LENGTH, model_width)
    mixed = low_back(low(mixed))
    branch = low_back(jnp.dot(mixed, attn_low[3], precision=highest))
    middle = values + branch
    normed_mid = low(layer_norm(middle, norm_params[2], norm_params[3]))
    up_rows = low_back(jnp.dot(normed_mid, up_low, precision=highest))
    activated = low(jax.nn.gelu(up_rows, approximate=True))
    return middle + low_back(jnp.dot(activated, down_low, precision=highest))

def moments(gradient, first, second):
    corr = 1.0 - 0.5 ** STEP
    new_first = 0.5 * first + 0.5 * gradient
    new_second = 0.5 * second + 0.5 * gradient * gradient
    return (new_first, new_second, new_first / corr / (jnp.sqrt(new_second / corr) + 1e-06))

def reference(tokens, cotangent, lengths, ln_params, attn_master, attn_first, attn_second, up_master, up_first, up_second, down_master, down_first, down_second, ln_first, ln_second):

    def one_sequence(carried, item):
        values, cotan, length = item

        def run_forward(inputs, attn_weight, up_weight, down_weight, norm_params):
            return mix_sequence(inputs, length, attn_weight, up_weight, down_weight, norm_params)
        result, backward = jax.vjp(run_forward, values.astype(jnp.float32), attn_master, up_master, down_master, ln_params)
        grads = backward(cotan.astype(jnp.float32))
        carried = tuple((total + piece for total, piece in zip(carried, grads[1:])))
        return (carried, (result.astype(jnp.bfloat16), grads[0]))
    start = (jnp.zeros_like(attn_master), jnp.zeros_like(up_master), jnp.zeros_like(down_master), jnp.zeros_like(ln_params))
    totals, (block_out, input_grad) = lax.scan(one_sequence, start, (tokens, cotangent, lengths))
    grad_attn, grad_up, grad_down, grad_norm = totals
    attn_moment1, attn_moment2, attn_dir = moments(grad_attn, attn_first, attn_second)
    up_moment1, up_moment2, up_dir = moments(grad_up, up_first, up_second)
    down_moment1, down_moment2, down_dir = moments(grad_down, down_first, down_second)
    ln_moment1, ln_moment2, ln_dir = moments(grad_norm, ln_first, ln_second)
    attn_step = attn_dir + 0.01 * attn_master
    up_step = up_dir + 0.01 * up_master
    down_step = down_dir + 0.01 * down_master
    weight_sq = jnp.concatenate([lax.optimization_barrier(jnp.sum(attn_master * attn_master, (1, 2))), jnp.sum(up_master * up_master)[None], jnp.sum(down_master * down_master)[None]])
    step_sq = jnp.concatenate([lax.optimization_barrier(jnp.sum(attn_step * attn_step, (1, 2))), jnp.sum(up_step * up_step)[None], jnp.sum(down_step * down_step)[None]])
    trust = jnp.sqrt(weight_sq) / jnp.sqrt(step_sq + 1e-06)
    attn_new = attn_master - 0.3 * trust[:4, None, None] * attn_step
    up_new = up_master - 0.3 * trust[4] * up_step
    down_new = down_master - 0.3 * trust[5] * down_step
    ln_new = ln_params - 0.5 * ln_dir
    norms = jnp.stack([jnp.sqrt(weight_sq), jnp.sqrt(step_sq)])
    return (block_out, input_grad, attn_moment1, attn_moment2, attn_new, attn_new.astype(jnp.bfloat16), up_moment1, up_moment2, up_new, up_new.astype(jnp.bfloat16), down_moment1, down_moment2, down_new, down_new.astype(jnp.bfloat16), ln_moment1, ln_moment2, ln_new, norms)
```

```python
import functools

import jax
import jax.numpy as jnp
from jax import lax
from jax.experimental import pallas as pl
from jax.experimental.pallas import tpu as pltpu
from jax.sharding import PartitionSpec as P

HEADS = 8
SPAN = 128
STEP = 5
CHUNKS = 2

masked_value = -1e30
decay_rate = 0.5
matrix_rate = 0.3
vector_rate = 0.5
weight_decay = 0.01
epsilon = 1e-06
gelu_a = 0.7978845608028654
gelu_b = 0.044715

f32 = jnp.float32
b16 = jnp.bfloat16
MIB = 1 << 20
NN = (((1,), (0,)), ((), ()))
NT = (((1,), (1,)), ((), ()))
TN = (((0,), (0,)), ((), ()))


def mm(a, b, dims=NN):
    return lax.dot_general(a, b, dims, preferred_element_type=f32)


def whole():
    return pl.BlockSpec(memory_space=pltpu.VMEM)


def scalars():
    return pl.BlockSpec(memory_space=pltpu.SMEM)


def per_step(*tail):
    zeros = (0,) * len(tail)
    return pl.BlockSpec((1,) + tail, lambda i: (i,) + zeros)


def fixed(*shape):
    zeros = (0,) * len(shape)
    return pl.BlockSpec(shape, lambda i: zeros)


def params(mib):
    return pltpu.CompilerParams(
        dimension_semantics=("arbitrary",), vmem_limit_bytes=mib * MIB
    )


def cost(flops, nbytes, trans=0):
    return pl.CostEstimate(flops=int(flops), bytes_accessed=int(nbytes), transcendentals=int(trans))


def norm_parts(values):
    center = values - jnp.mean(values, -1, keepdims=True)
    spread = jnp.mean(center * center, -1, keepdims=True)
    inverse = lax.rsqrt(spread + 1e-05)
    return center * inverse, inverse


def norm_back(gradient, normal, inverse, gain):
    scaled = gradient * gain
    inner = jnp.mean(scaled, -1, keepdims=True)
    cross = jnp.mean(scaled * normal, -1, keepdims=True)
    return inverse * (scaled - inner - normal * cross)


def copy_attn(w_ref, buf_ref, dims):
    cores, places, groups, rows, cols, width = dims
    for c in range(cores):
        for p in range(places):
            for g in range(groups):
                r0 = (p * cores + c) * rows
                for m in range(4):
                    w_ref[r0 : r0 + rows, m * width + g * cols : m * width + (g + 1) * cols] = (
                        buf_ref[c, p, g, m * rows : (m + 1) * rows, :]
                    )


def prep_kernel(scal_ref, x_ref, g_ref, ln_ref, normed_ref, normed_t_ref, g_t_ref, nsum_ref):
    i = pl.program_id(0)
    tok = x_ref.shape[1]
    spans = tok // SPAN
    normal, _ = norm_parts(x_ref[0].astype(f32))
    normed = (normal * ln_ref[0:1, :] + ln_ref[1:2, :]).astype(b16)
    normed_ref[0] = normed
    normed_t_ref[0] = normed.T
    g_t_ref[0] = g_ref[0].T
    left = scal_ref[1 + i] - scal_ref[0] * tok
    row = lax.broadcasted_iota(jnp.int32, (16, tok), 0)
    col = lax.broadcasted_iota(jnp.int32, (16, tok), 1)
    chosen = jnp.where((col // SPAN == row) & (col < left), 1.0, 0.0)
    amount = jnp.maximum(jnp.sum(chosen, 1, keepdims=True), 1.0)
    total = mm(chosen.astype(b16), normed) / amount
    high = total.astype(b16)
    low = (total - high.astype(f32)).astype(b16)
    nsum_ref[0, 0] = high[:spans]
    nsum_ref[0, 1] = low[:spans]


def pair_masks():
    lane = lax.broadcasted_iota(jnp.int32, (SPAN, SPAN), 1)
    return lane < SPAN // 2


def heads_apart(values):
    lane = lax.broadcasted_iota(jnp.int32, values.shape, 1)
    zero = jnp.zeros_like(values)
    first = lane < SPAN // 2
    return jnp.where(first, values, zero), jnp.where(first, zero, values)


def score_masks(scal_ref, i, span, spans, amount):
    length = scal_ref[1 + i]
    mine = scal_ref[0] * spans + span
    key = lax.broadcasted_iota(jnp.int32, (SPAN, SPAN), 0)
    query = lax.broadcasted_iota(jnp.int32, (SPAN, SPAN), 1)
    local = (key <= query) & (key < length - mine * SPAN)
    index = lax.broadcasted_iota(jnp.int32, (amount, SPAN), 0)
    summary = (index < mine) & (index * SPAN < length)
    return local, summary


def split_scores(scores, local, summary, amount):
    parts = (
        jnp.where(local, scores[:SPAN], masked_value),
        jnp.where(local, scores[SPAN : 2 * SPAN], masked_value),
        jnp.where(summary, scores[2 * SPAN : 2 * SPAN + amount], masked_value),
        jnp.where(summary, scores[2 * SPAN + amount :], masked_value),
    )
    return parts


def forward_kernel(
    dims, scal_ref, normed_ref, x_ref, buf_ref, nsum_ref, ln_ref,
    q_ref, k_ref, v_ref, ks_ref, vs_ref, lse_ref, mixed_ref, x2_ref, mid_ref, mid_t_ref, w_ref,
):
    i = pl.program_id(0)
    width = dims[-1]
    tok = normed_ref.shape[1]
    spans = tok // SPAN
    amount = nsum_ref.shape[2]
    factor = (width // HEADS) ** (-0.5)

    @pl.when(i == 0)
    def _():
        copy_attn(w_ref, buf_ref, dims)

    normed = normed_ref[0]
    q_ref[0] = mm(normed, w_ref[:, :width]).astype(b16)
    k_ref[0] = mm(normed, w_ref[:, width : 2 * width]).astype(b16)
    v_ref[0] = mm(normed, w_ref[:, 2 * width : 3 * width]).astype(b16)
    sums = mm(nsum_ref[0, 0], w_ref[:, width : 3 * width]) + mm(
        nsum_ref[0, 1], w_ref[:, width : 3 * width]
    )
    ks_ref[0] = sums[:, :width].astype(b16)
    vs_ref[0] = sums[:, width:].astype(b16)
    for span in range(spans):
        rows = slice(span * SPAN, (span + 1) * SPAN)
        local, summary = score_masks(scal_ref, i, span, spans, amount)
        for pair in range(width // SPAN):
            lanes = slice(pair * SPAN, (pair + 1) * SPAN)
            query = q_ref[0, rows, lanes] * b16(factor)
            keys = jnp.concatenate(
                heads_apart(k_ref[0, rows, lanes]) + heads_apart(ks_ref[0, :, lanes]), 0
            )
            values = jnp.concatenate(
                heads_apart(v_ref[0, rows, lanes]) + heads_apart(vs_ref[0, :, lanes]), 0
            )
            parts = split_scores(mm(keys, query, NT), local, summary, amount)
            probs = [None] * 4
            for h in range(2):
                here, there = parts[h], parts[2 + h]
                top = jnp.maximum(
                    jnp.max(here, 0, keepdims=True), jnp.max(there, 0, keepdims=True)
                )
                here, there = jnp.exp(here - top), jnp.exp(there - top)
                total = jnp.sum(here, 0, keepdims=True) + jnp.sum(there, 0, keepdims=True)
                inverse = 1.0 / total
                probs[h] = (here * inverse).astype(b16)
                probs[2 + h] = (there * inverse).astype(b16)
                lse_ref[0, span, 2 * pair + h : 2 * pair + h + 1, :] = top + jnp.log(total)
            mixed_ref[0, rows, lanes] = mm(jnp.concatenate(probs, 0), values, TN).astype(b16)
    x2 = x_ref[0].astype(f32) + mm(mixed_ref[0], w_ref[:, 3 * width :])
    x2_ref[0] = x2
    normal, _ = norm_parts(x2)
    mid = (normal * ln_ref[2:3, :] + ln_ref[3:4, :]).astype(b16)
    mid_ref[0] = mid
    mid_t_ref[0] = mid.T


def mlp_kernel(dims, last, *refs):
    if last:
        (mid_ref, mid_t_ref, g_ref, g_t_ref, buf_ref, x2_ref, y_in_ref, gm_in_ref,
         y_ref, gm_ref, out_ref, wu_ref, wd_ref, du_ref, dd_ref) = refs
    else:
        (mid_ref, mid_t_ref, g_ref, g_t_ref, buf_ref,
         y_ref, gm_ref, out_ref, wu_ref, wd_ref, du_ref, dd_ref) = refs
    cores, places, groups, rows, cols, sub, lanes = dims
    i = pl.program_id(0)

    def pieces():
        for c in range(cores):
            for p in range(places):
                b = p * cores + c
                for g in range(groups):
                    for h in range(sub):
                        yield (
                            (c, p, g, slice(h * rows, (h + 1) * rows)),
                            (
                                slice(b * rows, (b + 1) * rows),
                                slice((g * sub + h) * lanes, (g * sub + h + 1) * lanes),
                            ),
                            True,
                        )
                    yield (
                        (c, p, g, slice(sub * rows, sub * rows + cols)),
                        (slice(g * cols, (g + 1) * cols), slice(b * lanes, (b + 1) * lanes)),
                        False,
                    )

    @pl.when(i == 0)
    def _():
        for there, here, is_up in pieces():
            (wu_ref if is_up else wd_ref)[here] = buf_ref[there]
        du_ref[...] = jnp.zeros_like(du_ref)
        dd_ref[...] = jnp.zeros_like(dd_ref)

    mid, g = mid_ref[0], g_ref[0]
    up = mm(mid, wu_ref[...])
    grad_act = mm(g, wd_ref[...])
    square = up * up
    half = 0.5 + 0.5 * jnp.tanh(up * (gelu_a + gelu_a * gelu_b * square))
    act = (up * half).astype(b16)
    slope = half + (up * half * (1.0 - half)) * (
        2.0 * gelu_a + 6.0 * gelu_a * gelu_b * square
    )
    grad_up = (slope * grad_act).astype(b16)
    y = mm(act, wd_ref[...], NT)
    gm = mm(grad_up, wu_ref[...], NT)
    if last:
        y_ref[0] = (x2_ref[0] + y_in_ref[0] + y).astype(b16)
        gm_ref[0] = gm_in_ref[0] + gm
    else:
        y_ref[0] = y
        gm_ref[0] = gm
    dd_ref[...] += mm(g_t_ref[0], act)
    du_ref[...] += mm(mid_t_ref[0], grad_up)

    @pl.when(i == pl.num_programs(0) - 1)
    def _():
        for there, here, is_up in pieces():
            out_ref[there] = (du_ref if is_up else dd_ref)[here].astype(b16)


def backward_kernel(
    dims, scal_ref, gm_ref, g_ref, x2_ref, mixed_ref, q_ref, k_ref, v_ref, lse_ref, ks_ref, vs_ref,
    normed_t_ref, nsum_ref, buf_ref, ln_ref,
    gx2_ref, dqkv_ref, out_ref, hpart_ref, lng_ref, w_ref, dw_ref, do_ref,
):
    i = pl.program_id(0)
    cores, places, groups, wrows, cols, width = dims
    tok = g_ref.shape[1]
    spans = tok // SPAN
    amount = ks_ref.shape[1]
    factor = (width // HEADS) ** (-0.5)

    @pl.when(i == 0)
    def _():
        copy_attn(w_ref, buf_ref, dims)
        dw_ref[...] = jnp.zeros_like(dw_ref)
        lng_ref[...] = jnp.zeros_like(lng_ref)

    gm = gm_ref[0]
    normal, inverse = norm_parts(x2_ref[0])
    lng_ref[0:1, :] += jnp.sum(gm * normal, 0, keepdims=True)
    lng_ref[1:2, :] += jnp.sum(gm, 0, keepdims=True)
    gx2 = g_ref[0].astype(f32) + norm_back(gm, normal, inverse, ln_ref[2:3, :])
    gx2_ref[0] = gx2
    branch = gx2.astype(b16)
    dw_ref[:, 3 * width :] += mm(mixed_ref[0], branch, TN)
    do_ref[...] = mm(branch, w_ref[:, 3 * width :], NT).astype(b16)
    key_parts, value_parts = [], []
    for span in range(spans):
        rows = slice(span * SPAN, (span + 1) * SPAN)
        local, summary = score_masks(scal_ref, i, span, spans, amount)
        for pair in range(width // SPAN):
            lanes = slice(pair * SPAN, (pair + 1) * SPAN)
            query = q_ref[0, rows, lanes] * b16(factor)
            grad = do_ref[rows, lanes]
            keys = jnp.concatenate(
                heads_apart(k_ref[0, rows, lanes]) + heads_apart(ks_ref[0, :, lanes]), 0
            )
            values = jnp.concatenate(
                heads_apart(v_ref[0, rows, lanes]) + heads_apart(vs_ref[0, :, lanes]), 0
            )
            scores = split_scores(mm(keys, query, NT), local, summary, amount)
            grads = mm(values, grad, NT)
            grads = (
                grads[:SPAN],
                grads[SPAN : 2 * SPAN],
                grads[2 * SPAN : 2 * SPAN + amount],
                grads[2 * SPAN + amount :],
            )
            low, back = [None] * 4, [None] * 4
            for h in range(2):
                total = lse_ref[0, span, 2 * pair + h : 2 * pair + h + 1, :]
                here, there = jnp.exp(scores[h] - total), jnp.exp(scores[2 + h] - total)
                here_grad, there_grad = here * grads[h], there * grads[2 + h]
                dot = jnp.sum(here_grad, 0, keepdims=True) + jnp.sum(there_grad, 0, keepdims=True)
                low[h], low[2 + h] = here.astype(b16), there.astype(b16)
                back[h] = (here_grad - here * dot).astype(b16)
                back[2 + h] = (there_grad - there * dot).astype(b16)
            low_rows = jnp.concatenate(
                [jnp.concatenate(low[0:2], 1), jnp.concatenate(low[2:4], 1)], 0
            )
            back_rows = jnp.concatenate(
                [jnp.concatenate(back[0:2], 1), jnp.concatenate(back[2:4], 1)], 0
            )
            grad_value = mm(low_rows, jnp.concatenate(heads_apart(grad), 0))
            grad_key = mm(back_rows, jnp.concatenate(heads_apart(query), 0))
            grad_query = mm(jnp.concatenate(back, 0), keys, TN) * factor
            dqkv_ref[0, rows, lanes] = grad_query.astype(b16)
            dqkv_ref[0, rows, width + pair * SPAN : width + (pair + 1) * SPAN] = grad_key[
                :SPAN
            ].astype(b16)
            dqkv_ref[0, rows, 2 * width + pair * SPAN : 2 * width + (pair + 1) * SPAN] = grad_value[
                :SPAN
            ].astype(b16)
            key_parts.append(grad_key[SPAN:])
            value_parts.append(grad_value[SPAN:])
    pairs = width // SPAN

    def joined(parts):
        return jnp.concatenate(
            [sum(parts[s * pairs + p] for s in range(spans)) for p in range(pairs)], 1
        ).astype(b16)

    key_part, value_part = joined(key_parts), joined(value_parts)
    hpart_ref[0] = (
        mm(key_part, w_ref[:, width : 2 * width], NT)
        + mm(value_part, w_ref[:, 2 * width : 3 * width], NT)
    ).astype(b16)
    dw_ref[:, : 3 * width] += mm(normed_t_ref[0], dqkv_ref[0])
    nsum = nsum_ref[0, 0]
    dw_ref[:, width : 2 * width] += mm(nsum, key_part, TN)
    dw_ref[:, 2 * width : 3 * width] += mm(nsum, value_part, TN)

    @pl.when(i == pl.num_programs(0) - 1)
    def _():
        for c in range(cores):
            for p in range(places):
                r0 = (p * cores + c) * wrows
                for g in range(groups):
                    for m in range(4):
                        out_ref[c, p, g, m * wrows : (m + 1) * wrows, :] = dw_ref[
                            r0 : r0 + wrows, m * width + g * cols : m * width + (g + 1) * cols
                        ].astype(b16)


def input_kernel(
    dims, scal_ref, dqkv_ref, gx2_ref, x_ref, buf_ref, own_ref, ln_ref, out_ref, lng_ref, w_ref
):
    i = pl.program_id(0)
    width = dims[-1]
    tok = x_ref.shape[1]

    @pl.when(i == 0)
    def _():
        copy_attn(w_ref, buf_ref, dims)
        lng_ref[...] = jnp.zeros_like(lng_ref)

    grad = mm(dqkv_ref[0], w_ref[:, : 3 * width], NT)
    left = scal_ref[1 + i] - scal_ref[0] * tok
    place = lax.broadcasted_iota(jnp.int32, (tok, 1), 0)
    extra = []
    for span in range(tok // SPAN):
        rows = slice(span * SPAN, (span + 1) * SPAN)
        amount = jnp.clip(left - span * SPAN, 0, SPAN)
        share = jnp.where(place[rows] < left, 1.0, 0.0) / jnp.maximum(amount, 1).astype(f32)
        extra.append(share * own_ref[0, span : span + 1, :])
    grad = grad + jnp.concatenate(extra, 0)
    normal, inverse = norm_parts(x_ref[0].astype(f32))
    lng_ref[0:1, :] += jnp.sum(grad * normal, 0, keepdims=True)
    lng_ref[1:2, :] += jnp.sum(grad, 0, keepdims=True)
    out_ref[0] = gx2_ref[0] + norm_back(grad, normal, inverse, ln_ref[0:1, :])


def moments(gradient, first, second):
    corr = 1.0 - decay_rate**STEP
    new_first = decay_rate * first + (1.0 - decay_rate) * gradient
    new_second = decay_rate * second + (1.0 - decay_rate) * gradient * gradient
    return (new_first, new_second, new_first / corr / (jnp.sqrt(new_second / corr) + epsilon))


def fast_mesh(nb, ng, width):
    return nb == 8 and ng == 4 and width // ng == 128


def shift(values, by, ng):
    return lax.ppermute(values, "group", [(j, (j + by) % ng) for j in range(ng)])


def cross(values, bit, nb):
    return lax.ppermute(values, "blk", [(j, j ^ bit) for j in range(nb)])


def put(buffer, piece, at):
    return lax.dynamic_update_slice(buffer, piece[None], (at,) + (0,) * piece.ndim)


def take(buffer, at):
    return lax.dynamic_index_in_dim(buffer, at, 0, keepdims=False)


def gather_group(piece, place, ng):
    out = put(jnp.zeros((ng,) + piece.shape, piece.dtype), piece, place)
    for by in range(1, ng):
        out = put(out, shift(piece, by, ng), (place - by) % ng)
    return out


def gather_blk(piece, place, nb):
    spot, core = place // 2, place % 2
    out = put(jnp.zeros((nb // 2,) + piece.shape, piece.dtype), piece, spot)
    for move in range(1, nb // 2):
        out = put(out, cross(piece, 2 * move, nb), spot ^ move)
    other = cross(out, 1, nb)
    both = jnp.zeros((2,) + out.shape, out.dtype)
    return put(put(both, out, core), other, 1 - core)


def reduce_all(pieces, b, z, nb, ng):
    spot, core = b // 2, b % 2
    sent = cross(take(pieces, 1 - core), 1, nb)
    kept = take(pieces, core)

    def at(index):
        return take(kept, index).astype(f32) + take(sent, index).astype(f32)

    total = at(spot)
    for move in range(1, nb // 2):
        total = total + cross(at(spot ^ move).astype(b16), 2 * move, nb).astype(f32)
    total = total.astype(b16)
    out = take(total, z).astype(f32)
    for by in range(1, ng):
        out = out + shift(take(total, (z + by) % ng), by, ng).astype(f32)
    return out


def body(
    tokens, cotangent, lengths, ln_params, attn_master, attn_first, attn_second,
    up_master, up_first, up_second, down_master, down_first, down_second, ln_first, ln_second,
    *, nb, ng,
):
    seqs, tok, width = tokens.shape
    spans = tok // SPAN
    amount = nb * spans
    rows, cols = attn_master.shape[1:]
    ff_rows = down_master.shape[0]
    sub = nb // ng
    lanes = ff_rows // CHUNKS
    inner = nb * lanes
    b, z = lax.axis_index("blk"), lax.axis_index("group")
    fast = fast_mesh(nb, ng, width)
    scal = jnp.concatenate([b.astype(jnp.int32)[None], lengths.astype(jnp.int32)])
    seq = jax.ShapeDtypeStruct

    def rows_like(dtype, *tail):
        return seq((seqs,) + tail, dtype)

    attn_piece = attn_master.astype(b16).reshape(4 * rows, cols)
    up_low = up_master.astype(b16).reshape(rows, sub, CHUNKS, lanes)
    down_low = down_master.astype(b16).T.reshape(cols, CHUNKS, lanes)
    mlp_pieces = [
        jnp.concatenate(
            [jnp.swapaxes(up_low[:, :, j], 0, 1).reshape(sub * rows, lanes), down_low[:, j]], 0
        )
        for j in range(CHUNKS)
    ]

    normed, normed_t, cot_t, nsum = pl.pallas_call(
        prep_kernel,
        grid=(seqs,),
        in_specs=[scalars(), per_step(tok, width), per_step(tok, width), fixed(4, width)],
        out_specs=[
            per_step(tok, width), per_step(width, tok), per_step(width, tok),
            per_step(2, spans, width),
        ],
        out_shape=[
            rows_like(b16, tok, width), rows_like(b16, width, tok), rows_like(b16, width, tok),
            rows_like(b16, 2, spans, width),
        ],
        compiler_params=params(16),
        cost_estimate=cost(4e7, 5 * 5 * tok * width * 2),
        name="prep",
    )(scal, tokens, cotangent, ln_params)

    if fast:
        extra = nsum.reshape(-1, cols)
        attn_z = gather_group(attn_piece, z, ng).reshape(ng * 4 * rows, cols)
        attn_all = gather_blk(jnp.concatenate([attn_z, extra], 0), b, nb)
        main = ng * 4 * rows
        attn_buf = attn_all[:, :, :main].reshape(2, nb // 2, ng, 4 * rows, cols)
        nsum_all = attn_all[:, :, main:].reshape(2, nb // 2, seqs, 2, spans, width)
        nsum_all = jnp.transpose(nsum_all, (2, 3, 1, 0, 4, 5)).reshape(seqs, 2, amount, width)
        mlp_bufs = [gather_blk(gather_group(piece, z, ng), b, nb) for piece in mlp_pieces]
    else:

        def gather_any(piece):
            every = lax.all_gather(piece, ("blk", "group"))
            every = every.reshape((nb // 2, 2, ng) + piece.shape)
            return jnp.swapaxes(every, 0, 1)

        attn_buf = gather_any(attn_piece)
        mlp_bufs = [gather_any(piece) for piece in mlp_pieces]
        nsum_all = lax.all_gather(nsum, "blk", axis=2, tiled=True)

    def reduce_any(pieces):
        if fast:
            return reduce_all(pieces, b, z, nb, ng)
        pieces = jnp.swapaxes(pieces, 0, 1).reshape((nb,) + pieces.shape[2:])
        pieces = lax.psum_scatter(pieces, "blk", scatter_dimension=0)
        return lax.psum_scatter(pieces, "group", scatter_dimension=0).astype(f32)

    dims = (2, nb // 2, ng, rows, cols, width)
    act_bytes = seqs * tok * width
    q, k, v, ks, vs, lse, mixed, x2, mid, mid_t = pl.pallas_call(
        functools.partial(forward_kernel, dims),
        grid=(seqs,),
        in_specs=[
            scalars(), per_step(tok, width), per_step(tok, width), whole(),
            per_step(2, amount, width), fixed(4, width),
        ],
        out_specs=[
            per_step(tok, width), per_step(tok, width), per_step(tok, width),
            per_step(amount, width), per_step(amount, width), per_step(spans, HEADS, SPAN),
            per_step(tok, width), per_step(tok, width), per_step(tok, width),
            per_step(width, tok),
        ],
        out_shape=[
            rows_like(b16, tok, width), rows_like(b16, tok, width), rows_like(b16, tok, width),
            rows_like(b16, amount, width), rows_like(b16, amount, width),
            rows_like(f32, spans, HEADS, SPAN),
            rows_like(b16, tok, width), rows_like(f32, tok, width), rows_like(b16, tok, width),
            rows_like(b16, width, tok),
        ],
        scratch_shapes=[pltpu.VMEM((width, 4 * width), b16)],
        compiler_params=params(24),
        cost_estimate=cost(8e9, act_bytes * 18),
        name="forward",
    )(scal, normed, tokens, attn_buf, nsum_all, ln_params)

    mlp_dims = (2, nb // 2, ng, rows, cols, sub, lanes)
    mlp_out = seq((2, nb // 2, ng, sub * rows + cols, lanes), b16)
    grads = []
    y = gm = None
    for j in range(CHUNKS):
        last = j == CHUNKS - 1
        args = [mid, mid_t, cotangent, cot_t, mlp_bufs[j]]
        in_specs = [
            per_step(tok, width), per_step(width, tok), per_step(tok, width),
            per_step(width, tok), whole(),
        ]
        if last:
            args += [x2, y, gm]
            in_specs += [per_step(tok, width)] * 3
        y, gm, part = pl.pallas_call(
            functools.partial(mlp_kernel, mlp_dims, last),
            grid=(seqs,),
            in_specs=in_specs,
            out_specs=[per_step(tok, width), per_step(tok, width), whole()],
            out_shape=[
                rows_like(b16 if last else f32, tok, width), rows_like(f32, tok, width), mlp_out
            ],
            scratch_shapes=[
                pltpu.VMEM((width, inner), b16), pltpu.VMEM((width, inner), b16),
                pltpu.VMEM((width, inner), f32), pltpu.VMEM((width, inner), f32),
            ],
            compiler_params=params(32),
            cost_estimate=cost(9e9, act_bytes * 20),
            name="mlp",
        )(*args)
        grads.append(part)
    block_out = y

    gx2, dqkv, attn_part, hpart, ln_two = pl.pallas_call(
        functools.partial(backward_kernel, dims),
        grid=(seqs,),
        in_specs=[
            scalars(), per_step(tok, width), per_step(tok, width), per_step(tok, width),
            per_step(tok, width), per_step(tok, width), per_step(tok, width), per_step(tok, width),
            per_step(spans, HEADS, SPAN), per_step(amount, width), per_step(amount, width),
            per_step(width, tok), per_step(2, amount, width), whole(), fixed(4, width),
        ],
        out_specs=[
            per_step(tok, width), per_step(tok, 3 * width), whole(), per_step(amount, width),
            fixed(8, width),
        ],
        out_shape=[
            rows_like(f32, tok, width), rows_like(b16, tok, 3 * width),
            seq((2, nb // 2, ng, 4 * rows, cols), b16), rows_like(b16, amount, width),
            seq((8, width), f32),
        ],
        scratch_shapes=[
            pltpu.VMEM((width, 4 * width), b16), pltpu.VMEM((width, 4 * width), f32),
            pltpu.VMEM((tok, width), b16),
        ],
        compiler_params=params(32),
        cost_estimate=cost(14e9, act_bytes * 24),
        name="backward",
    )(
        scal, gm, cotangent, x2, mixed, q, k, v, lse, ks, vs, normed_t, nsum_all, attn_buf, ln_params
    )

    hpart = jnp.transpose(hpart.reshape(seqs, nb, spans, width), (1, 0, 2, 3))
    if fast:
        spread = lax.all_to_all(hpart, "blk", 0, 0, tiled=True)
        own = jnp.sum(spread.astype(f32), 0)
    else:
        own = lax.psum_scatter(hpart, "blk", scatter_dimension=0).astype(f32)

    input_grad, ln_one = pl.pallas_call(
        functools.partial(input_kernel, dims),
        grid=(seqs,),
        in_specs=[
            scalars(), per_step(tok, 3 * width), per_step(tok, width), per_step(tok, width),
            whole(), per_step(spans, width), fixed(4, width),
        ],
        out_specs=[per_step(tok, width), fixed(8, width)],
        out_shape=[rows_like(f32, tok, width), seq((8, width), f32)],
        scratch_shapes=[pltpu.VMEM((width, 4 * width), b16)],
        compiler_params=params(24),
        cost_estimate=cost(3e9, act_bytes * 16),
        name="input",
    )(scal, dqkv, gx2, tokens, attn_buf, own, ln_params)

    red_mlp = [reduce_any(part) for part in grads]
    red_attn = reduce_any(attn_part).reshape(4, rows, cols)
    red_up = jnp.stack(
        [jnp.swapaxes(r[: sub * rows].reshape(sub, rows, lanes), 0, 1) for r in red_mlp], 2
    ).reshape(rows, sub * CHUNKS * lanes)
    red_down = jnp.concatenate([r[sub * rows :] for r in red_mlp], 1).T

    attn_moment1, attn_moment2, attn_dir = moments(red_attn, attn_first, attn_second)
    up_moment1, up_moment2, up_dir = moments(red_up, up_first, up_second)
    down_moment1, down_moment2, down_dir = moments(red_down, down_first, down_second)
    attn_step = attn_dir + weight_decay * attn_master
    up_step = up_dir + weight_decay * up_master
    down_step = down_dir + weight_decay * down_master

    def squares(attn, up, down):
        return jnp.concatenate(
            [jnp.sum(attn * attn, (1, 2)), jnp.sum(up * up)[None], jnp.sum(down * down)[None]]
        )

    norm_partial = jnp.concatenate([ln_one[:2], ln_two[:2]], 0)
    both = jnp.concatenate(
        [squares(attn_master, up_master, down_master), squares(attn_step, up_step, down_step)]
    )
    if fast:
        line = jnp.pad(both, (0, width - both.shape[0]))[None]
        mine = jnp.concatenate([norm_partial, line, jnp.zeros((3, width), f32)], 0)
        every = lax.all_to_all(
            jnp.broadcast_to(mine[None], (nb * ng,) + mine.shape), ("blk", "group"), 0, 0, tiled=True
        )
        total = jnp.sum(every, 0)
        norm_grad, both = total[:4], total[4, : both.shape[0]]
    else:
        both, norm_grad = lax.psum((both, norm_partial), ("blk", "group"))
    sq_totals = both.reshape(2, -1)
    trust = jnp.sqrt(sq_totals[0]) / jnp.sqrt(sq_totals[1] + epsilon)
    attn_new = attn_master - matrix_rate * trust[:4, None, None] * attn_step
    up_new = up_master - matrix_rate * trust[4] * up_step
    down_new = down_master - matrix_rate * trust[5] * down_step
    ln_moment1, ln_moment2, ln_dir = moments(norm_grad, ln_first, ln_second)
    ln_new = ln_params - vector_rate * ln_dir
    return (
        block_out, input_grad,
        attn_moment1, attn_moment2, attn_new, attn_new.astype(b16),
        up_moment1, up_moment2, up_new, up_new.astype(b16),
        down_moment1, down_moment2, down_new, down_new.astype(b16),
        ln_moment1, ln_moment2, ln_new, jnp.sqrt(sq_totals),
    )


def solution(mesh):
    seq_spec = P("group", "blk", None)
    attn_spec = P(None, "blk", "group")
    flat_spec = P("blk", "group")
    return jax.shard_map(
        functools.partial(body, nb=mesh.shape["blk"], ng=mesh.shape["group"]),
        mesh=mesh,
        in_specs=(seq_spec, seq_spec, P("group"), P())
        + (attn_spec,) * 3
        + (flat_spec,) * 6
        + (P(), P()),
        out_specs=(seq_spec, seq_spec)
        + (attn_spec,) * 4
        + (flat_spec,) * 8
        + (P(),) * 4,
        check_vma=False,
    )
```

```python
import functools

import jax
import jax.numpy as jnp
from jax import lax
from jax.experimental import pallas as pl
from jax.experimental.pallas import tpu as pltpu
from jax.sharding import PartitionSpec as P

HEADS = 8
SPAN = 128
STEP = 5
CHUNKS = 2

masked_value = -1e30
decay_rate = 0.5
matrix_rate = 0.3
vector_rate = 0.5
weight_decay = 0.01
epsilon = 1e-06
gelu_a = 0.7978845608028654
gelu_b = 0.044715

f32 = jnp.float32
b16 = jnp.bfloat16
MIB = 1 << 20
NN = (((1,), (0,)), ((), ()))
NT = (((1,), (1,)), ((), ()))
TN = (((0,), (0,)), ((), ()))


def mm(a, b, dims=NN):
    return lax.dot_general(a, b, dims, preferred_element_type=f32)


def whole():
    return pl.BlockSpec(memory_space=pltpu.VMEM)


def scalars():
    return pl.BlockSpec(memory_space=pltpu.SMEM)


def per_step(*tail):
    zeros = (0,) * len(tail)
    return pl.BlockSpec((1,) + tail, lambda i: (i,) + zeros)


def fixed(*shape):
    zeros = (0,) * len(shape)
    return pl.BlockSpec(shape, lambda i: zeros)


def anywhere():
    return pl.BlockSpec(memory_space=pl.ANY)


def params(mib, steps=1):
    return pltpu.CompilerParams(
        dimension_semantics=("arbitrary",) * steps, vmem_limit_bytes=mib * MIB
    )


def cost(flops, nbytes, trans=0):
    return pl.CostEstimate(flops=int(flops), bytes_accessed=int(nbytes), transcendentals=int(trans))


def norm_parts(values):
    center = values - jnp.mean(values, -1, keepdims=True)
    spread = jnp.mean(center * center, -1, keepdims=True)
    inverse = lax.rsqrt(spread + 1e-05)
    return center * inverse, inverse


def norm_back(gradient, normal, inverse, gain):
    scaled = gradient * gain
    inner = jnp.mean(scaled, -1, keepdims=True)
    cross = jnp.mean(scaled * normal, -1, keepdims=True)
    return inverse * (scaled - inner - normal * cross)


def each_core(core, do):
    @pl.when(core == 0)
    def _():
        do(0, True)
        do(1, False)

    @pl.when(core != 0)
    def _():
        do(0, False)
        do(1, True)


def block(start, size):
    if isinstance(start, int):
        return slice(start, start + size)
    return pl.ds(pl.multiple_of(start, size), size)


def copy_attn(w_ref, own_refs, other_refs, spot, core, dims):
    groups, rows, cols, width = dims

    def do(c, mine):
        for move, buf_ref in enumerate(own_refs if mine else other_refs):
            place = move if spot is None else spot ^ move
            here = block((place * 2 + c) * rows, rows)
            for g in range(groups):
                for m in range(4):
                    at = (g * 4 + m) * rows
                    w_ref[here, m * width + g * cols : m * width + (g + 1) * cols] = buf_ref[
                        at : at + rows, :
                    ]

    each_core(core, do)


def prep_kernel(scal_ref, x_ref, ln_ref, normed_ref, rider_ref, sum_ref):
    i = pl.program_id(0)
    tok, width = x_ref.shape[1:]
    spans = tok // SPAN
    tiles = width // SPAN
    half = sum_ref.shape[0]
    normal, _ = norm_parts(x_ref[0].astype(f32))
    normed = (normal * ln_ref[0:1, :] + ln_ref[1:2, :]).astype(b16)
    normed_ref[0] = normed
    left = scal_ref[2 + i] - scal_ref[0] * tok
    row = lax.broadcasted_iota(jnp.int32, (16, tok), 0)
    col = lax.broadcasted_iota(jnp.int32, (16, tok), 1)
    chosen = jnp.where((col // SPAN == row) & (col < left), 1.0, 0.0)
    amount = jnp.maximum(jnp.sum(chosen, 1, keepdims=True), 1.0)
    total = mm(chosen.astype(b16), normed) / amount

    @pl.when(i == 0)
    def _():
        sum_ref[...] = jnp.zeros_like(sum_ref)

    for s in range(spans):
        for t in range(tiles):
            sum_ref[pl.ds((i * spans + s) * tiles + t, 1), :] = total[
                s : s + 1, t * SPAN : (t + 1) * SPAN
            ]

    @pl.when(i == pl.num_programs(0) - 1)
    def _():
        every = sum_ref[...]
        high = every.astype(b16)
        rider_ref[:half] = high
        rider_ref[half:] = (every - high.astype(f32)).astype(b16)


def pack_kernel(dims, up_ref, down_ref, dep_ref, *out_refs):
    rows, cols, sub, lanes = dims
    for j, out_ref in enumerate(out_refs):
        for h in range(sub):
            c0 = (h * CHUNKS + j) * lanes
            out_ref[h * rows : (h + 1) * rows, :] = up_ref[:, c0 : c0 + lanes].astype(b16)
        out_ref[sub * rows :, :] = down_ref[j * lanes : (j + 1) * lanes, :].T.astype(b16)


def heads_apart(values):
    first = lax.broadcasted_iota(jnp.int32, values.shape, 1) < SPAN // 2
    zero = jnp.zeros_like(values)
    return jnp.concatenate([jnp.where(first, values, zero), jnp.where(first, zero, values)], 0)


def score_masks(scal_ref, i, span, spans, amount):
    length = scal_ref[2 + i]
    mine = scal_ref[0] * spans + span
    key = lax.broadcasted_iota(jnp.int32, (SPAN, 2 * SPAN), 0)
    query = lax.broadcasted_iota(jnp.int32, (SPAN, 2 * SPAN), 1) % SPAN
    local = (key <= query) & (key < length - mine * SPAN)
    index = lax.broadcasted_iota(jnp.int32, (amount, 2 * SPAN), 0)
    summary = (index < mine) & (index * SPAN < length)
    return local, summary


def own_heads(both):
    half = SPAN // 2
    return jnp.concatenate([both[:half, :SPAN], both[half:, SPAN:]], 0)


def gate_kernel(in_ref, dep_ref, out_ref):
    out_ref[...] = in_ref[...]


def forward_kernel(dims, fast, places, scal_ref, normed_ref, x_ref, *refs):
    own_refs, refs = refs[:places], refs[places:]
    other_refs, refs = refs[:places], refs[places:]
    if fast:
        rown_refs, rother_refs = own_refs, other_refs
    else:
        rown_refs, refs = refs[:places], refs[places:]
        rother_refs, refs = refs[:places], refs[places:]
    (ln_ref, dep_ref, q_ref, k_ref, v_ref, ks_ref, vs_ref, nsum_ref, lse_ref, mixed_ref, x2_ref,
     mid_ref, w_ref, token_ref, sums_ref, line_ref) = refs
    i = pl.program_id(0)
    groups, rows, cols, width = dims
    tok = normed_ref.shape[1]
    spans = tok // SPAN
    tiles = width // SPAN
    amount = ks_ref.shape[1]
    factor = (width // HEADS) ** (-0.5)
    half = sums_ref.shape[2]
    base = groups * 4 * rows if fast else 0

    @pl.when(i == 0)
    def _():
        core = scal_ref[0] % 2
        spot = scal_ref[0] // 2 if fast else None
        copy_attn(w_ref, own_refs, other_refs, spot, core, dims)

        def do(c, mine):
            for move, buf_ref in enumerate(rown_refs if mine else rother_refs):
                place = spot ^ move if fast else move
                sums_ref[c, place] = buf_ref[base : base + half, :].astype(f32) + buf_ref[
                    base + half : base + 2 * half, :
                ].astype(f32)

        each_core(core, do)
        token_ref[...] = jnp.zeros_like(token_ref)

    for p in range(places):
        for c in range(2):
            for s in range(spans):
                for t in range(tiles):
                    r = (p * 2 + c) * spans + s
                    line_ref[r : r + 1, t * SPAN : (t + 1) * SPAN] = sums_ref[
                        c, p, pl.ds((i * spans + s) * tiles + t, 1), :
                    ]
    lines = line_ref[...]
    high = lines.astype(b16)
    low = (lines - high.astype(f32)).astype(b16)
    nsum_ref[0] = high
    normed = normed_ref[0]
    q_ref[0] = mm(normed, w_ref[:, :width]).astype(b16)
    k_ref[0] = mm(normed, w_ref[:, width : 2 * width]).astype(b16)
    v_ref[0] = mm(normed, w_ref[:, 2 * width : 3 * width]).astype(b16)
    sums = mm(high, w_ref[:, width : 3 * width]) + mm(low, w_ref[:, width : 3 * width])
    ks_ref[0] = sums[:, :width].astype(b16)
    vs_ref[0] = sums[:, width:].astype(b16)
    for span in range(spans):
        part = slice(span * SPAN, (span + 1) * SPAN)
        local, summary = score_masks(scal_ref, i, span, spans, amount)
        for pair in range(tiles):
            lanes = slice(pair * SPAN, (pair + 1) * SPAN)
            query = heads_apart(q_ref[0, part, lanes] * b16(factor))
            keys = jnp.concatenate([k_ref[0, part, lanes], ks_ref[0, :, lanes]], 0)
            values = jnp.concatenate([v_ref[0, part, lanes], vs_ref[0, :, lanes]], 0)
            scores = mm(keys, query, NT)
            here = jnp.where(local, scores[:SPAN], masked_value)
            there = jnp.where(summary, scores[SPAN:], masked_value)
            top = jnp.maximum(jnp.max(here, 0, keepdims=True), jnp.max(there, 0, keepdims=True))
            here, there = jnp.exp(here - top), jnp.exp(there - top)
            total = jnp.sum(here, 0, keepdims=True) + jnp.sum(there, 0, keepdims=True)
            probs = jnp.concatenate([here.astype(b16), there.astype(b16)], 0)
            lse_ref[0, span, pair : pair + 1, :] = top + jnp.log(total)
            out = mm(values, probs, TN) * (1.0 / total)
            mixed_ref[0, lanes, part] = own_heads(out).astype(b16)
    x2 = x_ref[0].astype(f32) + mm(mixed_ref[0], w_ref[:, 3 * width :], TN)
    x2_ref[0] = x2.astype(b16)
    normal, _ = norm_parts(x2)
    mid_ref[0] = (normal * ln_ref[2:3, :] + ln_ref[3:4, :]).astype(b16)


def mlp_kernel(dims, fast, places, last, scal_ref, mid_ref, g_ref, *refs):
    own_refs, refs = refs[:places], refs[places:]
    other_refs, refs = refs[:places], refs[places:]
    if last:
        (dep_ref, x2_ref, y_in_ref, gm_in_ref,
         y_ref, gm_ref, keep_ref, send_ref, wu_ref, wd_ref, du_ref, dd_ref) = refs
    else:
        (dep_ref, y_ref, gm_ref, keep_ref, send_ref, wu_ref, wd_ref, du_ref, dd_ref) = refs
    groups, rows, cols, sub, lanes = dims
    size = sub * rows + cols
    i = pl.program_id(0)
    core = scal_ref[0] % 2

    def pieces(place, c):
        b = place * 2 + c
        here = block(b * rows, rows)
        there = block(b * lanes, lanes)
        for g in range(groups):
            for h in range(sub):
                at = g * size + h * rows
                yield (
                    slice(at, at + rows),
                    (here, slice((g * sub + h) * lanes, (g * sub + h + 1) * lanes)),
                    True,
                )
            at = g * size + sub * rows
            yield slice(at, at + cols), (slice(g * cols, (g + 1) * cols), there), False

    @pl.when(i == 0)
    def _():
        def do(c, mine):
            for move, buf_ref in enumerate(own_refs if mine else other_refs):
                place = (scal_ref[0] // 2) ^ move if fast else move
                for there, here, is_up in pieces(place, c):
                    (wu_ref if is_up else wd_ref)[here] = buf_ref[there, :]

        each_core(core, do)
        du_ref[...] = jnp.zeros_like(du_ref)
        dd_ref[...] = jnp.zeros_like(dd_ref)

    mid, g = mid_ref[0], g_ref[0]
    up = mm(mid, wu_ref[...])
    grad_act = mm(g, wd_ref[...])
    square = up * up
    half = 0.5 + 0.5 * jnp.tanh(up * (gelu_a + gelu_a * gelu_b * square))
    act = (up * half).astype(b16)
    slope = half + (up * half * (1.0 - half)) * (2.0 * gelu_a + 6.0 * gelu_a * gelu_b * square)
    grad_up = (slope * grad_act).astype(b16)
    y = mm(act, wd_ref[...], NT)
    gm = mm(grad_up, wu_ref[...], NT)
    if last:
        y_ref[0] = (x2_ref[0].astype(f32) + y_in_ref[0].astype(f32) + y).astype(b16)
        gm_ref[0] = (gm_in_ref[0].astype(f32) + gm).astype(b16)
    else:
        y_ref[0] = y.astype(b16)
        gm_ref[0] = gm.astype(b16)
    dd_ref[...] += mm(g, act, TN)
    du_ref[...] += mm(mid, grad_up, TN)

    @pl.when(i == pl.num_programs(0) - 1)
    def _():
        def do(c, mine):
            out_ref = keep_ref if mine else send_ref
            for place in range(places):
                for there, here, is_up in pieces(place, c):
                    out_ref[place, there, :] = (du_ref if is_up else dd_ref)[here].astype(b16)

        each_core(core, do)


def middle_kernel(
    gm_ref, g_ref, x2_ref, mixed_ref, w_ref, ln_ref, gx2_ref, do_ref, dwo_ref, lng_ref
):
    i = pl.program_id(0)
    width = ln_ref.shape[1]

    @pl.when(i == 0)
    def _():
        dwo_ref[...] = jnp.zeros_like(dwo_ref)
        lng_ref[...] = jnp.zeros_like(lng_ref)

    gm = gm_ref[0].astype(f32)
    normal, inverse = norm_parts(x2_ref[0].astype(f32))
    lng_ref[0:1, :] += jnp.sum(gm * normal, 0, keepdims=True)
    lng_ref[1:2, :] += jnp.sum(gm, 0, keepdims=True)
    gx2 = g_ref[0].astype(f32) + norm_back(gm, normal, inverse, ln_ref[2:3, :])
    branch = gx2.astype(b16)
    gx2_ref[0] = branch
    dwo_ref[...] += mm(mixed_ref[0], branch)
    do_ref[0] = mm(branch, w_ref[:, 3 * width :], NT).astype(b16)


def backward_kernel(
    places, scal_ref, do_ref, q_ref, k_ref, v_ref, lse_ref, ks_ref, vs_ref, w_ref, dep_ref,
    dqkv_ref, key_ref, value_ref, h_ref, dqt_ref,
):
    i = pl.program_id(0)
    tok, width = do_ref.shape[1:]
    spans = tok // SPAN
    tiles = width // SPAN
    amount = ks_ref.shape[1]
    factor = (width // HEADS) ** (-0.5)

    @pl.when(i == 0)
    def _():
        h_ref[...] = jnp.zeros_like(h_ref)

    key_parts, value_parts = [], []
    for span in range(spans):
        part = slice(span * SPAN, (span + 1) * SPAN)
        local, summary = score_masks(scal_ref, i, span, spans, amount)
        for pair in range(tiles):
            lanes = slice(pair * SPAN, (pair + 1) * SPAN)
            query = heads_apart(q_ref[0, part, lanes] * b16(factor))
            grad = heads_apart(do_ref[0, part, lanes])
            keys = jnp.concatenate([k_ref[0, part, lanes], ks_ref[0, :, lanes]], 0)
            values = jnp.concatenate([v_ref[0, part, lanes], vs_ref[0, :, lanes]], 0)
            scores = mm(keys, query, NT)
            grads = mm(values, grad, NT)
            total = lse_ref[0, span, pair : pair + 1, :]
            here = jnp.exp(jnp.where(local, scores[:SPAN], masked_value) - total)
            there = jnp.exp(jnp.where(summary, scores[SPAN:], masked_value) - total)
            here_grad, there_grad = here * grads[:SPAN], there * grads[SPAN:]
            dot = jnp.sum(here_grad, 0, keepdims=True) + jnp.sum(there_grad, 0, keepdims=True)
            low = jnp.concatenate([here.astype(b16), there.astype(b16)], 0)
            back = jnp.concatenate(
                [(here_grad - here * dot).astype(b16), (there_grad - there * dot).astype(b16)], 0
            )
            grad_value = mm(low, grad)
            grad_key = mm(back, query)
            dqt_ref[lanes, part] = (own_heads(mm(keys, back, TN)) * factor).astype(b16)
            dqkv_ref[0, part, width + pair * SPAN : width + (pair + 1) * SPAN] = grad_key[
                :SPAN
            ].astype(b16)
            dqkv_ref[0, part, 2 * width + pair * SPAN : 2 * width + (pair + 1) * SPAN] = grad_value[
                :SPAN
            ].astype(b16)
            key_parts.append(grad_key[SPAN:])
            value_parts.append(grad_value[SPAN:])
    dqkv_ref[0, :, :width] = dqt_ref[...].T

    def joined(parts):
        return jnp.concatenate(
            [sum(parts[s * tiles + p] for s in range(spans)) for p in range(tiles)], 1
        ).astype(b16)

    key_part, value_part = joined(key_parts), joined(value_parts)
    key_ref[0], value_ref[0] = key_part, value_part
    extra = mm(key_part, w_ref[:, width : 2 * width], NT) + mm(
        value_part, w_ref[:, 2 * width : 3 * width], NT
    )
    for p in range(places):
        for c in range(2):
            for s in range(spans):
                for t in range(tiles):
                    r = (p * 2 + c) * spans + s
                    h_ref[c, p, pl.ds((i * spans + s) * tiles + t, 1), :] = extra[
                        r : r + 1, t * SPAN : (t + 1) * SPAN
                    ]


def grads_kernel(
    dims, fast, scal_ref, normed_ref, dqkv_ref, nsum_ref, key_ref, value_ref, dwo_ref, h_ref,
    two_ref, dep_ref, *refs
):
    if fast:
        keep_ref, send_ref, nt_ref, dw_ref = refs
        hkeep_ref, hsend_ref = keep_ref, send_ref
    else:
        keep_ref, send_ref, hkeep_ref, hsend_ref, nt_ref, dw_ref = refs
    groups, rows, cols, width = dims
    places, half = h_ref.shape[1:3]
    tiles = width // SPAN
    base = groups * 4 * rows if fast else 0
    used = -(-half // 16) * 16 - 8
    nt_ref[...] = normed_ref[...].T
    dw_ref[:, :width] = mm(nt_ref[...], dqkv_ref[:, :width])
    dw_ref[:, width : 2 * width] = mm(nt_ref[...], dqkv_ref[:, width : 2 * width]) + mm(
        nsum_ref[...], key_ref[...], TN
    )
    dw_ref[:, 2 * width :] = mm(nt_ref[...], dqkv_ref[:, 2 * width :]) + mm(
        nsum_ref[...], value_ref[...], TN
    )
    if fast:
        for p in range(places):
            for c in range(2):
                k, t = divmod(p * 2 + c, tiles)
                piece = two_ref[k : k + 1, t * SPAN : (t + 1) * SPAN]
                high = piece.astype(b16).astype(f32)
                h_ref[c, p, used : used + 1, :] = high
                h_ref[c, p, used + 1 : used + 2, :] = piece - high

    def do(c, mine):
        out_ref, hout_ref = (keep_ref, hkeep_ref) if mine else (send_ref, hsend_ref)
        for p in range(places):
            r0 = (p * 2 + c) * rows
            for g in range(groups):
                for m in range(4):
                    at = (g * 4 + m) * rows
                    from_ref = dwo_ref if m == 3 else dw_ref
                    c0 = g * cols if m == 3 else m * width + g * cols
                    out_ref[p, at : at + rows, :] = from_ref[
                        r0 : r0 + rows, c0 : c0 + cols
                    ].astype(b16)
            hout_ref[p, base : base + half, :] = h_ref[c, p].astype(b16)

    each_core(scal_ref[0] % 2, do)


def project_kernel(dqkv_ref, w_ref, dep_ref, out_ref):
    out_ref[0] = mm(dqkv_ref[0], w_ref[:, : dqkv_ref.shape[2]], NT).astype(out_ref.dtype)


def input_kernel(scal_ref, grad_ref, gx2_ref, x_ref, h_ref, ln_ref, out_ref, lng_ref):
    i = pl.program_id(0)
    tok, width = x_ref.shape[1:]
    spans = tok // SPAN
    tiles = width // SPAN

    @pl.when(i == 0)
    def _():
        lng_ref[...] = jnp.zeros_like(lng_ref)

    left = scal_ref[2 + i] - scal_ref[0] * tok
    place = lax.broadcasted_iota(jnp.int32, (tok, 1), 0)
    extra = []
    for s in range(spans):
        part = slice(s * SPAN, (s + 1) * SPAN)
        amount = jnp.clip(left - s * SPAN, 0, SPAN)
        share = jnp.where(place[part] < left, 1.0, 0.0) / jnp.maximum(amount, 1).astype(f32)
        line = jnp.concatenate(
            [h_ref[pl.ds((i * spans + s) * tiles + t, 1), :] for t in range(tiles)], 1
        )
        extra.append(share * line)
    grad = grad_ref[0].astype(f32) + jnp.concatenate(extra, 0)
    normal, inverse = norm_parts(x_ref[0].astype(f32))
    lng_ref[0:1, :] += jnp.sum(grad * normal, 0, keepdims=True)
    lng_ref[1:2, :] += jnp.sum(grad, 0, keepdims=True)
    out_ref[0] = gx2_ref[0].astype(f32) + norm_back(grad, normal, inverse, ln_ref[0:1, :])


def spread_kernel(count, scal_ref, *refs):
    keeps, gets, outs = refs[:count], refs[count : 2 * count], refs[-4:]
    spot = scal_ref[0] // 2
    at = 0
    for keep_ref, get_ref in zip(keeps, gets):
        size = keep_ref.shape[1]
        for move in range(4):
            there = spot ^ move
            total = keep_ref[there].astype(f32) + get_ref[there].astype(f32)
            outs[move][at : at + size, :] = total.astype(outs[move].dtype)
        at += size


def halves_kernel(scal_ref, *refs):
    spot = scal_ref[0] // 2
    for j, far in enumerate((1, 2)):
        keep_ref, get_ref = refs[j], refs[2 + j]
        stay_ref, out_ref = refs[4 + 2 * j], refs[5 + 2 * j]
        near = 3 - far
        for k, (ref, move) in enumerate(
            ((stay_ref, 0), (stay_ref, near), (out_ref, far), (out_ref, far ^ near))
        ):
            there = spot ^ move
            total = keep_ref[there].astype(f32) + get_ref[there].astype(f32)
            ref[k % 2] = total.astype(ref.dtype)


def turn_kernel(*refs):
    for j in range(2):
        stay_ref, get_ref = refs[2 * j], refs[2 * j + 1]
        own_ref, out_ref = refs[4 + 2 * j], refs[5 + 2 * j]
        own_ref[...] = stay_ref[0] + get_ref[0].astype(f32)
        out_ref[...] = (stay_ref[1] + get_ref[1].astype(f32)).astype(b16)


def collect_kernel(sizes, count, scal_ref, *refs):
    z = scal_ref[1]
    groups = 4
    outs = refs[len(sizes) * count + 1 :]

    def total(terms, start, size):
        rows = pl.ds(start, size)
        value = terms[0][rows, :].astype(f32)
        for ref in terms[1:]:
            value = value + ref[rows, :].astype(f32)
        return value

    at = 0
    for k, size in enumerate(sizes):
        terms = refs[k * count : (k + 1) * count]
        for by in range(groups):
            start = pl.multiple_of(((z + by) % groups) * size, size)
            outs[by][at : at + size, :] = total(terms, start, size).astype(outs[by].dtype)
        at += size
    if len(outs) > groups:
        outs[groups][...] = total(terms, groups * size, outs[groups].shape[0])


def moments(gradient, first, second):
    corr = 1.0 - decay_rate**STEP
    new_first = decay_rate * first + (1.0 - decay_rate) * gradient
    new_second = decay_rate * second + (1.0 - decay_rate) * gradient * gradient
    return (new_first, new_second, new_first / corr / (jnp.sqrt(new_second / corr) + epsilon))


def lane_line(values):
    lane = lax.broadcasted_iota(jnp.int32, (1, SPAN), 1)
    line = jnp.zeros((1, SPAN), f32)
    for at, value in values.items():
        line = line + jnp.where(lane == at, value, 0.0)
    return line


def square_sum(values):
    return jnp.sum(jnp.sum(values * values, 0, keepdims=True), 1, keepdims=True)


def add_up(refs, rows):
    total = refs[0][rows, :].astype(f32)
    for ref in refs[1:]:
        total = total + ref[rows, :].astype(f32)
    return total


def mlp_step_kernel(dims, count, *refs):
    grads = refs[:count]
    (um_ref, uf_ref, us_ref, dm_ref, df_ref, ds_ref,
     u1_ref, u2_ref, ustep_ref, d1_ref, d2_ref, dstep_ref, line_ref) = refs[count:]
    rows, cols, sub, lanes = dims
    size = sub * rows + cols
    sums = [jnp.zeros((1, 1), f32) for _ in range(4)]
    for j in range(CHUNKS):
        for h in range(sub):
            start = j * size + h * rows
            at = (slice(None), slice((h * CHUNKS + j) * lanes, (h * CHUNKS + j + 1) * lanes))
            first, second, way = moments(
                add_up(grads, slice(start, start + rows)), uf_ref[at], us_ref[at]
            )
            step = way + weight_decay * um_ref[at]
            u1_ref[at], u2_ref[at], ustep_ref[at] = first, second, step
            sums[0] += square_sum(um_ref[at])
            sums[2] += square_sum(step)
        start = j * size + sub * rows
        at = (slice(j * lanes, (j + 1) * lanes), slice(None))
        first, second, way = moments(
            add_up(grads, slice(start, start + cols)).T, df_ref[at], ds_ref[at]
        )
        step = way + weight_decay * dm_ref[at]
        d1_ref[at], d2_ref[at], dstep_ref[at] = first, second, step
        sums[1] += square_sum(dm_ref[at])
        sums[3] += square_sum(step)
    line_ref[...] = lane_line({4: sums[0], 5: sums[1], 10: sums[2], 11: sums[3]})


def attn_step_kernel(count, fast, *refs):
    grads = refs[:count]
    (m_ref, f_ref, s_ref, line_ref, one_ref, h_ref,
     m1_ref, m2_ref, step_ref, out_ref, all_ref) = refs[count:]
    rows = m_ref.shape[1]
    tiles = one_ref.shape[1] // SPAN
    values = {}
    for m in range(4):
        first, second, way = moments(
            add_up(grads, slice(m * rows, (m + 1) * rows)), f_ref[m], s_ref[m]
        )
        step = way + weight_decay * m_ref[m]
        m1_ref[m], m2_ref[m], step_ref[m] = first, second, step
        values[m] = square_sum(m_ref[m])
        values[6 + m] = square_sum(step)
    all_ref[...] = jnp.zeros_like(all_ref)
    for k in range(2):
        for t in range(tiles):
            all_ref[k * tiles + t : k * tiles + t + 1, :] = one_ref[
                k : k + 1, t * SPAN : (t + 1) * SPAN
            ]
    at = 2 * tiles
    if fast:
        used = h_ref.shape[0] - 8
        piece = h_ref[used : used + 1, :] + h_ref[used + 1 : used + 2, :]
        high = piece.astype(b16).astype(f32)
        all_ref[at : at + 1, :] = high
        all_ref[at + 1 : at + 2, :] = piece - high
    line = lane_line(values) + line_ref[...]
    for k in range(3):
        piece = line.astype(b16).astype(f32)
        all_ref[at + 2 + k : at + 3 + k, :] = piece
        line = line - piece
    message = all_ref[...].astype(b16)
    for k in range(out_ref.shape[0]):
        out_ref[k] = message


def final_kernel(
    groups, fast, every_ref, two_ref, am_ref, as_ref, um_ref, us_ref, dm_ref, ds_ref, ln_ref, lf_ref, ls_ref,
    an_ref, ac_ref, un_ref, uc_ref, dn_ref, dc_ref, l1_ref, l2_ref, ln_new_ref, norms_ref,
    all_ref, grad_ref,
):
    width = ln_ref.shape[1]
    tiles = width // SPAN
    at = 2 * tiles
    total = None
    for b in range(every_ref.shape[0] // groups):
        part = every_ref[b * groups].astype(f32)
        for k in range(b * groups + 1, (b + 1) * groups):
            part = part + every_ref[k].astype(f32)
        if fast:
            k, t = divmod(b, tiles)
            grad_ref[2 + k : 3 + k, t * SPAN : (t + 1) * SPAN] = (
                part[at : at + 1, :] + part[at + 1 : at + 2, :]
            )
        total = part if total is None else total + part
    all_ref[...] = total
    for k in range(2):
        for t in range(tiles):
            grad_ref[k : k + 1, t * SPAN : (t + 1) * SPAN] = all_ref[
                k * tiles + t : k * tiles + t + 1, :
            ]
    if not fast:
        grad_ref[2:4, :] = two_ref[0:2, :]
    line = all_ref[at + 2 : at + 3, :] + all_ref[at + 3 : at + 4, :] + all_ref[at + 4 : at + 5, :]
    roots = jnp.sqrt(line)
    norms_ref[0:1, :] = roots[:, 0:6]
    norms_ref[1:2, :] = roots[:, 6:12]
    lane = lax.broadcasted_iota(jnp.int32, line.shape, 1)

    def rate(k):
        weight = jnp.sum(jnp.where(lane == k, roots, 0.0), 1, keepdims=True)
        square = jnp.sum(jnp.where(lane == 6 + k, line, 0.0), 1, keepdims=True)
        return matrix_rate * (weight / jnp.sqrt(square + epsilon))

    for m in range(4):
        new = am_ref[m] - rate(m) * as_ref[m]
        an_ref[m] = new
        ac_ref[m] = new.astype(b16)
    new = um_ref[...] - rate(4) * us_ref[...]
    un_ref[...] = new
    uc_ref[...] = new.astype(b16)
    new = dm_ref[...] - rate(5) * ds_ref[...]
    dn_ref[...] = new
    dc_ref[...] = new.astype(b16)
    first, second, way = moments(grad_ref[...], lf_ref[...], ls_ref[...])
    l1_ref[...], l2_ref[...] = first, second
    ln_new_ref[...] = ln_ref[...] - vector_rate * way


def fast_mesh(nb, ng, width):
    return nb == 8 and ng == 4 and width // ng == SPAN


def shift(values, by, ng):
    return lax.ppermute(values, "group", [(j, (j + by) % ng) for j in range(ng)])


def cross(values, bit, nb):
    return lax.ppermute(values, "blk", [(j, j ^ bit) for j in range(nb)])


def put(buffer, piece, at):
    return lax.dynamic_update_slice(buffer, piece[None], (at,) + (0,) * piece.ndim)


def take(buffer, at):
    return lax.dynamic_index_in_dim(buffer, at, 0, keepdims=False)


def gather_group(piece, z, ng):
    out = put(jnp.zeros((ng,) + piece.shape, piece.dtype), piece, z)
    for by in range(1, ng):
        out = put(out, shift(piece, by, ng), (z - by) % ng)
    return out.reshape((-1,) + piece.shape[1:])


def gather_plane(piece, nb):
    return [piece] + [cross(piece, 2 * move, nb) for move in range(1, nb // 2)]


def other_core(pieces, nb):
    return [cross(piece, 1, nb) for piece in pieces]


def body(
    tokens, cotangent, lengths, ln_params, attn_master, attn_first, attn_second,
    up_master, up_first, up_second, down_master, down_first, down_second, ln_first, ln_second,
    *, nb, ng,
):
    seqs, tok, width = tokens.shape
    spans = tok // SPAN
    tiles = width // SPAN
    amount = nb * spans
    rows, cols = attn_master.shape[1:]
    ff_rows = down_master.shape[0]
    sub = nb // ng
    lanes = ff_rows // CHUNKS
    inner = nb * lanes
    places = nb // 2
    size = sub * rows + cols
    attn_rows = ng * 4 * rows
    half = -(-(seqs * spans * tiles + 8) // 16) * 16
    b, z = lax.axis_index("blk").astype(jnp.int32), lax.axis_index("group").astype(jnp.int32)
    core = b % 2
    fast = fast_mesh(nb, ng, width)
    scal = jnp.concatenate([jnp.stack([b, z]), lengths.astype(jnp.int32)])
    shape = jax.ShapeDtypeStruct

    def like(dtype, *tail):
        return shape((seqs,) + tail, dtype)

    def gather_any(piece, over=("blk", "group")):
        every = lax.all_gather(piece, over)
        every = every.reshape((places, 2, -1) + piece.shape[1:])
        every = jnp.swapaxes(every, 0, 1)
        own, other = take(every, core), take(every, 1 - core)
        return [own[p] for p in range(places)], [other[p] for p in range(places)]

    def reduce_any(keep, send, blocks):
        both = jnp.stack([jnp.where(core == 0, keep, send), jnp.where(core == 0, send, keep)])
        both = jnp.swapaxes(both, 0, 1).reshape((nb,) + keep.shape[1:])
        mine = lax.psum_scatter(both, "blk", scatter_dimension=0)
        if not blocks:
            return mine.astype(f32)
        mine = mine.reshape((ng, -1) + mine.shape[1:])
        return lax.psum_scatter(mine, "group", scatter_dimension=0).astype(f32)

    def flat(call, name, outs, scratch, work, *args, scalar=False):
        return pl.pallas_call(
            call,
            in_specs=[scalars()] * scalar + [whole()] * (len(args) - scalar),
            out_specs=[whole()] * len(outs),
            out_shape=outs,
            scratch_shapes=scratch,
            compiler_params=pltpu.CompilerParams(vmem_limit_bytes=16 * MIB),
            cost_estimate=work,
            name=name,
        )(*args)

    attn_piece = attn_master.astype(b16).reshape(4 * rows, cols)
    normed, rider = pl.pallas_call(
        prep_kernel,
        grid=(seqs,),
        in_specs=[scalars(), per_step(tok, width), fixed(4, width)],
        out_specs=[per_step(tok, width), fixed(2 * half, SPAN)],
        out_shape=[like(b16, tok, width), shape((2 * half, SPAN), b16)],
        scratch_shapes=[pltpu.VMEM((half, SPAN), f32)],
        compiler_params=params(16),
        cost_estimate=cost(4e7, 2 * seqs * tok * width * 2),
        name="prep",
    )(scal, tokens, ln_params)

    if fast:
        message = jnp.concatenate([gather_group(attn_piece, z, ng), rider], 0)
        attn_own = gather_plane(message, nb)
        attn_bufs = attn_own + other_core(attn_own, nb)
        pieces = flat(
            functools.partial(pack_kernel, (rows, cols, sub, lanes)), "pack",
            [shape((size, lanes), b16)] * CHUNKS, [], cost(1e6, 1e6),
            up_master, down_master, attn_own[1],
        )
        mlp_z = [gather_group(piece, z, ng) for piece in pieces]
        gates = [mlp_z[0]]
    else:
        up_low = up_master.astype(b16).reshape(rows, sub, CHUNKS, lanes)
        down_low = down_master.astype(b16).T.reshape(cols, CHUNKS, lanes)
        pieces = [
            jnp.concatenate(
                [jnp.swapaxes(up_low[:, :, j], 0, 1).reshape(sub * rows, lanes), down_low[:, j]], 0
            )
            for j in range(CHUNKS)
        ]
        attn_own, attn_other = gather_any(attn_piece)
        ride_own, ride_other = gather_any(rider, "blk")
        attn_bufs = attn_own + attn_other + ride_own + ride_other
        gates = [ln_params]

    dims = (ng, rows, cols, width)
    act_bytes = seqs * tok * width
    q, k, v, ks, vs, nsum, lse, mixed, x2, mid, w_attn, token = pl.pallas_call(
        functools.partial(forward_kernel, dims, fast, places),
        grid=(seqs,),
        in_specs=[scalars(), per_step(tok, width), per_step(tok, width)]
        + [whole()] * len(attn_bufs)
        + [fixed(4, width), whole()],
        out_specs=[
            per_step(tok, width), per_step(tok, width), per_step(tok, width),
            per_step(amount, width), per_step(amount, width), per_step(amount, width),
            per_step(spans, tiles, 2 * SPAN),
            per_step(width, tok), per_step(tok, width), per_step(tok, width),
            whole(), fixed(8, SPAN),
        ],
        out_shape=[
            like(b16, tok, width), like(b16, tok, width), like(b16, tok, width),
            like(b16, amount, width), like(b16, amount, width), like(b16, amount, width),
            like(f32, spans, tiles, 2 * SPAN),
            like(b16, width, tok), like(b16, tok, width), like(b16, tok, width),
            shape((width, 4 * width), b16), shape((8, SPAN), f32),
        ],
        scratch_shapes=[
            pltpu.VMEM((2, places, half, SPAN), f32), pltpu.VMEM((amount, width), f32)
        ],
        compiler_params=params(16),
        cost_estimate=cost(8e9, act_bytes * 18),
        name="forward",
    )(scal, normed, tokens, *attn_bufs, ln_params, gates[0])

    if fast:
        mlp_own = [gather_plane(mlp_z[0], nb)]
        for j in range(1, CHUNKS):
            (gated,) = flat(
                gate_kernel, "gate", [shape(mlp_z[j].shape, b16)], [], cost(1e6, 1e6),
                mlp_z[j], token,
            )
            gates.append(gated)
            mlp_own.append(gather_plane(gated, nb))
        mlp_bufs = [own + other_core(own, nb) for own in mlp_own]
    else:
        mlp_bufs = [sum(gather_any(piece), []) for piece in pieces]
        gates = gates * CHUNKS
    mlp_dims = (ng, rows, cols, sub, lanes)
    mlp_out = shape((places, ng * size, lanes), b16)
    keeps, sends = [], []
    y = gm = None
    for j in range(CHUNKS):
        last = j == CHUNKS - 1
        args = [scal, mid, cotangent, *mlp_bufs[j], gates[min(j + 1, CHUNKS - 1)]]
        in_specs = [scalars(), per_step(tok, width), per_step(tok, width)]
        in_specs += [whole()] * (len(mlp_bufs[j]) + 1)
        if last:
            args += [x2, y, gm]
            in_specs += [per_step(tok, width)] * 3
        y, gm, keep, send = pl.pallas_call(
            functools.partial(mlp_kernel, mlp_dims, fast, places, last),
            grid=(seqs,),
            in_specs=in_specs,
            out_specs=[per_step(tok, width), per_step(tok, width), whole(), whole()],
            out_shape=[like(b16, tok, width), like(b16, tok, width), mlp_out, mlp_out],
            scratch_shapes=[
                pltpu.VMEM((width, inner), b16), pltpu.VMEM((width, inner), b16),
                pltpu.VMEM((width, inner), f32), pltpu.VMEM((width, inner), f32),
            ],
            compiler_params=params(24),
            cost_estimate=cost(9e9, act_bytes * 20),
            name="mlp",
        )(*args)
        keeps.append(keep)
        sends.append(send)
    block_out = y
    if fast:
        gets = [cross(send, 1, nb) for send in sends]

    gx2, grad_mixed, dwo, ln_two = pl.pallas_call(
        middle_kernel,
        grid=(seqs,),
        in_specs=[
            per_step(tok, width), per_step(tok, width), per_step(tok, width),
            per_step(width, tok), whole(), fixed(4, width),
        ],
        out_specs=[
            per_step(tok, width), per_step(tok, width), fixed(width, width), fixed(8, width)
        ],
        out_shape=[
            like(b16, tok, width), like(b16, tok, width), shape((width, width), f32),
            shape((8, width), f32),
        ],
        compiler_params=params(16),
        cost_estimate=cost(3e9, act_bytes * 14),
        name="middle",
    )(gm, cotangent, x2, mixed, w_attn, ln_params)

    block = shape((ng * size, lanes), f32)
    block_low = shape((ng * size, lanes), b16)
    two, two_low = shape((2,) + block.shape, f32), shape((2,) + block.shape, b16)
    if fast:
        stay_a, out_a, stay_b, out_b = flat(
            halves_kernel, "halves", [two, two_low, two, two_low], [], cost(2e6, 16e6),
            scal, *keeps, *gets, scalar=True,
        )
        get_a, get_b = cross(out_a, 2, nb), cross(out_b, 4, nb)
        dep = stay_a
    else:
        dep = ln_two

    dqkv, key_part, value_part, h_part = pl.pallas_call(
        functools.partial(backward_kernel, places),
        grid=(seqs,),
        in_specs=[
            scalars(), per_step(tok, width),
            per_step(tok, width), per_step(tok, width), per_step(tok, width),
            per_step(spans, tiles, 2 * SPAN), per_step(amount, width), per_step(amount, width),
            whole(), anywhere(),
        ],
        out_specs=[
            per_step(tok, 3 * width), per_step(amount, width), per_step(amount, width), whole()
        ],
        out_shape=[
            like(b16, tok, 3 * width), like(b16, amount, width), like(b16, amount, width),
            shape((2, places, half, SPAN), f32),
        ],
        scratch_shapes=[pltpu.VMEM((width, tok), b16)],
        compiler_params=params(16),
        cost_estimate=cost(14e9, act_bytes * 24),
        name="backward",
    )(scal, grad_mixed, q, k, v, lse, ks, vs, w_attn, dep)

    if fast:
        own_a, out_a, own_b, out_b = flat(
            turn_kernel, "turn", [block, block_low] * 2, [], cost(1e6, 10e6),
            stay_a, get_a, stay_b, get_b,
        )
        mlp_parts = [own_a, cross(out_a, 4, nb), own_b, cross(out_b, 2, nb)]
        dep = own_a
    tail = half if fast else 0
    outs = [shape((places, attn_rows + tail, cols), b16)] * 2
    if not fast:
        outs += [shape((places, half, SPAN), b16)] * 2
    parts = flat(
        functools.partial(grads_kernel, dims, fast), "grads", outs,
        [pltpu.VMEM((width, seqs * tok), b16), pltpu.VMEM((width, 3 * width), f32)],
        cost(5e9, 1e7),
        scal, normed.reshape(-1, width), dqkv.reshape(-1, 3 * width), nsum.reshape(-1, width),
        key_part.reshape(-1, width), value_part.reshape(-1, width), dwo, h_part, ln_two, dep,
        scalar=True,
    )

    def collect(terms, sizes, count, tail):
        outs = [shape((sum(sizes), SPAN), f32)] + [shape((sum(sizes), SPAN), b16)] * 3
        if tail:
            outs.append(shape((tail, SPAN), f32))
        return flat(
            functools.partial(collect_kernel, sizes, count), "collect", outs, [], cost(1e6, 4e6),
            scal, *terms, scalar=True,
        )

    if fast:
        attn_low = shape((attn_rows + tail, cols), b16)
        attn_parts = flat(
            functools.partial(spread_kernel, 1), "spread",
            [shape(attn_low.shape, f32)] + [attn_low] * 3, [], cost(1e6, 4e6),
            scal, parts[0], cross(parts[1], 1, nb), scalar=True,
        )
        dep = attn_parts[0]
        attn_parts = [dep] + [cross(attn_parts[m], 2 * m, nb) for m in range(1, 4)]
    else:
        dep = parts[2]

    grad_in = pl.pallas_call(
        project_kernel,
        grid=(seqs,),
        in_specs=[per_step(tok, 3 * width), whole(), anywhere()],
        out_specs=per_step(tok, width),
        out_shape=like(b16, tok, width),
        compiler_params=params(16),
        cost_estimate=cost(3e9, act_bytes * 8),
        name="project",
    )(dqkv, w_attn, dep)

    if fast:
        mlp_sums = collect(mlp_parts + [grad_in], (size,) * CHUNKS, 2, 0)
        mlp_sums = [mlp_sums[0]] + [shift(mlp_sums[by], by, ng) for by in range(1, ng)]
        *attn_sums, own = collect(attn_parts + [grad_in], (4 * rows,), 4, half)
        attn_sums = [attn_sums[0]] + [shift(attn_sums[by], by, ng) for by in range(1, ng)]
    else:
        own = reduce_any(parts[2], parts[3], False)
        attn_sums = [reduce_any(parts[0], parts[1], True)]
        mlp_sums = [
            jnp.concatenate([reduce_any(keep, send, True) for keep, send in zip(keeps, sends)], 0)
        ]
        ln_two = lax.psum(ln_two, ("blk", "group"))

    input_grad, ln_one = pl.pallas_call(
        input_kernel,
        grid=(seqs,),
        in_specs=[
            scalars(), per_step(tok, width), per_step(tok, width), per_step(tok, width),
            whole(), fixed(4, width),
        ],
        out_specs=[per_step(tok, width), fixed(8, width)],
        out_shape=[like(f32, tok, width), shape((8, width), f32)],
        compiler_params=params(16),
        cost_estimate=cost(1e8, act_bytes * 10),
        name="input",
    )(scal, grad_in, gx2, tokens, own, ln_params)

    attn_shape = shape(attn_master.shape, f32)
    up_shape, down_shape = shape(up_master.shape, f32), shape(down_master.shape, f32)
    up_moment1, up_moment2, up_step, down_moment1, down_moment2, down_step, line = flat(
        functools.partial(mlp_step_kernel, (rows, cols, sub, lanes), len(mlp_sums)),
        "mlp_step",
        [up_shape] * 3 + [down_shape] * 3 + [shape((1, SPAN), f32)],
        [],
        cost(1e6, 2e6),
        *mlp_sums, up_master, up_first, up_second, down_master, down_first, down_second,
    )
    lines = -(-(2 * tiles + 5) // 16) * 16
    attn_moment1, attn_moment2, attn_step, message = flat(
        functools.partial(attn_step_kernel, len(attn_sums), fast),
        "attn_step",
        [attn_shape] * 3 + [shape((nb * ng, lines, SPAN), b16)],
        [pltpu.VMEM((lines, SPAN), f32)],
        cost(1e6, 2e6),
        *attn_sums, attn_master, attn_first, attn_second, line, ln_one, own,
    )
    every = lax.all_to_all(message, ("blk", "group"), 0, 0, tiled=True)

    def low(like_this):
        return shape(like_this.shape, b16)

    ln_shape = shape(ln_params.shape, f32)
    (attn_new, attn_copy, up_new, up_copy, down_new, down_copy,
     ln_moment1, ln_moment2, ln_new, norms) = flat(
        functools.partial(final_kernel, ng, fast),
        "final",
        [attn_shape, low(attn_master), up_shape, low(up_master), down_shape, low(down_master)]
        + [ln_shape] * 3 + [shape((2, 6), f32)],
        [pltpu.VMEM((lines, SPAN), f32), pltpu.VMEM((4, width), f32)],
        cost(1e6, 2e6),
        every, ln_two, attn_master, attn_step, up_master, up_step, down_master, down_step,
        ln_params, ln_first, ln_second,
    )
    return (
        block_out, input_grad,
        attn_moment1, attn_moment2, attn_new, attn_copy,
        up_moment1, up_moment2, up_new, up_copy,
        down_moment1, down_moment2, down_new, down_copy,
        ln_moment1, ln_moment2, ln_new, norms,
    )


def solution(mesh):
    seq_spec = P("group", "blk", None)
    attn_spec = P(None, "blk", "group")
    flat_spec = P("blk", "group")
    return jax.shard_map(
        functools.partial(body, nb=mesh.shape["blk"], ng=mesh.shape["group"]),
        mesh=mesh,
        in_specs=(seq_spec, seq_spec, P("group"), P())
        + (attn_spec,) * 3
        + (flat_spec,) * 6
        + (P(), P()),
        out_specs=(seq_spec, seq_spec)
        + (attn_spec,) * 4
        + (flat_spec,) * 8
        + (P(),) * 4,
        check_vma=False,
    )
```

```python
import functools

import jax
import jax.numpy as jnp
from jax import lax
from jax.experimental import pallas as pl
from jax.experimental.pallas import tpu as pltpu
from jax.sharding import PartitionSpec as P

HEADS = 8
SPAN = 128
STEP = 5
CHUNKS = 2
ROW_STEPS = 5
BATCH = 4

masked_value = -1e30
decay_rate = 0.5
matrix_rate = 0.3
vector_rate = 0.5
weight_decay = 0.01
epsilon = 1e-06
gelu_a = 0.7978845608028654
gelu_b = 0.044715

f32 = jnp.float32
b16 = jnp.bfloat16
MIB = 1 << 20
NN = (((1,), (0,)), ((), ()))
NT = (((1,), (1,)), ((), ()))
TN = (((0,), (0,)), ((), ()))


def mm(a, b, dims=NN):
    return lax.dot_general(a, b, dims, preferred_element_type=f32)


def whole():
    return pl.BlockSpec(memory_space=pltpu.VMEM)


def scalars():
    return pl.BlockSpec(memory_space=pltpu.SMEM)


def per_step(*tail):
    zeros = (0,) * len(tail)
    return pl.BlockSpec((1,) + tail, lambda i: (i,) + zeros)


def fixed(*shape):
    zeros = (0,) * len(shape)
    return pl.BlockSpec(shape, lambda i: zeros)


def anywhere():
    return pl.BlockSpec(memory_space=pl.ANY)


def params(mib, steps=1):
    return pltpu.CompilerParams(
        dimension_semantics=("arbitrary",) * steps, vmem_limit_bytes=mib * MIB
    )


def cost(flops, nbytes, trans=0):
    return pl.CostEstimate(flops=int(flops), bytes_accessed=int(nbytes), transcendentals=int(trans))


def norm_parts(values):
    center = values - jnp.mean(values, -1, keepdims=True)
    spread = jnp.mean(center * center, -1, keepdims=True)
    inverse = lax.rsqrt(spread + 1e-05)
    return center * inverse, inverse


def norm_back(gradient, normal, inverse, gain):
    scaled = gradient * gain
    inner = jnp.mean(scaled, -1, keepdims=True)
    cross = jnp.mean(scaled * normal, -1, keepdims=True)
    return inverse * (scaled - inner - normal * cross)


def each_core(core, do):
    @pl.when(core == 0)
    def _():
        do(0, True)
        do(1, False)

    @pl.when(core != 0)
    def _():
        do(0, False)
        do(1, True)


def block(start, size):
    if isinstance(start, int):
        return slice(start, start + size)
    return pl.ds(pl.multiple_of(start, size), size)


def copy_attn(w_ref, own_refs, other_refs, spot, core, dims):
    groups, rows, cols, width = dims

    def do(c, mine):
        for move, buf_ref in enumerate(own_refs if mine else other_refs):
            place = move if spot is None else spot ^ move
            here = block((place * 2 + c) * rows, rows)
            for g in range(groups):
                for m in range(3):
                    at = (g * 3 + m) * rows
                    w_ref[here, m * width + g * cols : m * width + (g + 1) * cols] = buf_ref[
                        at : at + rows, :
                    ]

    each_core(core, do)


def prep_kernel(scal_ref, x_ref, ln_ref, normed_ref, rider_ref, sum_ref):
    i = pl.program_id(0)
    tok, width = x_ref.shape[1:]
    spans = tok // SPAN
    tiles = width // SPAN
    half = sum_ref.shape[0]
    normal, _ = norm_parts(x_ref[0].astype(f32))
    normed = (normal * ln_ref[0:1, :] + ln_ref[1:2, :]).astype(b16)
    normed_ref[0] = normed
    left = scal_ref[2 + i] - scal_ref[0] * tok
    row = lax.broadcasted_iota(jnp.int32, (16, tok), 0)
    col = lax.broadcasted_iota(jnp.int32, (16, tok), 1)
    chosen = jnp.where((col // SPAN == row) & (col < left), 1.0, 0.0)
    amount = jnp.maximum(jnp.sum(chosen, 1, keepdims=True), 1.0)
    total = mm(chosen.astype(b16), normed) / amount

    @pl.when(i == 0)
    def _():
        sum_ref[...] = jnp.zeros_like(sum_ref)

    for s in range(spans):
        for t in range(tiles):
            sum_ref[pl.ds((i * spans + s) * tiles + t, 1), :] = total[
                s : s + 1, t * SPAN : (t + 1) * SPAN
            ]

    @pl.when(i == pl.num_programs(0) - 1)
    def _():
        every = sum_ref[...]
        high = every.astype(b16)
        rider_ref[:half] = high
        rider_ref[half:] = (every - high.astype(f32)).astype(b16)


def pack_kernel(dims, in_ref, up_ref, down_ref, dep_ref, out_ref):
    rows, cols, sub, lanes = dims
    out_ref[:rows, :] = in_ref[0].astype(b16)
    at = rows
    for j in range(CHUNKS):
        for h in range(sub):
            c0 = (h * CHUNKS + j) * lanes
            out_ref[at : at + rows, :] = up_ref[:, c0 : c0 + lanes].astype(b16)
            at += rows
        out_ref[at : at + cols, :] = down_ref[j * lanes : (j + 1) * lanes, :].T.astype(b16)
        at += cols


def heads_apart(values):
    first = lax.broadcasted_iota(jnp.int32, values.shape, 1) < SPAN // 2
    zero = jnp.zeros_like(values)
    return jnp.concatenate([jnp.where(first, values, zero), jnp.where(first, zero, values)], 0)


def score_masks(scal_ref, i, span, spans, amount):
    length = scal_ref[2 + i]
    mine = scal_ref[0] * spans + span
    key = lax.broadcasted_iota(jnp.int32, (SPAN, 2 * SPAN), 0)
    query = lax.broadcasted_iota(jnp.int32, (SPAN, 2 * SPAN), 1) % SPAN
    local = (key <= query) & (key < length - mine * SPAN)
    index = lax.broadcasted_iota(jnp.int32, (amount, 2 * SPAN), 0)
    summary = (index < mine) & (index * SPAN < length)
    return local, summary


def own_heads(both):
    half = SPAN // 2
    return jnp.concatenate([both[:half, :SPAN], both[half:, SPAN:]], 0)


def gate_kernel(count, *refs):
    for in_ref, out_ref in zip(refs[:count], refs[-count:]):
        out_ref[...] = in_ref[...]


def forward_kernel(dims, fast, places, scal_ref, normed_ref, *refs):
    own_refs, refs = refs[:places], refs[places:]
    other_refs, refs = refs[:places], refs[places:]
    if fast:
        rown_refs, rother_refs = own_refs, other_refs
    else:
        rown_refs, refs = refs[:places], refs[places:]
        rother_refs, refs = refs[:places], refs[places:]
    (dep_ref, q_ref, k_ref, v_ref, ks_ref, vs_ref, nsum_ref, lse_ref, mixed_ref,
     w_ref, token_ref, sums_ref, line_ref) = refs
    i = pl.program_id(0)
    groups, rows, cols, width = dims
    tok = normed_ref.shape[1]
    spans = tok // SPAN
    tiles = width // SPAN
    amount = ks_ref.shape[1]
    factor = (width // HEADS) ** (-0.5)
    half = sums_ref.shape[2]
    base = groups * 3 * rows if fast else 0

    @pl.when(i == 0)
    def _():
        core = scal_ref[0] % 2
        spot = scal_ref[0] // 2 if fast else None
        copy_attn(w_ref, own_refs, other_refs, spot, core, dims)

        def do(c, mine):
            for move, buf_ref in enumerate(rown_refs if mine else rother_refs):
                place = spot ^ move if fast else move
                sums_ref[c, place] = buf_ref[base : base + half, :].astype(f32) + buf_ref[
                    base + half : base + 2 * half, :
                ].astype(f32)

        each_core(core, do)
        token_ref[...] = jnp.zeros_like(token_ref)

    for p in range(places):
        for c in range(2):
            for s in range(spans):
                for t in range(tiles):
                    r = (p * 2 + c) * spans + s
                    line_ref[r : r + 1, t * SPAN : (t + 1) * SPAN] = sums_ref[
                        c, p, pl.ds((i * spans + s) * tiles + t, 1), :
                    ]
    lines = line_ref[...]
    high = lines.astype(b16)
    low = (lines - high.astype(f32)).astype(b16)
    nsum_ref[0] = high
    normed = normed_ref[0]
    q_ref[0] = mm(normed, w_ref[:, :width]).astype(b16)
    k_ref[0] = mm(normed, w_ref[:, width : 2 * width]).astype(b16)
    v_ref[0] = mm(normed, w_ref[:, 2 * width : 3 * width]).astype(b16)
    sums = mm(high, w_ref[:, width : 3 * width]) + mm(low, w_ref[:, width : 3 * width])
    ks_ref[0] = sums[:, :width].astype(b16)
    vs_ref[0] = sums[:, width:].astype(b16)
    for span in range(spans):
        part = slice(span * SPAN, (span + 1) * SPAN)
        local, summary = score_masks(scal_ref, i, span, spans, amount)
        pairs = [slice(pair * SPAN, (pair + 1) * SPAN) for pair in range(tiles)]
        scores = []
        for lanes in pairs:
            query = heads_apart(q_ref[0, part, lanes] * b16(factor))
            keys = jnp.concatenate([k_ref[0, part, lanes], ks_ref[0, :, lanes]], 0)
            scores.append(mm(keys, query, NT))
        probs = []
        for pair in range(tiles):
            here = jnp.where(local, scores[pair][:SPAN], masked_value)
            there = jnp.where(summary, scores[pair][SPAN:], masked_value)
            top = jnp.maximum(jnp.max(here, 0, keepdims=True), jnp.max(there, 0, keepdims=True))
            here, there = jnp.exp(here - top), jnp.exp(there - top)
            total = jnp.sum(here, 0, keepdims=True) + jnp.sum(there, 0, keepdims=True)
            lse_ref[0, span, pair : pair + 1, :] = top + jnp.log(total)
            probs.append(
                (jnp.concatenate([here.astype(b16), there.astype(b16)], 0), 1.0 / total)
            )
        for lanes, (prob, inverse) in zip(pairs, probs):
            values = jnp.concatenate([v_ref[0, part, lanes], vs_ref[0, :, lanes]], 0)
            mixed_ref[lanes, part] = own_heads(mm(values, prob, TN) * inverse).astype(b16)


def mlp_kernel(dims, near, places, first, last, scal_ref, *refs):
    if first:
        mixed_ref, x_ref, ln_ref, *refs = refs
    else:
        mid_ref, *refs = refs
    g_ref, *refs = refs
    if near:
        own_refs, refs = refs[:places], refs[places:]
        other_refs, refs = refs[:places], refs[places:]
    else:
        full_ref, *refs = refs
        if first:
            out_ref, *refs = refs
    dep_ref, *refs = refs
    if last:
        x2_ref, y_in_ref, gm_in_ref, *refs = refs
    if first:
        x2_ref, mid_ref, wo_ref, token_ref, *refs = refs
    y_ref, gm_ref, keep_ref, send_ref, wu_ref, wd_ref, du_ref, dd_ref = refs
    groups, rows, cols, sub, lanes = dims
    size = sub * rows + cols
    extra = rows if first and near else 0
    i = pl.program_id(0)
    core = scal_ref[0] % 2

    def pieces(place, c, skip=0):
        b = place * 2 + c
        here = block(b * rows, rows)
        there = block(b * lanes, lanes)
        for g in range(groups):
            at = g * (size + skip)
            if skip:
                yield slice(at, at + rows), (here, slice(g * cols, (g + 1) * cols)), 2
                at += skip
            for h in range(sub):
                yield (
                    slice(at + h * rows, at + (h + 1) * rows),
                    (here, slice((g * sub + h) * lanes, (g * sub + h + 1) * lanes)),
                    0,
                )
            at += sub * rows
            yield slice(at, at + cols), (slice(g * cols, (g + 1) * cols), there), 1

    @pl.when(i == 0)
    def _():
        def fill(buf, there, here, kind):
            to_ref = wu_ref if kind == 0 else wd_ref if kind == 1 else wo_ref
            to_ref[here] = buf[there, :]

        def do(c, mine):
            for move, buf_ref in enumerate(own_refs if mine else other_refs):
                for there, here, kind in pieces((scal_ref[0] // 2) ^ move, c, extra):
                    fill(buf_ref, there, here, kind)

        if near:
            each_core(core, do)
        else:
            for b in range(2 * places):
                for k, (there, here, kind) in enumerate(pieces(b // 2, b % 2)):
                    g = k // (sub + 1)
                    there = slice(there.start - g * size, there.stop - g * size)
                    fill(full_ref.at[b * groups + g], there, here, kind)
                if first:
                    for g in range(groups):
                        wo_ref[b * rows : (b + 1) * rows, g * cols : (g + 1) * cols] = out_ref[
                            b * groups + g
                        ]
        du_ref[...] = jnp.zeros_like(du_ref)
        dd_ref[...] = jnp.zeros_like(dd_ref)
        if first:
            token_ref[...] = jnp.zeros_like(token_ref)

    if first:
        x2 = x_ref[...].astype(f32) + mm(mixed_ref[...], wo_ref[...], TN)
        x2_ref[...] = x2.astype(b16)
        normal, _ = norm_parts(x2)
        mid = (normal * ln_ref[2:3, :] + ln_ref[3:4, :]).astype(b16)
        mid_ref[...] = mid
    else:
        mid = mid_ref[...]
    g = g_ref[...]
    up = mm(mid, wu_ref[...])
    grad_act = mm(g, wd_ref[...])
    square = up * up
    half = 0.5 + 0.5 * jnp.tanh(up * (gelu_a + gelu_a * gelu_b * square))
    act = (up * half).astype(b16)
    slope = half + (up * half * (1.0 - half)) * (2.0 * gelu_a + 6.0 * gelu_a * gelu_b * square)
    grad_up = (slope * grad_act).astype(b16)
    y = mm(act, wd_ref[...], NT)
    gm = mm(grad_up, wu_ref[...], NT)
    if last:
        y_ref[...] = (x2_ref[...].astype(f32) + y_in_ref[...].astype(f32) + y).astype(b16)
        gm_ref[...] = (gm_in_ref[...].astype(f32) + gm).astype(b16)
    else:
        y_ref[...] = y.astype(b16)
        gm_ref[...] = gm.astype(b16)
    dd_ref[...] += mm(g, act, TN)
    du_ref[...] += mm(mid, grad_up, TN)

    @pl.when(i == pl.num_programs(0) - 1)
    def _():
        def do(c, mine):
            to_ref = keep_ref if mine else send_ref
            for place in range(places):
                for there, here, kind in pieces(place, c):
                    to_ref[place, there, :] = (dd_ref if kind else du_ref)[here].astype(b16)

        each_core(core, do)


def middle_kernel(
    gm_ref, g_ref, x2_ref, mixed_ref, w_ref, ln_ref, gx2_ref, do_ref, dwo_ref, lng_ref
):
    i = pl.program_id(0)

    @pl.when(i == 0)
    def _():
        dwo_ref[...] = jnp.zeros_like(dwo_ref)
        lng_ref[...] = jnp.zeros_like(lng_ref)

    gm = gm_ref[...].astype(f32)
    normal, inverse = norm_parts(x2_ref[...].astype(f32))
    lng_ref[0:1, :] += jnp.sum(gm * normal, 0, keepdims=True)
    lng_ref[1:2, :] += jnp.sum(gm, 0, keepdims=True)
    gx2 = g_ref[...].astype(f32) + norm_back(gm, normal, inverse, ln_ref[2:3, :])
    branch = gx2.astype(b16)
    gx2_ref[...] = branch
    dwo_ref[...] += mm(mixed_ref[...], branch)
    do_ref[...] = mm(branch, w_ref[...], NT).astype(b16)


def backward_kernel(
    places, scal_ref, do_ref, q_ref, k_ref, v_ref, lse_ref, ks_ref, vs_ref, w_ref, dep_ref,
    dqkv_ref, key_ref, value_ref, h_ref, dqt_ref,
):
    i = pl.program_id(0)
    tok, width = do_ref.shape[1:]
    spans = tok // SPAN
    tiles = width // SPAN
    amount = ks_ref.shape[1]
    factor = (width // HEADS) ** (-0.5)

    @pl.when(i == 0)
    def _():
        h_ref[...] = jnp.zeros_like(h_ref)

    key_parts, value_parts = [], []
    for span in range(spans):
        part = slice(span * SPAN, (span + 1) * SPAN)
        local, summary = score_masks(scal_ref, i, span, spans, amount)
        pairs = [slice(pair * SPAN, (pair + 1) * SPAN) for pair in range(tiles)]
        for two in range(0, tiles, BATCH):
            batch = pairs[two : two + BATCH]
            queries = [heads_apart(q_ref[0, part, lanes] * b16(factor)) for lanes in batch]
            grads = [heads_apart(do_ref[0, part, lanes]) for lanes in batch]
            keys = [
                jnp.concatenate([k_ref[0, part, lanes], ks_ref[0, :, lanes]], 0) for lanes in batch
            ]
            scores = [mm(key, query, NT) for key, query in zip(keys, queries)]
            changes = [
                mm(jnp.concatenate([v_ref[0, part, lanes], vs_ref[0, :, lanes]], 0), grad, NT)
                for lanes, grad in zip(batch, grads)
            ]
            lows, backs = [], []
            for k, (score, change) in enumerate(zip(scores, changes)):
                total = lse_ref[0, span, two + k : two + k + 1, :]
                here = jnp.exp(jnp.where(local, score[:SPAN], masked_value) - total)
                there = jnp.exp(jnp.where(summary, score[SPAN:], masked_value) - total)
                here_grad, there_grad = here * change[:SPAN], there * change[SPAN:]
                dot = jnp.sum(here_grad, 0, keepdims=True) + jnp.sum(there_grad, 0, keepdims=True)
                lows.append(jnp.concatenate([here.astype(b16), there.astype(b16)], 0))
                backs.append(
                    jnp.concatenate(
                        [
                            (here_grad - here * dot).astype(b16),
                            (there_grad - there * dot).astype(b16),
                        ],
                        0,
                    )
                )
            for k, lanes in enumerate(batch):
                grad_value = mm(lows[k], grads[k])
                grad_key = mm(backs[k], queries[k])
                dqt_ref[lanes, part] = (own_heads(mm(keys[k], backs[k], TN)) * factor).astype(b16)
                c0 = width + (two + k) * SPAN
                dqkv_ref[0, part, c0 : c0 + SPAN] = grad_key[:SPAN].astype(b16)
                dqkv_ref[0, part, c0 + width : c0 + width + SPAN] = grad_value[:SPAN].astype(b16)
                key_parts.append(grad_key[SPAN:])
                value_parts.append(grad_value[SPAN:])
    dqkv_ref[0, :, :width] = dqt_ref[...].T

    def joined(parts):
        return jnp.concatenate(
            [sum(parts[s * tiles + p] for s in range(spans)) for p in range(tiles)], 1
        ).astype(b16)

    key_part, value_part = joined(key_parts), joined(value_parts)
    key_ref[0], value_ref[0] = key_part, value_part
    extra = mm(key_part, w_ref[:, width : 2 * width], NT) + mm(
        value_part, w_ref[:, 2 * width : 3 * width], NT
    )
    for p in range(places):
        for c in range(2):
            for s in range(spans):
                for t in range(tiles):
                    r = (p * 2 + c) * spans + s
                    h_ref[c, p, pl.ds((i * spans + s) * tiles + t, 1), :] = extra[
                        r : r + 1, t * SPAN : (t + 1) * SPAN
                    ]


def grads_kernel(normed_ref, dqkv_ref, nsum_ref, key_ref, value_ref, dw_ref, nt_ref):
    width = normed_ref.shape[1]
    nt_ref[...] = normed_ref[...].T
    dw_ref[:, :width] = mm(nt_ref[...], dqkv_ref[:, :width])
    dw_ref[:, width : 2 * width] = mm(nt_ref[...], dqkv_ref[:, width : 2 * width]) + mm(
        nsum_ref[...], key_ref[...], TN
    )
    dw_ref[:, 2 * width :] = mm(nt_ref[...], dqkv_ref[:, 2 * width :]) + mm(
        nsum_ref[...], value_ref[...], TN
    )


def cut_kernel(dims, fast, scal_ref, dw_ref, dwo_ref, h_ref, two_ref, dep_ref, *refs):
    if fast:
        keep_ref, send_ref = refs
        hkeep_ref, hsend_ref = keep_ref, send_ref
    else:
        keep_ref, send_ref, hkeep_ref, hsend_ref = refs
    groups, rows, cols, width = dims
    places, half = h_ref.shape[1:3]
    tiles = width // SPAN
    base = groups * 4 * rows if fast else 0
    used = half - 8

    def do(c, mine):
        out_ref, hout_ref = (keep_ref, hkeep_ref) if mine else (send_ref, hsend_ref)
        for p in range(places):
            r0 = (p * 2 + c) * rows
            for g in range(groups):
                for m in range(4):
                    at = (g * 4 + m) * rows
                    from_ref = dwo_ref if m == 3 else dw_ref
                    c0 = g * cols if m == 3 else m * width + g * cols
                    out_ref[p, at : at + rows, :] = from_ref[
                        r0 : r0 + rows, c0 : c0 + cols
                    ].astype(b16)
            ride = h_ref[c, p]
            if fast:
                k, t = divmod(p * 2 + c, tiles)
                piece = two_ref[k : k + 1, t * SPAN : (t + 1) * SPAN]
                high = piece.astype(b16).astype(f32)
                row = lax.broadcasted_iota(jnp.int32, ride.shape, 0)
                ride = jnp.where(row == used, high, ride)
                ride = jnp.where(row == used + 1, piece - high, ride)
            hout_ref[p, base : base + half, :] = ride.astype(b16)

    each_core(scal_ref[0] % 2, do)


def project_kernel(dqkv_ref, w_ref, dep_ref, out_ref):
    out_ref[0] = mm(dqkv_ref[0], w_ref[:, : dqkv_ref.shape[2]], NT).astype(out_ref.dtype)


def input_kernel(scal_ref, grad_ref, gx2_ref, x_ref, h_ref, ln_ref, out_ref, lng_ref):
    i = pl.program_id(0)
    tok, width = x_ref.shape[1:]
    spans = tok // SPAN
    tiles = width // SPAN

    @pl.when(i == 0)
    def _():
        lng_ref[...] = jnp.zeros_like(lng_ref)

    left = scal_ref[2 + i] - scal_ref[0] * tok
    place = lax.broadcasted_iota(jnp.int32, (tok, 1), 0)
    extra = []
    for s in range(spans):
        part = slice(s * SPAN, (s + 1) * SPAN)
        amount = jnp.clip(left - s * SPAN, 0, SPAN)
        share = jnp.where(place[part] < left, 1.0, 0.0) / jnp.maximum(amount, 1).astype(f32)
        line = jnp.concatenate(
            [h_ref[pl.ds((i * spans + s) * tiles + t, 1), :] for t in range(tiles)], 1
        )
        extra.append(share * line)
    grad = grad_ref[0].astype(f32) + jnp.concatenate(extra, 0)
    normal, inverse = norm_parts(x_ref[0].astype(f32))
    lng_ref[0:1, :] += jnp.sum(grad * normal, 0, keepdims=True)
    lng_ref[1:2, :] += jnp.sum(grad, 0, keepdims=True)
    out_ref[0] = gx2_ref[0].astype(f32) + norm_back(grad, normal, inverse, ln_ref[0:1, :])


def spread_kernel(count, scal_ref, *refs):
    keeps, gets, outs = refs[:count], refs[count : 2 * count], refs[-4:]
    spot = scal_ref[0] // 2
    at = 0
    for keep_ref, get_ref in zip(keeps, gets):
        size = keep_ref.shape[1]
        for move in range(4):
            there = spot ^ move
            total = keep_ref[there].astype(f32) + get_ref[there].astype(f32)
            outs[move][at : at + size, :] = total.astype(outs[move].dtype)
        at += size


def halves_kernel(scal_ref, *refs):
    spot = scal_ref[0] // 2
    for j, far in enumerate((1, 2)):
        keep_ref, get_ref = refs[j], refs[2 + j]
        stay_ref, out_ref = refs[4 + 2 * j], refs[5 + 2 * j]
        near = 3 - far
        for k, (ref, move) in enumerate(
            ((stay_ref, 0), (stay_ref, near), (out_ref, far), (out_ref, far ^ near))
        ):
            there = spot ^ move
            total = keep_ref[there].astype(f32) + get_ref[there].astype(f32)
            ref[k % 2] = total.astype(ref.dtype)


def turn_kernel(*refs):
    for j in range(2):
        stay_ref, get_ref = refs[2 * j], refs[2 * j + 1]
        own_ref, out_ref = refs[4 + 2 * j], refs[5 + 2 * j]
        own_ref[...] = stay_ref[0] + get_ref[0].astype(f32)
        out_ref[...] = (stay_ref[1] + get_ref[1].astype(f32)).astype(b16)


def collect_kernel(sizes, count, scal_ref, *refs):
    z = scal_ref[1]
    groups = 4
    outs = refs[len(sizes) * count + 1 :]

    def total(terms, start, size):
        rows = pl.ds(start, size)
        value = terms[0][rows, :].astype(f32)
        for ref in terms[1:]:
            value = value + ref[rows, :].astype(f32)
        return value

    at = 0
    for k, size in enumerate(sizes):
        terms = refs[k * count : (k + 1) * count]
        for by in range(groups):
            start = pl.multiple_of(((z + by) % groups) * size, size)
            outs[by][at : at + size, :] = total(terms, start, size).astype(outs[by].dtype)
        at += size
    if len(outs) > groups:
        outs[groups][...] = total(terms, groups * size, outs[groups].shape[0])


def moments(gradient, first, second):
    corr = 1.0 - decay_rate**STEP
    new_first = decay_rate * first + (1.0 - decay_rate) * gradient
    new_second = decay_rate * second + (1.0 - decay_rate) * gradient * gradient
    return (new_first, new_second, new_first / corr / (jnp.sqrt(new_second / corr) + epsilon))


def lane_line(values):
    lane = lax.broadcasted_iota(jnp.int32, (1, SPAN), 1)
    line = jnp.zeros((1, SPAN), f32)
    for at, value in values.items():
        line = line + jnp.where(lane == at, value, 0.0)
    return line


def square_sum(values):
    return jnp.sum(jnp.sum(values * values, 0, keepdims=True), 1, keepdims=True)


def add_up(refs, rows):
    total = refs[0][rows, :].astype(f32)
    for ref in refs[1:]:
        total = total + ref[rows, :].astype(f32)
    return total


def mlp_step_kernel(dims, count, *refs):
    grads = refs[:count]
    (um_ref, uf_ref, us_ref, dm_ref, df_ref, ds_ref,
     u1_ref, u2_ref, ustep_ref, d1_ref, d2_ref, dstep_ref, line_ref) = refs[count:]
    rows, cols, sub, lanes = dims
    size = sub * rows + cols
    sums = [jnp.zeros((1, 1), f32) for _ in range(4)]
    for j in range(CHUNKS):
        for h in range(sub):
            start = j * size + h * rows
            at = (slice(None), slice((h * CHUNKS + j) * lanes, (h * CHUNKS + j + 1) * lanes))
            first, second, way = moments(
                add_up(grads, slice(start, start + rows)), uf_ref[at], us_ref[at]
            )
            step = way + weight_decay * um_ref[at]
            u1_ref[at], u2_ref[at], ustep_ref[at] = first, second, step
            sums[0] += square_sum(um_ref[at])
            sums[2] += square_sum(step)
        start = j * size + sub * rows
        at = (slice(j * lanes, (j + 1) * lanes), slice(None))
        first, second, way = moments(
            add_up(grads, slice(start, start + cols)).T, df_ref[at], ds_ref[at]
        )
        step = way + weight_decay * dm_ref[at]
        d1_ref[at], d2_ref[at], dstep_ref[at] = first, second, step
        sums[1] += square_sum(dm_ref[at])
        sums[3] += square_sum(step)
    line_ref[...] = lane_line({4: sums[0], 5: sums[1], 10: sums[2], 11: sums[3]})


def attn_step_kernel(count, fast, *refs):
    grads = refs[:count]
    (m_ref, f_ref, s_ref, line_ref, one_ref, h_ref,
     m1_ref, m2_ref, step_ref, out_ref, all_ref) = refs[count:]
    rows = m_ref.shape[1]
    tiles = one_ref.shape[1] // SPAN
    values = {}
    for m in range(4):
        first, second, way = moments(
            add_up(grads, slice(m * rows, (m + 1) * rows)), f_ref[m], s_ref[m]
        )
        step = way + weight_decay * m_ref[m]
        m1_ref[m], m2_ref[m], step_ref[m] = first, second, step
        values[m] = square_sum(m_ref[m])
        values[6 + m] = square_sum(step)
    all_ref[...] = jnp.zeros_like(all_ref)
    for k in range(2):
        for t in range(tiles):
            all_ref[k * tiles + t : k * tiles + t + 1, :] = one_ref[
                k : k + 1, t * SPAN : (t + 1) * SPAN
            ]
    at = 2 * tiles
    if fast:
        used = h_ref.shape[0] - 8
        piece = h_ref[used : used + 1, :] + h_ref[used + 1 : used + 2, :]
        high = piece.astype(b16).astype(f32)
        all_ref[at : at + 1, :] = high
        all_ref[at + 1 : at + 2, :] = piece - high
    line = lane_line(values) + line_ref[...]
    for k in range(3):
        piece = line.astype(b16).astype(f32)
        all_ref[at + 2 + k : at + 3 + k, :] = piece
        line = line - piece
    message = all_ref[...].astype(b16)
    for k in range(out_ref.shape[0]):
        out_ref[k] = message


def final_kernel(
    groups, fast, every_ref, two_ref, am_ref, as_ref, um_ref, us_ref, dm_ref, ds_ref, ln_ref, lf_ref, ls_ref,
    an_ref, ac_ref, un_ref, uc_ref, dn_ref, dc_ref, l1_ref, l2_ref, ln_new_ref, norms_ref,
    all_ref, grad_ref,
):
    width = ln_ref.shape[1]
    tiles = width // SPAN
    at = 2 * tiles
    total = None
    for b in range(every_ref.shape[0] // groups):
        part = every_ref[b * groups].astype(f32)
        for k in range(b * groups + 1, (b + 1) * groups):
            part = part + every_ref[k].astype(f32)
        if fast:
            k, t = divmod(b, tiles)
            grad_ref[2 + k : 3 + k, t * SPAN : (t + 1) * SPAN] = (
                part[at : at + 1, :] + part[at + 1 : at + 2, :]
            )
        total = part if total is None else total + part
    all_ref[...] = total
    for k in range(2):
        for t in range(tiles):
            grad_ref[k : k + 1, t * SPAN : (t + 1) * SPAN] = all_ref[
                k * tiles + t : k * tiles + t + 1, :
            ]
    if not fast:
        grad_ref[2:4, :] = two_ref[0:2, :]
    line = all_ref[at + 2 : at + 3, :] + all_ref[at + 3 : at + 4, :] + all_ref[at + 4 : at + 5, :]
    roots = jnp.sqrt(line)
    norms_ref[0:1, :] = roots[:, 0:6]
    norms_ref[1:2, :] = roots[:, 6:12]
    lane = lax.broadcasted_iota(jnp.int32, line.shape, 1)

    def rate(k):
        weight = jnp.sum(jnp.where(lane == k, roots, 0.0), 1, keepdims=True)
        square = jnp.sum(jnp.where(lane == 6 + k, line, 0.0), 1, keepdims=True)
        return matrix_rate * (weight / jnp.sqrt(square + epsilon))

    for m in range(4):
        new = am_ref[m] - rate(m) * as_ref[m]
        an_ref[m] = new
        ac_ref[m] = new.astype(b16)
    new = um_ref[...] - rate(4) * us_ref[...]
    un_ref[...] = new
    uc_ref[...] = new.astype(b16)
    new = dm_ref[...] - rate(5) * ds_ref[...]
    dn_ref[...] = new
    dc_ref[...] = new.astype(b16)
    first, second, way = moments(grad_ref[...], lf_ref[...], ls_ref[...])
    l1_ref[...], l2_ref[...] = first, second
    ln_new_ref[...] = ln_ref[...] - vector_rate * way


def fast_mesh(nb, ng, width):
    return nb == 8 and ng == 4 and width // ng == SPAN


def shift(values, by, ng):
    return lax.ppermute(values, "group", [(j, (j + by) % ng) for j in range(ng)])


def cross(values, bit, nb):
    return lax.ppermute(values, "blk", [(j, j ^ bit) for j in range(nb)])


def put(buffer, piece, at):
    return lax.dynamic_update_slice(buffer, piece[None], (at,) + (0,) * piece.ndim)


def take(buffer, at):
    return lax.dynamic_index_in_dim(buffer, at, 0, keepdims=False)


def gather_group(piece, z, ng):
    out = put(jnp.zeros((ng,) + piece.shape, piece.dtype), piece, z)
    for by in range(1, ng):
        out = put(out, shift(piece, by, ng), (z - by) % ng)
    return out.reshape((-1,) + piece.shape[1:])


def gather_plane(piece, nb):
    return [piece] + [cross(piece, 2 * move, nb) for move in range(1, nb // 2)]


def gather_cut(piece, cuts, z, ng):
    came = [(piece, z)] + [(shift(piece, by, ng), (z - by) % ng) for by in range(1, ng)]
    outs = []
    for start, stop in cuts:
        out = jnp.zeros((ng, stop - start, piece.shape[1]), piece.dtype)
        for part, at in came:
            out = put(out, part[start:stop], at)
        outs.append(out.reshape(-1, piece.shape[1]))
    return outs


def other_core(pieces, nb):
    return [cross(piece, 1, nb) for piece in pieces]


def body(
    tokens, cotangent, lengths, ln_params, attn_master, attn_first, attn_second,
    up_master, up_first, up_second, down_master, down_first, down_second, ln_first, ln_second,
    *, nb, ng,
):
    seqs, tok, width = tokens.shape
    spans = tok // SPAN
    tiles = width // SPAN
    amount = nb * spans
    rows, cols = attn_master.shape[1:]
    ff_rows = down_master.shape[0]
    sub = nb // ng
    lanes = ff_rows // CHUNKS
    inner = nb * lanes
    places = nb // 2
    size = sub * rows + cols
    attn_rows = ng * 4 * rows
    half = -(-(seqs * spans * tiles + 8) // 16) * 16
    b, z = lax.axis_index("blk").astype(jnp.int32), lax.axis_index("group").astype(jnp.int32)
    core = b % 2
    fast = fast_mesh(nb, ng, width)
    scal = jnp.concatenate([jnp.stack([b, z]), lengths.astype(jnp.int32)])
    shape = jax.ShapeDtypeStruct

    def like(dtype, *tail):
        return shape((seqs,) + tail, dtype)

    def gather_any(piece, over=("blk", "group")):
        every = lax.all_gather(piece, over)
        every = every.reshape((places, 2, -1) + piece.shape[1:])
        every = jnp.swapaxes(every, 0, 1)
        own, other = take(every, core), take(every, 1 - core)
        return [own[p] for p in range(places)], [other[p] for p in range(places)]

    def reduce_any(keep, send, blocks):
        both = jnp.stack([jnp.where(core == 0, keep, send), jnp.where(core == 0, send, keep)])
        both = jnp.swapaxes(both, 0, 1).reshape((nb,) + keep.shape[1:])
        mine = lax.psum_scatter(both, "blk", scatter_dimension=0)
        if not blocks:
            return mine.astype(f32)
        mine = mine.reshape((ng, -1) + mine.shape[1:])
        return lax.psum_scatter(mine, "group", scatter_dimension=0).astype(f32)

    def flat(call, name, outs, scratch, work, *args, scalar=False):
        return pl.pallas_call(
            call,
            in_specs=[scalars()] * scalar + [whole()] * (len(args) - scalar),
            out_specs=[whole()] * len(outs),
            out_shape=outs,
            scratch_shapes=scratch,
            compiler_params=pltpu.CompilerParams(vmem_limit_bytes=16 * MIB),
            cost_estimate=work,
            name=name,
        )(*args)

    pack_dims = (rows, cols, sub, lanes)

    attn_piece = attn_master[:3].astype(b16).reshape(3 * rows, cols)
    if fast:
        attn_z = gather_group(attn_piece, z, ng)
    normed, rider = pl.pallas_call(
        prep_kernel,
        grid=(seqs,),
        in_specs=[scalars(), per_step(tok, width), fixed(4, width)],
        out_specs=[per_step(tok, width), fixed(2 * half, SPAN)],
        out_shape=[like(b16, tok, width), shape((2 * half, SPAN), b16)],
        scratch_shapes=[pltpu.VMEM((half, SPAN), f32)],
        compiler_params=params(16),
        cost_estimate=cost(4e7, 2 * seqs * tok * width * 2),
        name="prep",
    )(scal, tokens, ln_params)

    def gate(pieces, *deps):
        return flat(
            functools.partial(gate_kernel, len(pieces)), "gate",
            [shape(piece.shape, b16) for piece in pieces], [], cost(1e6, 1e6), *pieces, *deps,
        )

    def everywhere(piece):
        return lax.all_gather(piece, ("blk", "group"))

    if fast:
        message = jnp.concatenate([attn_z, rider], 0)
        attn_own = gather_plane(message, nb)
        attn_bufs = attn_own + other_core(attn_own, nb)
        pack_out = shape((rows + CHUNKS * size, lanes), b16)
        piece = pl.pallas_call(
            functools.partial(pack_kernel, pack_dims),
            grid=(1,),
            in_specs=[
                pl.BlockSpec((1, rows, cols), lambda i: (3, 0, 0)), fixed(*up_master.shape),
                fixed(*down_master.shape), whole(),
            ],
            out_specs=fixed(*pack_out.shape),
            out_shape=pack_out,
            cost_estimate=cost(1e6, 1e6),
            name="pack",
        )(attn_master, up_master, down_master, attn_bufs[places])
        mlp_z, late_z = gather_cut(piece, [(0, rows + size), (rows + size, rows + 2 * size)], z, ng)
        mlp_own = gather_plane(mlp_z, nb)
        dep = mlp_z
    else:
        out_piece = attn_master[3].astype(b16)
        up_low = up_master.astype(b16).reshape(rows, sub, CHUNKS, lanes)
        down_low = down_master.astype(b16).T.reshape(cols, CHUNKS, lanes)
        attn_own, attn_other = gather_any(attn_piece)
        ride_own, ride_other = gather_any(rider, "blk")
        attn_bufs = attn_own + attn_other + ride_own + ride_other
        mlp_bufs = []
        for j in range(CHUNKS):
            piece = [jnp.swapaxes(up_low[:, :, j], 0, 1).reshape(sub * rows, lanes), down_low[:, j]]
            mlp_bufs.append([everywhere(jnp.concatenate(piece, 0))])
        mlp_bufs[0].append(everywhere(out_piece))
        dep = ln_params

    dims = (ng, rows, cols, width)
    act_bytes = seqs * tok * width
    q, k, v, ks, vs, nsum, lse, mixed, w_attn, token = pl.pallas_call(
        functools.partial(forward_kernel, dims, fast, places),
        grid=(seqs,),
        in_specs=[scalars(), per_step(tok, width)] + [whole()] * (len(attn_bufs) + 1),
        out_specs=[
            per_step(tok, width), per_step(tok, width), per_step(tok, width),
            per_step(amount, width), per_step(amount, width), per_step(amount, width),
            per_step(spans, tiles, 2 * SPAN),
            pl.BlockSpec((width, tok), lambda i: (0, i)),
            whole(), fixed(8, SPAN),
        ],
        out_shape=[
            like(b16, tok, width), like(b16, tok, width), like(b16, tok, width),
            like(b16, amount, width), like(b16, amount, width), like(b16, amount, width),
            like(f32, spans, tiles, 2 * SPAN),
            shape((width, seqs * tok), b16),
            shape((width, 3 * width), b16), shape((8, SPAN), f32),
        ],
        scratch_shapes=[
            pltpu.VMEM((2, places, half, SPAN), f32), pltpu.VMEM((amount, width), f32)
        ],
        compiler_params=params(16),
        cost_estimate=cost(8e9, act_bytes * 14),
        name="forward",
    )(scal, normed, *attn_bufs, dep)

    if fast:
        mlp_own[1:] = gate(mlp_own[1:], token)
        late_own = gather_plane(gate([late_z], token)[0], nb)
        mlp_bufs = [mlp_own + other_core(mlp_own, nb)]
        dep = late_own[0]
    mlp_dims = (ng, rows, cols, sub, lanes)
    mlp_out = shape((places, ng * size, lanes), b16)
    every_row = seqs * tok
    tile = every_row // ROW_STEPS
    flat_tokens, flat_cot = tokens.reshape(-1, width), cotangent.reshape(-1, width)
    by_rows = pl.BlockSpec((tile, width), lambda i: (i, 0))
    rows_out = shape((every_row, width), b16)
    keeps, sends = [], []
    y = gm = x2 = mid = wo = None
    for j in range(CHUNKS):
        first, last = j == 0, j == CHUNKS - 1
        if fast and not first:
            late_own[1:] = gate(late_own[1:], token)
            mlp_bufs.append(late_own + other_core(late_own, nb))
        if first:
            args = [scal, mixed, flat_tokens, ln_params, flat_cot]
            in_specs = [
                scalars(), pl.BlockSpec((width, tile), lambda i: (0, i)), by_rows, fixed(4, width),
                by_rows,
            ]
        else:
            args, in_specs = [scal, mid, flat_cot], [scalars(), by_rows, by_rows]
        args += [*mlp_bufs[j], dep]
        in_specs += [whole()] * (len(mlp_bufs[j]) + 1)
        outs = [(by_rows, rows_out), (by_rows, rows_out), (whole(), mlp_out), (whole(), mlp_out)]
        if first:
            outs = [
                (by_rows, rows_out), (by_rows, rows_out), (whole(), shape((width, width), b16)),
                (fixed(8, SPAN), shape((8, SPAN), f32)),
            ] + outs
        if last:
            args += [x2, y, gm]
            in_specs += [by_rows] * 3
        *more, y, gm, keep, send = pl.pallas_call(
            functools.partial(mlp_kernel, mlp_dims, fast, places, first, last),
            grid=(ROW_STEPS,),
            in_specs=in_specs,
            out_specs=[spec for spec, _ in outs],
            out_shape=[out for _, out in outs],
            scratch_shapes=[
                pltpu.VMEM((width, inner), b16), pltpu.VMEM((width, inner), b16),
                pltpu.VMEM((width, inner), f32), pltpu.VMEM((width, inner), f32),
            ],
            compiler_params=params(24),
            cost_estimate=cost(9e9, act_bytes * 20),
            name="mlp",
        )(*args)
        if first:
            x2, mid, wo, token = more
        keeps.append(keep)
        sends.append(send)
    block_out = y.reshape(tokens.shape)
    if fast:
        gets = [cross(send, 1, nb) for send in sends]

    by_tok = pl.BlockSpec((tok, width), lambda i: (i, 0))
    gx2, grad_mixed, dwo, ln_two = pl.pallas_call(
        middle_kernel,
        grid=(seqs,),
        in_specs=[
            by_tok, by_tok, by_tok, pl.BlockSpec((width, tok), lambda i: (0, i)), whole(),
            fixed(4, width),
        ],
        out_specs=[by_tok, by_tok, fixed(width, width), fixed(8, width)],
        out_shape=[rows_out, rows_out, shape((width, width), f32), shape((8, width), f32)],
        compiler_params=params(16),
        cost_estimate=cost(3e9, act_bytes * 14),
        name="middle",
    )(gm, flat_cot, x2, mixed, wo, ln_params)
    gx2, grad_mixed = gx2.reshape(tokens.shape), grad_mixed.reshape(tokens.shape)

    block = shape((ng * size, lanes), f32)
    block_low = shape((ng * size, lanes), b16)
    two, two_low = shape((2,) + block.shape, f32), shape((2,) + block.shape, b16)
    if fast:
        stay_a, out_a, stay_b, out_b = flat(
            halves_kernel, "halves", [two, two_low, two, two_low], [], cost(2e6, 16e6),
            scal, *keeps, *gets, scalar=True,
        )
        get_a, get_b = cross(out_a, 2, nb), cross(out_b, 4, nb)
        dep = stay_a
    else:
        dep = ln_two

    dqkv, key_part, value_part, h_part = pl.pallas_call(
        functools.partial(backward_kernel, places),
        grid=(seqs,),
        in_specs=[
            scalars(), per_step(tok, width),
            per_step(tok, width), per_step(tok, width), per_step(tok, width),
            per_step(spans, tiles, 2 * SPAN), per_step(amount, width), per_step(amount, width),
            whole(), anywhere(),
        ],
        out_specs=[
            per_step(tok, 3 * width), per_step(amount, width), per_step(amount, width), whole()
        ],
        out_shape=[
            like(b16, tok, 3 * width), like(b16, amount, width), like(b16, amount, width),
            shape((2, places, half, SPAN), f32),
        ],
        scratch_shapes=[pltpu.VMEM((width, tok), b16)],
        compiler_params=params(16),
        cost_estimate=cost(14e9, act_bytes * 24),
        name="backward",
    )(scal, grad_mixed, q, k, v, lse, ks, vs, w_attn, dep)

    if fast:
        own_a, out_a, own_b, out_b = flat(
            turn_kernel, "turn", [block, block_low] * 2, [], cost(1e6, 10e6),
            stay_a, get_a, stay_b, get_b,
        )
        mlp_parts = [own_a, cross(out_a, 4, nb), own_b, cross(out_b, 2, nb)]
        dep = own_a
    tail = half if fast else 0
    outs = [shape((places, attn_rows + tail, cols), b16)] * 2
    if not fast:
        outs += [shape((places, half, SPAN), b16)] * 2
    (dw,) = flat(
        grads_kernel, "grads", [shape((width, 3 * width), f32)],
        [pltpu.VMEM((width, seqs * tok), b16)], cost(1e6, 1e5),
        normed.reshape(-1, width), dqkv.reshape(-1, 3 * width), nsum.reshape(-1, width),
        key_part.reshape(-1, width), value_part.reshape(-1, width),
    )
    parts = flat(
        functools.partial(cut_kernel, dims, fast), "cut", outs, [], cost(1e6, 1e5),
        scal, dw, dwo, h_part, ln_two, dep, scalar=True,
    )

    def collect(terms, sizes, count, tail):
        outs = [shape((sum(sizes), SPAN), f32)] + [shape((sum(sizes), SPAN), b16)] * 3
        if tail:
            outs.append(shape((tail, SPAN), f32))
        return flat(
            functools.partial(collect_kernel, sizes, count), "collect", outs, [], cost(1e6, 4e6),
            scal, *terms, scalar=True,
        )

    if fast:
        attn_low = shape((attn_rows + tail, cols), b16)
        attn_parts = flat(
            functools.partial(spread_kernel, 1), "spread",
            [shape(attn_low.shape, f32)] + [attn_low] * 3, [], cost(1e6, 4e6),
            scal, parts[0], cross(parts[1], 1, nb), scalar=True,
        )
        dep = attn_parts[0]
        attn_parts = [dep] + [cross(attn_parts[m], 2 * m, nb) for m in range(1, 4)]
    else:
        dep = parts[2]

    grad_in = pl.pallas_call(
        project_kernel,
        grid=(seqs,),
        in_specs=[per_step(tok, 3 * width), whole(), anywhere()],
        out_specs=per_step(tok, width),
        out_shape=like(b16, tok, width),
        compiler_params=params(16),
        cost_estimate=cost(3e9, act_bytes * 8),
        name="project",
    )(dqkv, w_attn, dep)

    if fast:
        mlp_sums = collect(mlp_parts + [grad_in], (size,) * CHUNKS, 2, 0)
        mlp_sums = [mlp_sums[0]] + [shift(mlp_sums[by], by, ng) for by in range(1, ng)]
        *attn_sums, own = collect(attn_parts + [grad_in], (4 * rows,), 4, half)
        attn_sums = [attn_sums[0]] + [shift(attn_sums[by], by, ng) for by in range(1, ng)]
    else:
        own = reduce_any(parts[2], parts[3], False)
        attn_sums = [reduce_any(parts[0], parts[1], True)]
        mlp_sums = [
            jnp.concatenate([reduce_any(keep, send, True) for keep, send in zip(keeps, sends)], 0)
        ]
        ln_two = lax.psum(ln_two, ("blk", "group"))

    input_grad, ln_one = pl.pallas_call(
        input_kernel,
        grid=(seqs,),
        in_specs=[
            scalars(), per_step(tok, width), per_step(tok, width), per_step(tok, width),
            whole(), fixed(4, width),
        ],
        out_specs=[per_step(tok, width), fixed(8, width)],
        out_shape=[like(f32, tok, width), shape((8, width), f32)],
        compiler_params=params(16),
        cost_estimate=cost(1e8, act_bytes * 10),
        name="input",
    )(scal, grad_in, gx2, tokens, own, ln_params)

    attn_shape = shape(attn_master.shape, f32)
    up_shape, down_shape = shape(up_master.shape, f32), shape(down_master.shape, f32)
    up_moment1, up_moment2, up_step, down_moment1, down_moment2, down_step, line = flat(
        functools.partial(mlp_step_kernel, (rows, cols, sub, lanes), len(mlp_sums)),
        "mlp_step",
        [up_shape] * 3 + [down_shape] * 3 + [shape((1, SPAN), f32)],
        [],
        cost(1e6, 2e6),
        *mlp_sums, up_master, up_first, up_second, down_master, down_first, down_second,
    )
    lines = -(-(2 * tiles + 5) // 16) * 16
    attn_moment1, attn_moment2, attn_step, message = flat(
        functools.partial(attn_step_kernel, len(attn_sums), fast),
        "attn_step",
        [attn_shape] * 3 + [shape((nb * ng, lines, SPAN), b16)],
        [pltpu.VMEM((lines, SPAN), f32)],
        cost(1e6, 2e6),
        *attn_sums, attn_master, attn_first, attn_second, line, ln_one, own,
    )
    every = lax.all_to_all(message, ("blk", "group"), 0, 0, tiled=True)

    def low(like_this):
        return shape(like_this.shape, b16)

    ln_shape = shape(ln_params.shape, f32)
    (attn_new, attn_copy, up_new, up_copy, down_new, down_copy,
     ln_moment1, ln_moment2, ln_new, norms) = flat(
        functools.partial(final_kernel, ng, fast),
        "final",
        [attn_shape, low(attn_master), up_shape, low(up_master), down_shape, low(down_master)]
        + [ln_shape] * 3 + [shape((2, 6), f32)],
        [pltpu.VMEM((lines, SPAN), f32), pltpu.VMEM((4, width), f32)],
        cost(1e6, 2e6),
        every, ln_two, attn_master, attn_step, up_master, up_step, down_master, down_step,
        ln_params, ln_first, ln_second,
    )
    return (
        block_out, input_grad,
        attn_moment1, attn_moment2, attn_new, attn_copy,
        up_moment1, up_moment2, up_new, up_copy,
        down_moment1, down_moment2, down_new, down_copy,
        ln_moment1, ln_moment2, ln_new, norms,
    )


def solution(mesh):
    seq_spec = P("group", "blk", None)
    attn_spec = P(None, "blk", "group")
    flat_spec = P("blk", "group")
    return jax.shard_map(
        functools.partial(body, nb=mesh.shape["blk"], ng=mesh.shape["group"]),
        mesh=mesh,
        in_specs=(seq_spec, seq_spec, P("group"), P())
        + (attn_spec,) * 3
        + (flat_spec,) * 6
        + (P(), P()),
        out_specs=(seq_spec, seq_spec)
        + (attn_spec,) * 4
        + (flat_spec,) * 8
        + (P(),) * 4,
        check_vma=False,
    )
```

```python
import functools

import jax
import jax.numpy as jnp
from jax import lax
from jax.experimental import pallas as pl
from jax.experimental.pallas import tpu as pltpu
from jax.sharding import PartitionSpec as P

HEADS = 8
SPAN = 128
STEP = 5
CHUNKS = 2
ROW_STEPS = 5
BATCH = 4

masked_value = -1e30
decay_rate = 0.5
matrix_rate = 0.3
vector_rate = 0.5
weight_decay = 0.01
epsilon = 1e-06
gelu_a = 0.7978845608028654
gelu_b = 0.044715

f32 = jnp.float32
b16 = jnp.bfloat16
MIB = 1 << 20
NN = (((1,), (0,)), ((), ()))
NT = (((1,), (1,)), ((), ()))
TN = (((0,), (0,)), ((), ()))


def mm(a, b, dims=NN):
    return lax.dot_general(a, b, dims, preferred_element_type=f32)


def whole():
    return pl.BlockSpec(memory_space=pltpu.VMEM)


def scalars():
    return pl.BlockSpec(memory_space=pltpu.SMEM)


def per_step(*tail):
    zeros = (0,) * len(tail)
    return pl.BlockSpec((1,) + tail, lambda i: (i,) + zeros)


def fixed(*shape):
    zeros = (0,) * len(shape)
    return pl.BlockSpec(shape, lambda i: zeros)


def anywhere():
    return pl.BlockSpec(memory_space=pl.ANY)


def params(mib, steps=1):
    return pltpu.CompilerParams(
        dimension_semantics=("arbitrary",) * steps, vmem_limit_bytes=mib * MIB
    )


def cost(flops, nbytes, trans=0):
    return pl.CostEstimate(flops=int(flops * 0.03), bytes_accessed=int(nbytes * 0.03), transcendentals=int(trans))


def norm_parts(values):
    center = values - jnp.mean(values, -1, keepdims=True)
    spread = jnp.mean(center * center, -1, keepdims=True)
    inverse = lax.rsqrt(spread + 1e-05)
    return center * inverse, inverse


def norm_back(gradient, normal, inverse, gain):
    scaled = gradient * gain
    inner = jnp.mean(scaled, -1, keepdims=True)
    cross = jnp.mean(scaled * normal, -1, keepdims=True)
    return inverse * (scaled - inner - normal * cross)


def each_core(core, do):
    @pl.when(core == 0)
    def _():
        do(0, True)
        do(1, False)

    @pl.when(core != 0)
    def _():
        do(0, False)
        do(1, True)


def block(start, size):
    if isinstance(start, int):
        return slice(start, start + size)
    return pl.ds(pl.multiple_of(start, size), size)


def copy_attn(w_ref, own_refs, other_refs, spot, core, dims):
    groups, rows, cols, width = dims

    def do(c, mine):
        for move, buf_ref in enumerate(own_refs if mine else other_refs):
            place = move if spot is None else spot ^ move
            here = block((place * 2 + c) * rows, rows)
            for g in range(groups):
                for m in range(3):
                    at = (g * 3 + m) * rows
                    w_ref[here, m * width + g * cols : m * width + (g + 1) * cols] = buf_ref[
                        at : at + rows, :
                    ]

    each_core(core, do)


def prep_kernel(scal_ref, x_ref, ln_ref, normed_ref, rider_ref, sum_ref):
    i = pl.program_id(0)
    tok, width = x_ref.shape[1:]
    spans = tok // SPAN
    tiles = width // SPAN
    half = sum_ref.shape[0]
    normal, _ = norm_parts(x_ref[0].astype(f32))
    normed = (normal * ln_ref[0:1, :] + ln_ref[1:2, :]).astype(b16)
    normed_ref[0] = normed
    left = scal_ref[2 + i] - scal_ref[0] * tok
    row = lax.broadcasted_iota(jnp.int32, (16, tok), 0)
    col = lax.broadcasted_iota(jnp.int32, (16, tok), 1)
    chosen = jnp.where((col // SPAN == row) & (col < left), 1.0, 0.0)
    amount = jnp.maximum(jnp.sum(chosen, 1, keepdims=True), 1.0)
    total = mm(chosen.astype(b16), normed) / amount

    @pl.when(i == 0)
    def _():
        sum_ref[...] = jnp.zeros_like(sum_ref)

    for s in range(spans):
        for t in range(tiles):
            sum_ref[pl.ds((i * spans + s) * tiles + t, 1), :] = total[
                s : s + 1, t * SPAN : (t + 1) * SPAN
            ]

    @pl.when(i == pl.num_programs(0) - 1)
    def _():
        every = sum_ref[...]
        high = every.astype(b16)
        rider_ref[:half] = high
        rider_ref[half:] = (every - high.astype(f32)).astype(b16)


def pack_kernel(dims, in_ref, up_ref, down_ref, dep_ref, out_ref):
    rows, cols, sub, lanes = dims
    out_ref[:rows, :] = in_ref[0].astype(b16)
    at = rows
    for j in range(CHUNKS):
        for h in range(sub):
            c0 = (h * CHUNKS + j) * lanes
            out_ref[at : at + rows, :] = up_ref[:, c0 : c0 + lanes].astype(b16)
            at += rows
        out_ref[at : at + cols, :] = down_ref[j * lanes : (j + 1) * lanes, :].T.astype(b16)
        at += cols


def heads_apart(values):
    first = lax.broadcasted_iota(jnp.int32, values.shape, 1) < SPAN // 2
    zero = jnp.zeros_like(values)
    return jnp.concatenate([jnp.where(first, values, zero), jnp.where(first, zero, values)], 0)


def score_masks(scal_ref, i, span, spans, amount):
    length = scal_ref[2 + i]
    mine = scal_ref[0] * spans + span
    key = lax.broadcasted_iota(jnp.int32, (SPAN, 2 * SPAN), 0)
    query = lax.broadcasted_iota(jnp.int32, (SPAN, 2 * SPAN), 1) % SPAN
    local = (key <= query) & (key < length - mine * SPAN)
    index = lax.broadcasted_iota(jnp.int32, (amount, 2 * SPAN), 0)
    summary = (index < mine) & (index * SPAN < length)
    return local, summary


def own_heads(both):
    half = SPAN // 2
    return jnp.concatenate([both[:half, :SPAN], both[half:, SPAN:]], 0)


def gate_kernel(count, *refs):
    for in_ref, out_ref in zip(refs[:count], refs[-count:]):
        out_ref[...] = in_ref[...]


def forward_kernel(dims, fast, places, scal_ref, normed_ref, *refs):
    own_refs, refs = refs[:places], refs[places:]
    other_refs, refs = refs[:places], refs[places:]
    if fast:
        rown_refs, rother_refs = own_refs, other_refs
    else:
        rown_refs, refs = refs[:places], refs[places:]
        rother_refs, refs = refs[:places], refs[places:]
    (dep_ref, q_ref, k_ref, v_ref, ks_ref, vs_ref, nsum_ref, lse_ref, mixed_ref,
     w_ref, token_ref, sums_ref, line_ref) = refs
    i = pl.program_id(0)
    groups, rows, cols, width = dims
    tok = normed_ref.shape[1]
    spans = tok // SPAN
    tiles = width // SPAN
    amount = ks_ref.shape[1]
    factor = (width // HEADS) ** (-0.5)
    half = sums_ref.shape[2]
    base = groups * 3 * rows if fast else 0

    @pl.when(i == 0)
    def _():
        core = scal_ref[0] % 2
        spot = scal_ref[0] // 2 if fast else None
        copy_attn(w_ref, own_refs, other_refs, spot, core, dims)

        def do(c, mine):
            for move, buf_ref in enumerate(rown_refs if mine else rother_refs):
                place = spot ^ move if fast else move
                sums_ref[c, place] = buf_ref[base : base + half, :].astype(f32) + buf_ref[
                    base + half : base + 2 * half, :
                ].astype(f32)

        each_core(core, do)
        token_ref[...] = jnp.zeros_like(token_ref)

    for p in range(places):
        for c in range(2):
            for s in range(spans):
                for t in range(tiles):
                    r = (p * 2 + c) * spans + s
                    line_ref[r : r + 1, t * SPAN : (t + 1) * SPAN] = sums_ref[
                        c, p, pl.ds((i * spans + s) * tiles + t, 1), :
                    ]
    lines = line_ref[...]
    high = lines.astype(b16)
    low = (lines - high.astype(f32)).astype(b16)
    nsum_ref[0] = high
    normed = normed_ref[0]
    q_ref[0] = mm(normed, w_ref[:, :width]).astype(b16)
    k_ref[0] = mm(normed, w_ref[:, width : 2 * width]).astype(b16)
    v_ref[0] = mm(normed, w_ref[:, 2 * width : 3 * width]).astype(b16)
    sums = mm(high, w_ref[:, width : 3 * width]) + mm(low, w_ref[:, width : 3 * width])
    ks_ref[0] = sums[:, :width].astype(b16)
    vs_ref[0] = sums[:, width:].astype(b16)
    for span in range(spans):
        part = slice(span * SPAN, (span + 1) * SPAN)
        local, summary = score_masks(scal_ref, i, span, spans, amount)
        pairs = [slice(pair * SPAN, (pair + 1) * SPAN) for pair in range(tiles)]
        scores = []
        for lanes in pairs:
            query = heads_apart(q_ref[0, part, lanes] * b16(factor))
            keys = jnp.concatenate([k_ref[0, part, lanes], ks_ref[0, :, lanes]], 0)
            scores.append(mm(keys, query, NT))
        probs = []
        for pair in range(tiles):
            here = jnp.where(local, scores[pair][:SPAN], masked_value)
            there = jnp.where(summary, scores[pair][SPAN:], masked_value)
            top = jnp.maximum(jnp.max(here, 0, keepdims=True), jnp.max(there, 0, keepdims=True))
            here, there = jnp.exp(here - top), jnp.exp(there - top)
            total = jnp.sum(here, 0, keepdims=True) + jnp.sum(there, 0, keepdims=True)
            lse_ref[0, span, pair : pair + 1, :] = top + jnp.log(total)
            probs.append(
                (jnp.concatenate([here.astype(b16), there.astype(b16)], 0), 1.0 / total)
            )
        for lanes, (prob, inverse) in zip(pairs, probs):
            values = jnp.concatenate([v_ref[0, part, lanes], vs_ref[0, :, lanes]], 0)
            mixed_ref[lanes, part] = own_heads(mm(values, prob, TN) * inverse).astype(b16)


def mlp_kernel(dims, near, places, first, last, scal_ref, *refs):
    if first:
        mixed_ref, x_ref, ln_ref, *refs = refs
    else:
        mid_ref, *refs = refs
    g_ref, *refs = refs
    if near:
        own_refs, refs = refs[:places], refs[places:]
        other_refs, refs = refs[:places], refs[places:]
    else:
        full_ref, *refs = refs
        if first:
            out_ref, *refs = refs
    dep_ref, *refs = refs
    if last:
        x2_ref, y_in_ref, gm_in_ref, *refs = refs
    if first:
        x2_ref, mid_ref, wo_ref, token_ref, *refs = refs
    y_ref, gm_ref, keep_ref, send_ref, wu_ref, wd_ref, du_ref, dd_ref = refs
    groups, rows, cols, sub, lanes = dims
    size = sub * rows + cols
    extra = rows if first and near else 0
    i = pl.program_id(0)
    core = scal_ref[0] % 2

    def pieces(place, c, skip=0):
        b = place * 2 + c
        here = block(b * rows, rows)
        there = block(b * lanes, lanes)
        for g in range(groups):
            at = g * (size + skip)
            if skip:
                yield slice(at, at + rows), (here, slice(g * cols, (g + 1) * cols)), 2
                at += skip
            for h in range(sub):
                yield (
                    slice(at + h * rows, at + (h + 1) * rows),
                    (here, slice((g * sub + h) * lanes, (g * sub + h + 1) * lanes)),
                    0,
                )
            at += sub * rows
            yield slice(at, at + cols), (slice(g * cols, (g + 1) * cols), there), 1

    @pl.when(i == 0)
    def _():
        def fill(buf, there, here, kind):
            to_ref = wu_ref if kind == 0 else wd_ref if kind == 1 else wo_ref
            to_ref[here] = buf[there, :]

        def do(c, mine):
            for move, buf_ref in enumerate(own_refs if mine else other_refs):
                for there, here, kind in pieces((scal_ref[0] // 2) ^ move, c, extra):
                    fill(buf_ref, there, here, kind)

        if near:
            each_core(core, do)
        else:
            for b in range(2 * places):
                for k, (there, here, kind) in enumerate(pieces(b // 2, b % 2)):
                    g = k // (sub + 1)
                    there = slice(there.start - g * size, there.stop - g * size)
                    fill(full_ref.at[b * groups + g], there, here, kind)
                if first:
                    for g in range(groups):
                        wo_ref[b * rows : (b + 1) * rows, g * cols : (g + 1) * cols] = out_ref[
                            b * groups + g
                        ]
        du_ref[...] = jnp.zeros_like(du_ref)
        dd_ref[...] = jnp.zeros_like(dd_ref)
        if first:
            token_ref[...] = jnp.zeros_like(token_ref)

    if first:
        x2 = x_ref[...].astype(f32) + mm(mixed_ref[...], wo_ref[...], TN)
        x2_ref[...] = x2.astype(b16)
        normal, _ = norm_parts(x2)
        mid = (normal * ln_ref[2:3, :] + ln_ref[3:4, :]).astype(b16)
        mid_ref[...] = mid
    else:
        mid = mid_ref[...]
    g = g_ref[...]
    up = mm(mid, wu_ref[...])
    grad_act = mm(g, wd_ref[...])
    square = up * up
    half = 0.5 + 0.5 * jnp.tanh(up * (gelu_a + gelu_a * gelu_b * square))
    act = (up * half).astype(b16)
    slope = half + (up * half * (1.0 - half)) * (2.0 * gelu_a + 6.0 * gelu_a * gelu_b * square)
    grad_up = (slope * grad_act).astype(b16)
    y = mm(act, wd_ref[...], NT)
    gm = mm(grad_up, wu_ref[...], NT)
    if last:
        y_ref[...] = (x2_ref[...].astype(f32) + y_in_ref[...].astype(f32) + y).astype(b16)
        gm_ref[...] = (gm_in_ref[...].astype(f32) + gm).astype(b16)
    else:
        y_ref[...] = y.astype(b16)
        gm_ref[...] = gm.astype(b16)
    dd_ref[...] += mm(g, act, TN)
    du_ref[...] += mm(mid, grad_up, TN)

    @pl.when(i == pl.num_programs(0) - 1)
    def _():
        def do(c, mine):
            to_ref = keep_ref if mine else send_ref
            for place in range(places):
                for there, here, kind in pieces(place, c):
                    to_ref[place, there, :] = (dd_ref if kind else du_ref)[here].astype(b16)

        each_core(core, do)


def middle_kernel(
    gm_ref, g_ref, x2_ref, mixed_ref, w_ref, ln_ref, gx2_ref, do_ref, dwo_ref, lng_ref
):
    i = pl.program_id(0)

    @pl.when(i == 0)
    def _():
        dwo_ref[...] = jnp.zeros_like(dwo_ref)
        lng_ref[...] = jnp.zeros_like(lng_ref)

    gm = gm_ref[...].astype(f32)
    normal, inverse = norm_parts(x2_ref[...].astype(f32))
    lng_ref[0:1, :] += jnp.sum(gm * normal, 0, keepdims=True)
    lng_ref[1:2, :] += jnp.sum(gm, 0, keepdims=True)
    gx2 = g_ref[...].astype(f32) + norm_back(gm, normal, inverse, ln_ref[2:3, :])
    branch = gx2.astype(b16)
    gx2_ref[...] = branch
    dwo_ref[...] += mm(mixed_ref[...], branch)
    do_ref[...] = mm(branch, w_ref[...], NT).astype(b16)


def backward_kernel(
    places, scal_ref, do_ref, q_ref, k_ref, v_ref, lse_ref, ks_ref, vs_ref, w_ref, dep_ref,
    dqkv_ref, key_ref, value_ref, h_ref, dqt_ref,
):
    i = pl.program_id(0)
    tok, width = do_ref.shape[1:]
    spans = tok // SPAN
    tiles = width // SPAN
    amount = ks_ref.shape[1]
    factor = (width // HEADS) ** (-0.5)

    @pl.when(i == 0)
    def _():
        h_ref[...] = jnp.zeros_like(h_ref)

    key_parts, value_parts = [], []
    for span in range(spans):
        part = slice(span * SPAN, (span + 1) * SPAN)
        local, summary = score_masks(scal_ref, i, span, spans, amount)
        pairs = [slice(pair * SPAN, (pair + 1) * SPAN) for pair in range(tiles)]
        for two in range(0, tiles, BATCH):
            batch = pairs[two : two + BATCH]
            queries = [heads_apart(q_ref[0, part, lanes] * b16(factor)) for lanes in batch]
            grads = [heads_apart(do_ref[0, part, lanes]) for lanes in batch]
            keys = [
                jnp.concatenate([k_ref[0, part, lanes], ks_ref[0, :, lanes]], 0) for lanes in batch
            ]
            scores = [mm(key, query, NT) for key, query in zip(keys, queries)]
            changes = [
                mm(jnp.concatenate([v_ref[0, part, lanes], vs_ref[0, :, lanes]], 0), grad, NT)
                for lanes, grad in zip(batch, grads)
            ]
            lows, backs = [], []
            for k, (score, change) in enumerate(zip(scores, changes)):
                total = lse_ref[0, span, two + k : two + k + 1, :]
                here = jnp.exp(jnp.where(local, score[:SPAN], masked_value) - total)
                there = jnp.exp(jnp.where(summary, score[SPAN:], masked_value) - total)
                here_grad, there_grad = here * change[:SPAN], there * change[SPAN:]
                dot = jnp.sum(here_grad, 0, keepdims=True) + jnp.sum(there_grad, 0, keepdims=True)
                lows.append(jnp.concatenate([here.astype(b16), there.astype(b16)], 0))
                backs.append(
                    jnp.concatenate(
                        [
                            (here_grad - here * dot).astype(b16),
                            (there_grad - there * dot).astype(b16),
                        ],
                        0,
                    )
                )
            for k, lanes in enumerate(batch):
                grad_value = mm(lows[k], grads[k])
                grad_key = mm(backs[k], queries[k])
                dqt_ref[lanes, part] = (own_heads(mm(keys[k], backs[k], TN)) * factor).astype(b16)
                c0 = width + (two + k) * SPAN
                dqkv_ref[0, part, c0 : c0 + SPAN] = grad_key[:SPAN].astype(b16)
                dqkv_ref[0, part, c0 + width : c0 + width + SPAN] = grad_value[:SPAN].astype(b16)
                key_parts.append(grad_key[SPAN:])
                value_parts.append(grad_value[SPAN:])
    dqkv_ref[0, :, :width] = dqt_ref[...].T

    def joined(parts):
        return jnp.concatenate(
            [sum(parts[s * tiles + p] for s in range(spans)) for p in range(tiles)], 1
        ).astype(b16)

    key_part, value_part = joined(key_parts), joined(value_parts)
    key_ref[0], value_ref[0] = key_part, value_part
    extra = mm(key_part, w_ref[:, width : 2 * width], NT) + mm(
        value_part, w_ref[:, 2 * width : 3 * width], NT
    )
    for p in range(places):
        for c in range(2):
            for s in range(spans):
                for t in range(tiles):
                    r = (p * 2 + c) * spans + s
                    h_ref[c, p, pl.ds((i * spans + s) * tiles + t, 1), :] = extra[
                        r : r + 1, t * SPAN : (t + 1) * SPAN
                    ]


def grads_kernel(normed_ref, dqkv_ref, nsum_ref, key_ref, value_ref, dw_ref, nt_ref):
    width = normed_ref.shape[1]
    nt_ref[...] = normed_ref[...].T
    dw_ref[:, :width] = mm(nt_ref[...], dqkv_ref[:, :width])
    dw_ref[:, width : 2 * width] = mm(nt_ref[...], dqkv_ref[:, width : 2 * width]) + mm(
        nsum_ref[...], key_ref[...], TN
    )
    dw_ref[:, 2 * width :] = mm(nt_ref[...], dqkv_ref[:, 2 * width :]) + mm(
        nsum_ref[...], value_ref[...], TN
    )


def cut_kernel(dims, fast, scal_ref, dw_ref, dwo_ref, h_ref, two_ref, dep_ref, *refs):
    if fast:
        keep_ref, send_ref = refs
        hkeep_ref, hsend_ref = keep_ref, send_ref
    else:
        keep_ref, send_ref, hkeep_ref, hsend_ref = refs
    groups, rows, cols, width = dims
    places, half = h_ref.shape[1:3]
    tiles = width // SPAN
    base = groups * 4 * rows if fast else 0
    used = half - 8

    def do(c, mine):
        out_ref, hout_ref = (keep_ref, hkeep_ref) if mine else (send_ref, hsend_ref)
        for p in range(places):
            r0 = (p * 2 + c) * rows
            for g in range(groups):
                for m in range(4):
                    at = (g * 4 + m) * rows
                    from_ref = dwo_ref if m == 3 else dw_ref
                    c0 = g * cols if m == 3 else m * width + g * cols
                    out_ref[p, at : at + rows, :] = from_ref[
                        r0 : r0 + rows, c0 : c0 + cols
                    ].astype(b16)
            ride = h_ref[c, p]
            if fast:
                k, t = divmod(p * 2 + c, tiles)
                piece = two_ref[k : k + 1, t * SPAN : (t + 1) * SPAN]
                high = piece.astype(b16).astype(f32)
                row = lax.broadcasted_iota(jnp.int32, ride.shape, 0)
                ride = jnp.where(row == used, high, ride)
                ride = jnp.where(row == used + 1, piece - high, ride)
            hout_ref[p, base : base + half, :] = ride.astype(b16)

    each_core(scal_ref[0] % 2, do)


def project_kernel(dqkv_ref, w_ref, dep_ref, out_ref):
    out_ref[0] = mm(dqkv_ref[0], w_ref[:, : dqkv_ref.shape[2]], NT).astype(out_ref.dtype)


def input_kernel(scal_ref, grad_ref, gx2_ref, x_ref, h_ref, ln_ref, out_ref, lng_ref):
    i = pl.program_id(0)
    tok, width = x_ref.shape[1:]
    spans = tok // SPAN
    tiles = width // SPAN

    @pl.when(i == 0)
    def _():
        lng_ref[...] = jnp.zeros_like(lng_ref)

    left = scal_ref[2 + i] - scal_ref[0] * tok
    place = lax.broadcasted_iota(jnp.int32, (tok, 1), 0)
    extra = []
    for s in range(spans):
        part = slice(s * SPAN, (s + 1) * SPAN)
        amount = jnp.clip(left - s * SPAN, 0, SPAN)
        share = jnp.where(place[part] < left, 1.0, 0.0) / jnp.maximum(amount, 1).astype(f32)
        line = jnp.concatenate(
            [h_ref[pl.ds((i * spans + s) * tiles + t, 1), :] for t in range(tiles)], 1
        )
        extra.append(share * line)
    grad = grad_ref[0].astype(f32) + jnp.concatenate(extra, 0)
    normal, inverse = norm_parts(x_ref[0].astype(f32))
    lng_ref[0:1, :] += jnp.sum(grad * normal, 0, keepdims=True)
    lng_ref[1:2, :] += jnp.sum(grad, 0, keepdims=True)
    out_ref[0] = gx2_ref[0].astype(f32) + norm_back(grad, normal, inverse, ln_ref[0:1, :])


def spread_kernel(count, scal_ref, *refs):
    keeps, gets, outs = refs[:count], refs[count : 2 * count], refs[-4:]
    spot = scal_ref[0] // 2
    at = 0
    for keep_ref, get_ref in zip(keeps, gets):
        size = keep_ref.shape[1]
        for move in range(4):
            there = spot ^ move
            total = keep_ref[there].astype(f32) + get_ref[there].astype(f32)
            outs[move][at : at + size, :] = total.astype(outs[move].dtype)
        at += size


def halves_kernel(scal_ref, *refs):
    spot = scal_ref[0] // 2
    for j, far in enumerate((1, 2)):
        keep_ref, get_ref = refs[j], refs[2 + j]
        stay_ref, out_ref = refs[4 + 2 * j], refs[5 + 2 * j]
        near = 3 - far
        for k, (ref, move) in enumerate(
            ((stay_ref, 0), (stay_ref, near), (out_ref, far), (out_ref, far ^ near))
        ):
            there = spot ^ move
            total = keep_ref[there].astype(f32) + get_ref[there].astype(f32)
            ref[k % 2] = total.astype(ref.dtype)


def turn_kernel(*refs):
    for j in range(2):
        stay_ref, get_ref = refs[2 * j], refs[2 * j + 1]
        own_ref, out_ref = refs[4 + 2 * j], refs[5 + 2 * j]
        own_ref[...] = stay_ref[0] + get_ref[0].astype(f32)
        out_ref[...] = (stay_ref[1] + get_ref[1].astype(f32)).astype(b16)


def collect_kernel(sizes, count, scal_ref, *refs):
    z = scal_ref[1]
    groups = 4
    outs = refs[len(sizes) * count + 1 :]

    def total(terms, start, size):
        rows = pl.ds(start, size)
        value = terms[0][rows, :].astype(f32)
        for ref in terms[1:]:
            value = value + ref[rows, :].astype(f32)
        return value

    at = 0
    for k, size in enumerate(sizes):
        terms = refs[k * count : (k + 1) * count]
        for by in range(groups):
            start = pl.multiple_of(((z + by) % groups) * size, size)
            outs[by][at : at + size, :] = total(terms, start, size).astype(outs[by].dtype)
        at += size
    if len(outs) > groups:
        outs[groups][...] = total(terms, groups * size, outs[groups].shape[0])


def moments(gradient, first, second):
    corr = 1.0 - decay_rate**STEP
    new_first = decay_rate * first + (1.0 - decay_rate) * gradient
    new_second = decay_rate * second + (1.0 - decay_rate) * gradient * gradient
    return (new_first, new_second, new_first / corr / (jnp.sqrt(new_second / corr) + epsilon))


def lane_line(values):
    lane = lax.broadcasted_iota(jnp.int32, (1, SPAN), 1)
    line = jnp.zeros((1, SPAN), f32)
    for at, value in values.items():
        line = line + jnp.where(lane == at, value, 0.0)
    return line


def square_sum(values):
    return jnp.sum(jnp.sum(values * values, 0, keepdims=True), 1, keepdims=True)


def add_up(refs, rows):
    total = refs[0][rows, :].astype(f32)
    for ref in refs[1:]:
        total = total + ref[rows, :].astype(f32)
    return total


def mlp_step_kernel(dims, count, *refs):
    grads = refs[:count]
    (um_ref, uf_ref, us_ref, dm_ref, df_ref, ds_ref,
     u1_ref, u2_ref, ustep_ref, d1_ref, d2_ref, dstep_ref, line_ref) = refs[count:]
    rows, cols, sub, lanes = dims
    size = sub * rows + cols
    sums = [jnp.zeros((1, 1), f32) for _ in range(4)]
    for j in range(CHUNKS):
        for h in range(sub):
            start = j * size + h * rows
            at = (slice(None), slice((h * CHUNKS + j) * lanes, (h * CHUNKS + j + 1) * lanes))
            first, second, way = moments(
                add_up(grads, slice(start, start + rows)), uf_ref[at], us_ref[at]
            )
            step = way + weight_decay * um_ref[at]
            u1_ref[at], u2_ref[at], ustep_ref[at] = first, second, step
            sums[0] += square_sum(um_ref[at])
            sums[2] += square_sum(step)
        start = j * size + sub * rows
        at = (slice(j * lanes, (j + 1) * lanes), slice(None))
        first, second, way = moments(
            add_up(grads, slice(start, start + cols)).T, df_ref[at], ds_ref[at]
        )
        step = way + weight_decay * dm_ref[at]
        d1_ref[at], d2_ref[at], dstep_ref[at] = first, second, step
        sums[1] += square_sum(dm_ref[at])
        sums[3] += square_sum(step)
    line_ref[...] = lane_line({4: sums[0], 5: sums[1], 10: sums[2], 11: sums[3]})


def attn_step_kernel(count, fast, *refs):
    grads = refs[:count]
    (m_ref, f_ref, s_ref, line_ref, one_ref, h_ref,
     m1_ref, m2_ref, step_ref, out_ref, all_ref) = refs[count:]
    rows = m_ref.shape[1]
    tiles = one_ref.shape[1] // SPAN
    values = {}
    for m in range(4):
        first, second, way = moments(
            add_up(grads, slice(m * rows, (m + 1) * rows)), f_ref[m], s_ref[m]
        )
        step = way + weight_decay * m_ref[m]
        m1_ref[m], m2_ref[m], step_ref[m] = first, second, step
        values[m] = square_sum(m_ref[m])
        values[6 + m] = square_sum(step)
    all_ref[...] = jnp.zeros_like(all_ref)
    for k in range(2):
        for t in range(tiles):
            all_ref[k * tiles + t : k * tiles + t + 1, :] = one_ref[
                k : k + 1, t * SPAN : (t + 1) * SPAN
            ]
    at = 2 * tiles
    if fast:
        used = h_ref.shape[0] - 8
        piece = h_ref[used : used + 1, :] + h_ref[used + 1 : used + 2, :]
        high = piece.astype(b16).astype(f32)
        all_ref[at : at + 1, :] = high
        all_ref[at + 1 : at + 2, :] = piece - high
    line = lane_line(values) + line_ref[...]
    for k in range(3):
        piece = line.astype(b16).astype(f32)
        all_ref[at + 2 + k : at + 3 + k, :] = piece
        line = line - piece
    message = all_ref[...].astype(b16)
    for k in range(out_ref.shape[0]):
        out_ref[k] = message


def final_kernel(
    groups, fast, every_ref, two_ref, am_ref, as_ref, um_ref, us_ref, dm_ref, ds_ref, ln_ref, lf_ref, ls_ref,
    an_ref, ac_ref, un_ref, uc_ref, dn_ref, dc_ref, l1_ref, l2_ref, ln_new_ref, norms_ref,
    all_ref, grad_ref,
):
    width = ln_ref.shape[1]
    tiles = width // SPAN
    at = 2 * tiles
    total = None
    for b in range(every_ref.shape[0] // groups):
        part = every_ref[b * groups].astype(f32)
        for k in range(b * groups + 1, (b + 1) * groups):
            part = part + every_ref[k].astype(f32)
        if fast:
            k, t = divmod(b, tiles)
            grad_ref[2 + k : 3 + k, t * SPAN : (t + 1) * SPAN] = (
                part[at : at + 1, :] + part[at + 1 : at + 2, :]
            )
        total = part if total is None else total + part
    all_ref[...] = total
    for k in range(2):
        for t in range(tiles):
            grad_ref[k : k + 1, t * SPAN : (t + 1) * SPAN] = all_ref[
                k * tiles + t : k * tiles + t + 1, :
            ]
    if not fast:
        grad_ref[2:4, :] = two_ref[0:2, :]
    line = all_ref[at + 2 : at + 3, :] + all_ref[at + 3 : at + 4, :] + all_ref[at + 4 : at + 5, :]
    roots = jnp.sqrt(line)
    norms_ref[0:1, :] = roots[:, 0:6]
    norms_ref[1:2, :] = roots[:, 6:12]
    lane = lax.broadcasted_iota(jnp.int32, line.shape, 1)

    def rate(k):
        weight = jnp.sum(jnp.where(lane == k, roots, 0.0), 1, keepdims=True)
        square = jnp.sum(jnp.where(lane == 6 + k, line, 0.0), 1, keepdims=True)
        return matrix_rate * (weight / jnp.sqrt(square + epsilon))

    for m in range(4):
        new = am_ref[m] - rate(m) * as_ref[m]
        an_ref[m] = new
        ac_ref[m] = new.astype(b16)
    new = um_ref[...] - rate(4) * us_ref[...]
    un_ref[...] = new
    uc_ref[...] = new.astype(b16)
    new = dm_ref[...] - rate(5) * ds_ref[...]
    dn_ref[...] = new
    dc_ref[...] = new.astype(b16)
    first, second, way = moments(grad_ref[...], lf_ref[...], ls_ref[...])
    l1_ref[...], l2_ref[...] = first, second
    ln_new_ref[...] = ln_ref[...] - vector_rate * way


def fast_mesh(nb, ng, width):
    return nb == 8 and ng == 4 and width // ng == SPAN


def shift(values, by, ng):
    return lax.ppermute(values, "group", [(j, (j + by) % ng) for j in range(ng)])


def cross(values, bit, nb):
    return lax.ppermute(values, "blk", [(j, j ^ bit) for j in range(nb)])


def put(buffer, piece, at):
    return lax.dynamic_update_slice(buffer, piece[None], (at,) + (0,) * piece.ndim)


def take(buffer, at):
    return lax.dynamic_index_in_dim(buffer, at, 0, keepdims=False)


def gather_group(piece, z, ng):
    out = put(jnp.zeros((ng,) + piece.shape, piece.dtype), piece, z)
    for by in range(1, ng):
        out = put(out, shift(piece, by, ng), (z - by) % ng)
    return out.reshape((-1,) + piece.shape[1:])


def gather_plane(piece, nb):
    return [piece] + [cross(piece, 2 * move, nb) for move in range(1, nb // 2)]


def gather_cut(piece, cuts, z, ng):
    near, far = shift(piece, 1, ng), shift(piece, ng - 1, ng)
    came = [
        (piece, z), (near, (z - 1) % ng), (far, (z + 1) % ng), (shift(near, 1, ng), (z - 2) % ng)
    ]
    outs = []
    for start, stop in cuts:
        out = jnp.zeros((ng, stop - start, piece.shape[1]), piece.dtype)
        for part, at in came:
            out = put(out, part[start:stop], at)
        outs.append(out.reshape(-1, piece.shape[1]))
    return outs


def other_core(pieces, nb):
    return [cross(piece, 1, nb) for piece in pieces]


def body(
    tokens, cotangent, lengths, ln_params, attn_master, attn_first, attn_second,
    up_master, up_first, up_second, down_master, down_first, down_second, ln_first, ln_second,
    *, nb, ng,
):
    seqs, tok, width = tokens.shape
    spans = tok // SPAN
    tiles = width // SPAN
    amount = nb * spans
    rows, cols = attn_master.shape[1:]
    ff_rows = down_master.shape[0]
    sub = nb // ng
    lanes = ff_rows // CHUNKS
    inner = nb * lanes
    places = nb // 2
    size = sub * rows + cols
    attn_rows = ng * 4 * rows
    half = -(-(seqs * spans * tiles + 8) // 16) * 16
    b, z = lax.axis_index("blk").astype(jnp.int32), lax.axis_index("group").astype(jnp.int32)
    core = b % 2
    fast = fast_mesh(nb, ng, width)
    scal = jnp.concatenate([jnp.stack([b, z]), lengths.astype(jnp.int32)])
    shape = jax.ShapeDtypeStruct

    def like(dtype, *tail):
        return shape((seqs,) + tail, dtype)

    def gather_any(piece, over=("blk", "group")):
        every = lax.all_gather(piece, over)
        every = every.reshape((places, 2, -1) + piece.shape[1:])
        every = jnp.swapaxes(every, 0, 1)
        own, other = take(every, core), take(every, 1 - core)
        return [own[p] for p in range(places)], [other[p] for p in range(places)]

    def reduce_any(keep, send, blocks):
        both = jnp.stack([jnp.where(core == 0, keep, send), jnp.where(core == 0, send, keep)])
        both = jnp.swapaxes(both, 0, 1).reshape((nb,) + keep.shape[1:])
        mine = lax.psum_scatter(both, "blk", scatter_dimension=0)
        if not blocks:
            return mine.astype(f32)
        mine = mine.reshape((ng, -1) + mine.shape[1:])
        return lax.psum_scatter(mine, "group", scatter_dimension=0).astype(f32)

    def flat(call, name, outs, scratch, work, *args, scalar=False):
        return pl.pallas_call(
            call,
            in_specs=[scalars()] * scalar + [whole()] * (len(args) - scalar),
            out_specs=[whole()] * len(outs),
            out_shape=outs,
            scratch_shapes=scratch,
            compiler_params=pltpu.CompilerParams(vmem_limit_bytes=16 * MIB),
            cost_estimate=work,
            name=name,
        )(*args)

    pack_dims = (rows, cols, sub, lanes)

    attn_piece = attn_master[:3].astype(b16).reshape(3 * rows, cols)
    if fast:
        attn_z = gather_group(attn_piece, z, ng)
    normed, rider = pl.pallas_call(
        prep_kernel,
        grid=(seqs,),
        in_specs=[scalars(), per_step(tok, width), fixed(4, width)],
        out_specs=[per_step(tok, width), fixed(2 * half, SPAN)],
        out_shape=[like(b16, tok, width), shape((2 * half, SPAN), b16)],
        scratch_shapes=[pltpu.VMEM((half, SPAN), f32)],
        compiler_params=params(16),
        cost_estimate=cost(4e7, 2 * seqs * tok * width * 2),
        name="prep",
    )(scal, tokens, ln_params)

    def gate(pieces, *deps):
        return flat(
            functools.partial(gate_kernel, len(pieces)), "gate",
            [shape(piece.shape, b16) for piece in pieces], [], cost(1e6, 1e6), *pieces, *deps,
        )

    def everywhere(piece):
        return lax.all_gather(piece, ("blk", "group"))

    if fast:
        message = jnp.concatenate([attn_z, rider], 0)
        attn_own = gather_plane(message, nb)
        attn_bufs = attn_own + other_core(attn_own, nb)
        pack_out = shape((rows + CHUNKS * size, lanes), b16)
        piece = pl.pallas_call(
            functools.partial(pack_kernel, pack_dims),
            grid=(1,),
            in_specs=[
                pl.BlockSpec((1, rows, cols), lambda i: (3, 0, 0)), fixed(*up_master.shape),
                fixed(*down_master.shape), whole(),
            ],
            out_specs=fixed(*pack_out.shape),
            out_shape=pack_out,
            cost_estimate=cost(1e6, 1e6),
            name="pack",
        )(attn_master, up_master, down_master, attn_piece)
        mlp_z, late_z = gather_cut(piece, [(0, rows + size), (rows + size, rows + 2 * size)], z, ng)
        mlp_own = gather_plane(mlp_z, nb)
        dep = mlp_z
    else:
        out_piece = attn_master[3].astype(b16)
        up_low = up_master.astype(b16).reshape(rows, sub, CHUNKS, lanes)
        down_low = down_master.astype(b16).T.reshape(cols, CHUNKS, lanes)
        attn_own, attn_other = gather_any(attn_piece)
        ride_own, ride_other = gather_any(rider, "blk")
        attn_bufs = attn_own + attn_other + ride_own + ride_other
        mlp_bufs = []
        for j in range(CHUNKS):
            piece = [jnp.swapaxes(up_low[:, :, j], 0, 1).reshape(sub * rows, lanes), down_low[:, j]]
            mlp_bufs.append([everywhere(jnp.concatenate(piece, 0))])
        mlp_bufs[0].append(everywhere(out_piece))
        dep = ln_params

    dims = (ng, rows, cols, width)
    act_bytes = seqs * tok * width
    q, k, v, ks, vs, nsum, lse, mixed, w_attn, token = pl.pallas_call(
        functools.partial(forward_kernel, dims, fast, places),
        grid=(seqs,),
        in_specs=[scalars(), per_step(tok, width)] + [whole()] * (len(attn_bufs) + 1),
        out_specs=[
            per_step(tok, width), per_step(tok, width), per_step(tok, width),
            per_step(amount, width), per_step(amount, width), per_step(amount, width),
            per_step(spans, tiles, 2 * SPAN),
            pl.BlockSpec((width, tok), lambda i: (0, i)),
            whole(), fixed(8, SPAN),
        ],
        out_shape=[
            like(b16, tok, width), like(b16, tok, width), like(b16, tok, width),
            like(b16, amount, width), like(b16, amount, width), like(b16, amount, width),
            like(f32, spans, tiles, 2 * SPAN),
            shape((width, seqs * tok), b16),
            shape((width, 3 * width), b16), shape((8, SPAN), f32),
        ],
        scratch_shapes=[
            pltpu.VMEM((2, places, half, SPAN), f32), pltpu.VMEM((amount, width), f32)
        ],
        compiler_params=params(16),
        cost_estimate=cost(8e9, act_bytes * 14),
        name="forward",
    )(scal, normed, *attn_bufs, dep)

    if fast:
        mlp_own[1:] = gate(mlp_own[1:], token)
        late_own = gather_plane(gate([late_z], token)[0], nb)
        mlp_bufs = [mlp_own + other_core(mlp_own, nb)]
        dep = late_own[0]
    mlp_dims = (ng, rows, cols, sub, lanes)
    mlp_out = shape((places, ng * size, lanes), b16)
    every_row = seqs * tok
    tile = every_row // ROW_STEPS
    flat_tokens, flat_cot = tokens.reshape(-1, width), cotangent.reshape(-1, width)
    by_rows = pl.BlockSpec((tile, width), lambda i: (i, 0))
    rows_out = shape((every_row, width), b16)
    keeps, sends = [], []
    y = gm = x2 = mid = wo = None
    for j in range(CHUNKS):
        first, last = j == 0, j == CHUNKS - 1
        if fast and not first:
            late_own[1:] = gate(late_own[1:], token)
            mlp_bufs.append(late_own + other_core(late_own, nb))
        if first:
            args = [scal, mixed, flat_tokens, ln_params, flat_cot]
            in_specs = [
                scalars(), pl.BlockSpec((width, tile), lambda i: (0, i)), by_rows, fixed(4, width),
                by_rows,
            ]
        else:
            args, in_specs = [scal, mid, flat_cot], [scalars(), by_rows, by_rows]
        args += [*mlp_bufs[j], dep]
        in_specs += [whole()] * (len(mlp_bufs[j]) + 1)
        outs = [(by_rows, rows_out), (by_rows, rows_out), (whole(), mlp_out), (whole(), mlp_out)]
        if first:
            outs = [
                (by_rows, rows_out), (by_rows, rows_out), (whole(), shape((width, width), b16)),
                (fixed(8, SPAN), shape((8, SPAN), f32)),
            ] + outs
        if last:
            args += [x2, y, gm]
            in_specs += [by_rows] * 3
        *more, y, gm, keep, send = pl.pallas_call(
            functools.partial(mlp_kernel, mlp_dims, fast, places, first, last),
            grid=(ROW_STEPS,),
            in_specs=in_specs,
            out_specs=[spec for spec, _ in outs],
            out_shape=[out for _, out in outs],
            scratch_shapes=[
                pltpu.VMEM((width, inner), b16), pltpu.VMEM((width, inner), b16),
                pltpu.VMEM((width, inner), f32), pltpu.VMEM((width, inner), f32),
            ],
            compiler_params=params(24),
            cost_estimate=cost(9e9, act_bytes * 20),
            name="mlp",
        )(*args)
        if first:
            x2, mid, wo, token = more
        keeps.append(keep)
        sends.append(send)
    block_out = y.reshape(tokens.shape)
    if fast:
        gets = [cross(send, 1, nb) for send in sends]

    by_tok = pl.BlockSpec((tok, width), lambda i: (i, 0))
    gx2, grad_mixed, dwo, ln_two = pl.pallas_call(
        middle_kernel,
        grid=(seqs,),
        in_specs=[
            by_tok, by_tok, by_tok, pl.BlockSpec((width, tok), lambda i: (0, i)), whole(),
            fixed(4, width),
        ],
        out_specs=[by_tok, by_tok, fixed(width, width), fixed(8, width)],
        out_shape=[rows_out, rows_out, shape((width, width), f32), shape((8, width), f32)],
        compiler_params=params(16),
        cost_estimate=cost(3e9, act_bytes * 14),
        name="middle",
    )(gm, flat_cot, x2, mixed, wo, ln_params)
    gx2, grad_mixed = gx2.reshape(tokens.shape), grad_mixed.reshape(tokens.shape)

    block = shape((ng * size, lanes), f32)
    block_low = shape((ng * size, lanes), b16)
    two, two_low = shape((2,) + block.shape, f32), shape((2,) + block.shape, b16)
    if fast:
        stay_a, out_a, stay_b, out_b = flat(
            halves_kernel, "halves", [two, two_low, two, two_low], [], cost(2e6, 16e6),
            scal, *keeps, *gets, scalar=True,
        )
        get_a, get_b = cross(out_a, 2, nb), cross(out_b, 4, nb)
        dep = stay_a
    else:
        dep = ln_two

    dqkv, key_part, value_part, h_part = pl.pallas_call(
        functools.partial(backward_kernel, places),
        grid=(seqs,),
        in_specs=[
            scalars(), per_step(tok, width),
            per_step(tok, width), per_step(tok, width), per_step(tok, width),
            per_step(spans, tiles, 2 * SPAN), per_step(amount, width), per_step(amount, width),
            whole(), anywhere(),
        ],
        out_specs=[
            per_step(tok, 3 * width), per_step(amount, width), per_step(amount, width), whole()
        ],
        out_shape=[
            like(b16, tok, 3 * width), like(b16, amount, width), like(b16, amount, width),
            shape((2, places, half, SPAN), f32),
        ],
        scratch_shapes=[pltpu.VMEM((width, tok), b16)],
        compiler_params=params(16),
        cost_estimate=cost(14e9, act_bytes * 24),
        name="backward",
    )(scal, grad_mixed, q, k, v, lse, ks, vs, w_attn, dep)

    if fast:
        own_a, out_a, own_b, out_b = flat(
            turn_kernel, "turn", [block, block_low] * 2, [], cost(1e6, 10e6),
            stay_a, get_a, stay_b, get_b,
        )
        mlp_parts = [own_a, cross(out_a, 4, nb), own_b, cross(out_b, 2, nb)]
        dep = own_a
    tail = half if fast else 0
    outs = [shape((places, attn_rows + tail, cols), b16)] * 2
    if not fast:
        outs += [shape((places, half, SPAN), b16)] * 2
    (dw,) = flat(
        grads_kernel, "grads", [shape((width, 3 * width), f32)],
        [pltpu.VMEM((width, seqs * tok), b16)], cost(1e6, 1e5),
        normed.reshape(-1, width), dqkv.reshape(-1, 3 * width), nsum.reshape(-1, width),
        key_part.reshape(-1, width), value_part.reshape(-1, width),
    )
    parts = flat(
        functools.partial(cut_kernel, dims, fast), "cut", outs, [], cost(1e6, 1e5),
        scal, dw, dwo, h_part, ln_two, dep, scalar=True,
    )

    def collect(terms, sizes, count, tail):
        outs = [shape((sum(sizes), SPAN), f32)] + [shape((sum(sizes), SPAN), b16)] * 3
        if tail:
            outs.append(shape((tail, SPAN), f32))
        return flat(
            functools.partial(collect_kernel, sizes, count), "collect", outs, [], cost(1e6, 4e6),
            scal, *terms, scalar=True,
        )

    if fast:
        attn_low = shape((attn_rows + tail, cols), b16)
        attn_parts = flat(
            functools.partial(spread_kernel, 1), "spread",
            [shape(attn_low.shape, f32)] + [attn_low] * 3, [], cost(1e6, 4e6),
            scal, parts[0], cross(parts[1], 1, nb), scalar=True,
        )
        dep = attn_parts[0]
        attn_parts = [dep] + [cross(attn_parts[m], 2 * m, nb) for m in range(1, 4)]
    else:
        dep = parts[2]

    grad_in = pl.pallas_call(
        project_kernel,
        grid=(seqs,),
        in_specs=[per_step(tok, 3 * width), whole(), anywhere()],
        out_specs=per_step(tok, width),
        out_shape=like(b16, tok, width),
        compiler_params=params(16),
        cost_estimate=cost(3e9, act_bytes * 8),
        name="project",
    )(dqkv, w_attn, dep)

    if fast:
        mlp_sums = collect(mlp_parts + [grad_in], (size,) * CHUNKS, 2, 0)
        mlp_sums = [mlp_sums[0]] + [shift(mlp_sums[by], by, ng) for by in range(1, ng)]
        *attn_sums, own = collect(attn_parts + [grad_in], (4 * rows,), 4, half)
        attn_sums = [attn_sums[0]] + [shift(attn_sums[by], by, ng) for by in range(1, ng)]
    else:
        own = reduce_any(parts[2], parts[3], False)
        attn_sums = [reduce_any(parts[0], parts[1], True)]
        mlp_sums = [
            jnp.concatenate([reduce_any(keep, send, True) for keep, send in zip(keeps, sends)], 0)
        ]
        ln_two = lax.psum(ln_two, ("blk", "group"))

    input_grad, ln_one = pl.pallas_call(
        input_kernel,
        grid=(seqs,),
        in_specs=[
            scalars(), per_step(tok, width), per_step(tok, width), per_step(tok, width),
            whole(), fixed(4, width),
        ],
        out_specs=[per_step(tok, width), fixed(8, width)],
        out_shape=[like(f32, tok, width), shape((8, width), f32)],
        compiler_params=params(16),
        cost_estimate=cost(1e8, act_bytes * 10),
        name="input",
    )(scal, grad_in, gx2, tokens, own, ln_params)

    attn_shape = shape(attn_master.shape, f32)
    up_shape, down_shape = shape(up_master.shape, f32), shape(down_master.shape, f32)
    up_moment1, up_moment2, up_step, down_moment1, down_moment2, down_step, line = flat(
        functools.partial(mlp_step_kernel, (rows, cols, sub, lanes), len(mlp_sums)),
        "mlp_step",
        [up_shape] * 3 + [down_shape] * 3 + [shape((1, SPAN), f32)],
        [],
        cost(1e6, 2e6),
        *mlp_sums, up_master, up_first, up_second, down_master, down_first, down_second,
    )
    lines = -(-(2 * tiles + 5) // 16) * 16
    attn_moment1, attn_moment2, attn_step, message = flat(
        functools.partial(attn_step_kernel, len(attn_sums), fast),
        "attn_step",
        [attn_shape] * 3 + [shape((nb * ng, lines, SPAN), b16)],
        [pltpu.VMEM((lines, SPAN), f32)],
        cost(1e6, 2e6),
        *attn_sums, attn_master, attn_first, attn_second, line, ln_one, own,
    )
    every = lax.all_to_all(message, ("blk", "group"), 0, 0, tiled=True)

    def low(like_this):
        return shape(like_this.shape, b16)

    ln_shape = shape(ln_params.shape, f32)
    (attn_new, attn_copy, up_new, up_copy, down_new, down_copy,
     ln_moment1, ln_moment2, ln_new, norms) = flat(
        functools.partial(final_kernel, ng, fast),
        "final",
        [attn_shape, low(attn_master), up_shape, low(up_master), down_shape, low(down_master)]
        + [ln_shape] * 3 + [shape((2, 6), f32)],
        [pltpu.VMEM((lines, SPAN), f32), pltpu.VMEM((4, width), f32)],
        cost(1e6, 2e6),
        every, ln_two, attn_master, attn_step, up_master, up_step, down_master, down_step,
        ln_params, ln_first, ln_second,
    )
    return (
        block_out, input_grad,
        attn_moment1, attn_moment2, attn_new, attn_copy,
        up_moment1, up_moment2, up_new, up_copy,
        down_moment1, down_moment2, down_new, down_copy,
        ln_moment1, ln_moment2, ln_new, norms,
    )


def solution(mesh):
    seq_spec = P("group", "blk", None)
    attn_spec = P(None, "blk", "group")
    flat_spec = P("blk", "group")
    return jax.shard_map(
        functools.partial(body, nb=mesh.shape["blk"], ng=mesh.shape["group"]),
        mesh=mesh,
        in_specs=(seq_spec, seq_spec, P("group"), P())
        + (attn_spec,) * 3
        + (flat_spec,) * 6
        + (P(), P()),
        out_specs=(seq_spec, seq_spec)
        + (attn_spec,) * 4
        + (flat_spec,) * 8
        + (P(),) * 4,
        check_vma=False,
    )
```

```python
import functools

import jax
import jax.numpy as jnp
from jax import lax
from jax.experimental import pallas as pl
from jax.experimental.pallas import tpu as pltpu
from jax.sharding import PartitionSpec as P

HEADS = 8
SPAN = 128
STEP = 5
CHUNKS = 2
ROW_STEPS = 5
BATCH = 4

masked_value = -1e30
decay_rate = 0.5
matrix_rate = 0.3
vector_rate = 0.5
weight_decay = 0.01
epsilon = 1e-06
gelu_a = 0.7978845608028654
gelu_b = 0.044715

f32 = jnp.float32
b16 = jnp.bfloat16
MIB = 1 << 20
NN = (((1,), (0,)), ((), ()))
NT = (((1,), (1,)), ((), ()))
TN = (((0,), (0,)), ((), ()))


def mm(a, b, dims=NN):
    return lax.dot_general(a, b, dims, preferred_element_type=f32)


def whole():
    return pl.BlockSpec(memory_space=pltpu.VMEM)


def scalars():
    return pl.BlockSpec(memory_space=pltpu.SMEM)


def per_step(*tail):
    zeros = (0,) * len(tail)
    return pl.BlockSpec((1,) + tail, lambda i: (i,) + zeros)


def fixed(*shape):
    zeros = (0,) * len(shape)
    return pl.BlockSpec(shape, lambda i: zeros)


def anywhere():
    return pl.BlockSpec(memory_space=pl.ANY)


def params(mib, steps=1):
    return pltpu.CompilerParams(
        dimension_semantics=("arbitrary",) * steps, vmem_limit_bytes=mib * MIB
    )


def cost(flops, nbytes, trans=0):
    return pl.CostEstimate(flops=int(flops * 0.03), bytes_accessed=int(nbytes * 0.03), transcendentals=int(trans))


def norm_parts(values):
    center = values - jnp.mean(values, -1, keepdims=True)
    spread = jnp.mean(center * center, -1, keepdims=True)
    inverse = lax.rsqrt(spread + 1e-05)
    return center * inverse, inverse


def norm_back(gradient, normal, inverse, gain):
    scaled = gradient * gain
    inner = jnp.mean(scaled, -1, keepdims=True)
    cross = jnp.mean(scaled * normal, -1, keepdims=True)
    return inverse * (scaled - inner - normal * cross)


def each_core(core, do):
    @pl.when(core == 0)
    def _():
        do(0, True)
        do(1, False)

    @pl.when(core != 0)
    def _():
        do(0, False)
        do(1, True)


def block(start, size):
    if isinstance(start, int):
        return slice(start, start + size)
    return pl.ds(pl.multiple_of(start, size), size)


def copy_attn(w_ref, own_refs, other_refs, spot, core, dims):
    groups, rows, cols, width = dims

    def do(c, mine):
        for move, buf_ref in enumerate(own_refs if mine else other_refs):
            place = move if spot is None else spot ^ move
            here = block((place * 2 + c) * rows, rows)
            for g in range(groups):
                for m in range(3):
                    at = (g * 3 + m) * rows
                    w_ref[here, m * width + g * cols : m * width + (g + 1) * cols] = buf_ref[
                        at : at + rows, :
                    ]

    each_core(core, do)


def prep_kernel(scal_ref, x_ref, ln_ref, normed_ref, rider_ref, sum_ref):
    i = pl.program_id(0)
    tok, width = x_ref.shape[1:]
    spans = tok // SPAN
    tiles = width // SPAN
    half = sum_ref.shape[0]
    normal, _ = norm_parts(x_ref[0].astype(f32))
    normed = (normal * ln_ref[0:1, :] + ln_ref[1:2, :]).astype(b16)
    normed_ref[0] = normed
    left = scal_ref[2 + i] - scal_ref[0] * tok
    row = lax.broadcasted_iota(jnp.int32, (16, tok), 0)
    col = lax.broadcasted_iota(jnp.int32, (16, tok), 1)
    chosen = jnp.where((col // SPAN == row) & (col < left), 1.0, 0.0)
    amount = jnp.maximum(jnp.sum(chosen, 1, keepdims=True), 1.0)
    total = mm(chosen.astype(b16), normed) / amount

    @pl.when(i == 0)
    def _():
        sum_ref[...] = jnp.zeros_like(sum_ref)

    for s in range(spans):
        for t in range(tiles):
            sum_ref[pl.ds((i * spans + s) * tiles + t, 1), :] = total[
                s : s + 1, t * SPAN : (t + 1) * SPAN
            ]

    @pl.when(i == pl.num_programs(0) - 1)
    def _():
        every = sum_ref[...]
        high = every.astype(b16)
        rider_ref[:half] = high
        rider_ref[half:] = (every - high.astype(f32)).astype(b16)


def pack_kernel(dims, in_ref, up_ref, down_ref, dep_ref, out_ref):
    rows, cols, sub, lanes = dims
    out_ref[:rows, :] = in_ref[0].astype(b16)
    at = rows
    for j in range(CHUNKS):
        for h in range(sub):
            c0 = (h * CHUNKS + j) * lanes
            out_ref[at : at + rows, :] = up_ref[:, c0 : c0 + lanes].astype(b16)
            at += rows
        out_ref[at : at + cols, :] = down_ref[j * lanes : (j + 1) * lanes, :].T.astype(b16)
        at += cols


def heads_apart(values):
    first = lax.broadcasted_iota(jnp.int32, values.shape, 1) < SPAN // 2
    zero = jnp.zeros_like(values)
    return jnp.concatenate([jnp.where(first, values, zero), jnp.where(first, zero, values)], 0)


def score_masks(scal_ref, i, span, spans, amount):
    length = scal_ref[2 + i]
    mine = scal_ref[0] * spans + span
    key = lax.broadcasted_iota(jnp.int32, (SPAN, 2 * SPAN), 0)
    query = lax.broadcasted_iota(jnp.int32, (SPAN, 2 * SPAN), 1) % SPAN
    local = (key <= query) & (key < length - mine * SPAN)
    index = lax.broadcasted_iota(jnp.int32, (amount, 2 * SPAN), 0)
    summary = (index < mine) & (index * SPAN < length)
    return local, summary


def own_heads(both):
    half = SPAN // 2
    return jnp.concatenate([both[:half, :SPAN], both[half:, SPAN:]], 0)


def gate_kernel(count, *refs):
    for in_ref, out_ref in zip(refs[:count], refs[-count:]):
        out_ref[...] = in_ref[...]


def forward_kernel(dims, fast, places, scal_ref, normed_ref, *refs):
    own_refs, refs = refs[:places], refs[places:]
    other_refs, refs = refs[:places], refs[places:]
    if fast:
        rown_refs, rother_refs = own_refs, other_refs
    else:
        rown_refs, refs = refs[:places], refs[places:]
        rother_refs, refs = refs[:places], refs[places:]
    (dep_ref, q_ref, k_ref, v_ref, ks_ref, vs_ref, nsum_ref, lse_ref, mixed_ref,
     w_ref, token_ref, sums_ref, line_ref) = refs
    i = pl.program_id(0)
    groups, rows, cols, width = dims
    tok = normed_ref.shape[1]
    spans = tok // SPAN
    tiles = width // SPAN
    amount = ks_ref.shape[1]
    factor = (width // HEADS) ** (-0.5)
    half = sums_ref.shape[2]
    base = groups * 3 * rows if fast else 0

    @pl.when(i == 0)
    def _():
        core = scal_ref[0] % 2
        spot = scal_ref[0] // 2 if fast else None
        copy_attn(w_ref, own_refs, other_refs, spot, core, dims)

        def do(c, mine):
            for move, buf_ref in enumerate(rown_refs if mine else rother_refs):
                place = spot ^ move if fast else move
                sums_ref[c, place] = buf_ref[base : base + half, :].astype(f32) + buf_ref[
                    base + half : base + 2 * half, :
                ].astype(f32)

        each_core(core, do)
        token_ref[...] = jnp.zeros_like(token_ref)

    for p in range(places):
        for c in range(2):
            for s in range(spans):
                for t in range(tiles):
                    r = (p * 2 + c) * spans + s
                    line_ref[r : r + 1, t * SPAN : (t + 1) * SPAN] = sums_ref[
                        c, p, pl.ds((i * spans + s) * tiles + t, 1), :
                    ]
    lines = line_ref[...]
    high = lines.astype(b16)
    low = (lines - high.astype(f32)).astype(b16)
    nsum_ref[0] = high
    normed = normed_ref[0]
    q_ref[0] = mm(normed, w_ref[:, :width]).astype(b16)
    k_ref[0] = mm(normed, w_ref[:, width : 2 * width]).astype(b16)
    v_ref[0] = mm(normed, w_ref[:, 2 * width : 3 * width]).astype(b16)
    sums = mm(high, w_ref[:, width : 3 * width]) + mm(low, w_ref[:, width : 3 * width])
    ks_ref[0] = sums[:, :width].astype(b16)
    vs_ref[0] = sums[:, width:].astype(b16)
    units = [(span, pair) for span in range(spans) for pair in range(tiles)]
    masks = [score_masks(scal_ref, i, span, spans, amount) for span in range(spans)]

    def places(span, pair):
        return slice(span * SPAN, (span + 1) * SPAN), slice(pair * SPAN, (pair + 1) * SPAN)

    scores = []
    for unit in units:
        part, lanes = places(*unit)
        query = heads_apart(q_ref[0, part, lanes] * b16(factor))
        keys = jnp.concatenate([k_ref[0, part, lanes], ks_ref[0, :, lanes]], 0)
        scores.append(mm(keys, query, NT))
    probs = []
    for (span, pair), score in zip(units, scores):
        local, summary = masks[span]
        here = jnp.where(local, score[:SPAN], masked_value)
        there = jnp.where(summary, score[SPAN:], masked_value)
        top = jnp.maximum(jnp.max(here, 0, keepdims=True), jnp.max(there, 0, keepdims=True))
        here, there = jnp.exp(here - top), jnp.exp(there - top)
        total = jnp.sum(here, 0, keepdims=True) + jnp.sum(there, 0, keepdims=True)
        lse_ref[0, span, pair : pair + 1, :] = top + jnp.log(total)
        probs.append((jnp.concatenate([here.astype(b16), there.astype(b16)], 0), 1.0 / total))
    for unit, (prob, inverse) in zip(units, probs):
        part, lanes = places(*unit)
        values = jnp.concatenate([v_ref[0, part, lanes], vs_ref[0, :, lanes]], 0)
        mixed_ref[lanes, part] = own_heads(mm(values, prob, TN) * inverse).astype(b16)


def mlp_kernel(dims, near, places, first, last, scal_ref, *refs):
    if first:
        mixed_ref, x_ref, ln_ref, *refs = refs
    else:
        mid_ref, *refs = refs
    g_ref, *refs = refs
    if near:
        own_refs, refs = refs[:places], refs[places:]
        other_refs, refs = refs[:places], refs[places:]
    else:
        full_ref, *refs = refs
        if first:
            out_ref, *refs = refs
    dep_ref, *refs = refs
    if last:
        x2_ref, y_in_ref, gm_in_ref, *refs = refs
    if first:
        x2_ref, mid_ref, wo_ref, token_ref, *refs = refs
    y_ref, gm_ref, keep_ref, send_ref, wu_ref, wd_ref, du_ref, dd_ref = refs
    groups, rows, cols, sub, lanes = dims
    size = sub * rows + cols
    extra = rows if first and near else 0
    i = pl.program_id(0)
    core = scal_ref[0] % 2

    def pieces(place, c, skip=0):
        b = place * 2 + c
        here = block(b * rows, rows)
        there = block(b * lanes, lanes)
        for g in range(groups):
            at = g * (size + skip)
            if skip:
                yield slice(at, at + rows), (here, slice(g * cols, (g + 1) * cols)), 2
                at += skip
            for h in range(sub):
                yield (
                    slice(at + h * rows, at + (h + 1) * rows),
                    (here, slice((g * sub + h) * lanes, (g * sub + h + 1) * lanes)),
                    0,
                )
            at += sub * rows
            yield slice(at, at + cols), (slice(g * cols, (g + 1) * cols), there), 1

    @pl.when(i == 0)
    def _():
        def fill(buf, there, here, kind):
            to_ref = wu_ref if kind == 0 else wd_ref if kind == 1 else wo_ref
            to_ref[here] = buf[there, :]

        def do(c, mine):
            for move, buf_ref in enumerate(own_refs if mine else other_refs):
                for there, here, kind in pieces((scal_ref[0] // 2) ^ move, c, extra):
                    fill(buf_ref, there, here, kind)

        if near:
            each_core(core, do)
        else:
            for b in range(2 * places):
                for k, (there, here, kind) in enumerate(pieces(b // 2, b % 2)):
                    g = k // (sub + 1)
                    there = slice(there.start - g * size, there.stop - g * size)
                    fill(full_ref.at[b * groups + g], there, here, kind)
                if first:
                    for g in range(groups):
                        wo_ref[b * rows : (b + 1) * rows, g * cols : (g + 1) * cols] = out_ref[
                            b * groups + g
                        ]
        du_ref[...] = jnp.zeros_like(du_ref)
        dd_ref[...] = jnp.zeros_like(dd_ref)
        if first:
            token_ref[...] = jnp.zeros_like(token_ref)

    if first:
        x2 = x_ref[...].astype(f32) + mm(mixed_ref[...], wo_ref[...], TN)
        x2_ref[...] = x2.astype(b16)
        normal, _ = norm_parts(x2)
        mid = (normal * ln_ref[2:3, :] + ln_ref[3:4, :]).astype(b16)
        mid_ref[...] = mid
    else:
        mid = mid_ref[...]
    g = g_ref[...]
    up = mm(mid, wu_ref[...])
    grad_act = mm(g, wd_ref[...])
    square = up * up
    half = 0.5 + 0.5 * jnp.tanh(up * (gelu_a + gelu_a * gelu_b * square))
    act = (up * half).astype(b16)
    slope = half + (up * half * (1.0 - half)) * (2.0 * gelu_a + 6.0 * gelu_a * gelu_b * square)
    grad_up = (slope * grad_act).astype(b16)
    y = mm(act, wd_ref[...], NT)
    gm = mm(grad_up, wu_ref[...], NT)
    if last:
        y_ref[...] = (x2_ref[...].astype(f32) + y_in_ref[...].astype(f32) + y).astype(b16)
        gm_ref[...] = (gm_in_ref[...].astype(f32) + gm).astype(b16)
    else:
        y_ref[...] = y.astype(b16)
        gm_ref[...] = gm.astype(b16)
    dd_ref[...] += mm(g, act, TN)
    du_ref[...] += mm(mid, grad_up, TN)

    @pl.when(i == pl.num_programs(0) - 1)
    def _():
        def do(c, mine):
            to_ref = keep_ref if mine else send_ref
            for place in range(places):
                for there, here, kind in pieces(place, c):
                    to_ref[place, there, :] = (dd_ref if kind else du_ref)[here].astype(b16)

        each_core(core, do)


def middle_kernel(
    second, gm_ref, g_ref, x2_ref, mixed_ref, w_ref, ln_ref, *refs
):
    gx2_ref, do_ref, dwo_ref, lng_ref = refs[-4:]
    gm = gm_ref[...].astype(f32)
    normal, inverse = norm_parts(x2_ref[...].astype(f32))
    lng_ref[...] = refs[3][...] if second else jnp.zeros_like(lng_ref)
    lng_ref[0:1, :] += jnp.sum(gm * normal, 0, keepdims=True)
    lng_ref[1:2, :] += jnp.sum(gm, 0, keepdims=True)
    gx2 = g_ref[...].astype(f32) + norm_back(gm, normal, inverse, ln_ref[2:3, :])
    branch = gx2.astype(b16)
    gx2_ref[...] = branch
    grad = mm(mixed_ref[...], branch)
    dwo_ref[...] = grad + refs[2][...] if second else grad
    do_ref[...] = mm(branch, w_ref[...], NT).astype(b16)


def backward_kernel(
    places, scal_ref, do_ref, q_ref, k_ref, v_ref, lse_ref, ks_ref, vs_ref, w_ref, dep_ref,
    dqkv_ref, key_ref, value_ref, h_ref, dqt_ref,
):
    i = pl.program_id(0)
    tok, width = do_ref.shape[1:]
    spans = tok // SPAN
    tiles = width // SPAN
    amount = ks_ref.shape[1]
    factor = (width // HEADS) ** (-0.5)

    @pl.when(i == 0)
    def _():
        h_ref[...] = jnp.zeros_like(h_ref)

    key_parts, value_parts = [], []
    for span in range(spans):
        part = slice(span * SPAN, (span + 1) * SPAN)
        local, summary = score_masks(scal_ref, i, span, spans, amount)
        pairs = [slice(pair * SPAN, (pair + 1) * SPAN) for pair in range(tiles)]
        for two in range(0, tiles, BATCH):
            batch = pairs[two : two + BATCH]
            queries = [heads_apart(q_ref[0, part, lanes] * b16(factor)) for lanes in batch]
            grads = [heads_apart(do_ref[0, part, lanes]) for lanes in batch]
            keys = [
                jnp.concatenate([k_ref[0, part, lanes], ks_ref[0, :, lanes]], 0) for lanes in batch
            ]
            scores = [mm(key, query, NT) for key, query in zip(keys, queries)]
            changes = [
                mm(jnp.concatenate([v_ref[0, part, lanes], vs_ref[0, :, lanes]], 0), grad, NT)
                for lanes, grad in zip(batch, grads)
            ]
            lows, backs = [], []
            for k, (score, change) in enumerate(zip(scores, changes)):
                total = lse_ref[0, span, two + k : two + k + 1, :]
                here = jnp.exp(jnp.where(local, score[:SPAN], masked_value) - total)
                there = jnp.exp(jnp.where(summary, score[SPAN:], masked_value) - total)
                here_grad, there_grad = here * change[:SPAN], there * change[SPAN:]
                dot = jnp.sum(here_grad, 0, keepdims=True) + jnp.sum(there_grad, 0, keepdims=True)
                lows.append(jnp.concatenate([here.astype(b16), there.astype(b16)], 0))
                backs.append(
                    jnp.concatenate(
                        [
                            (here_grad - here * dot).astype(b16),
                            (there_grad - there * dot).astype(b16),
                        ],
                        0,
                    )
                )
            for k, lanes in enumerate(batch):
                grad_value = mm(lows[k], grads[k])
                grad_key = mm(backs[k], queries[k])
                dqt_ref[lanes, part] = (own_heads(mm(keys[k], backs[k], TN)) * factor).astype(b16)
                c0 = width + (two + k) * SPAN
                dqkv_ref[0, part, c0 : c0 + SPAN] = grad_key[:SPAN].astype(b16)
                dqkv_ref[0, part, c0 + width : c0 + width + SPAN] = grad_value[:SPAN].astype(b16)
                key_parts.append(grad_key[SPAN:])
                value_parts.append(grad_value[SPAN:])
    dqkv_ref[0, :, :width] = dqt_ref[...].T

    def joined(parts):
        return jnp.concatenate(
            [sum(parts[s * tiles + p] for s in range(spans)) for p in range(tiles)], 1
        ).astype(b16)

    key_part, value_part = joined(key_parts), joined(value_parts)
    key_ref[0], value_ref[0] = key_part, value_part
    extra = mm(key_part, w_ref[:, width : 2 * width], NT) + mm(
        value_part, w_ref[:, 2 * width : 3 * width], NT
    )
    for p in range(places):
        for c in range(2):
            for s in range(spans):
                for t in range(tiles):
                    r = (p * 2 + c) * spans + s
                    h_ref[c, p, pl.ds((i * spans + s) * tiles + t, 1), :] = extra[
                        r : r + 1, t * SPAN : (t + 1) * SPAN
                    ]


def grads_kernel(normed_ref, dqkv_ref, nsum_ref, key_ref, value_ref, dw_ref, nt_ref):
    width = normed_ref.shape[1]
    nt_ref[...] = normed_ref[...].T
    dw_ref[:, :width] = mm(nt_ref[...], dqkv_ref[:, :width])
    dw_ref[:, width : 2 * width] = mm(nt_ref[...], dqkv_ref[:, width : 2 * width]) + mm(
        nsum_ref[...], key_ref[...], TN
    )
    dw_ref[:, 2 * width :] = mm(nt_ref[...], dqkv_ref[:, 2 * width :]) + mm(
        nsum_ref[...], value_ref[...], TN
    )


def cut_kernel(dims, fast, scal_ref, dw_ref, dwo_ref, h_ref, two_ref, dep_ref, *refs):
    if fast:
        keep_ref, send_ref = refs
        hkeep_ref, hsend_ref = keep_ref, send_ref
    else:
        keep_ref, send_ref, hkeep_ref, hsend_ref = refs
    groups, rows, cols, width = dims
    places, half = h_ref.shape[1:3]
    tiles = width // SPAN
    base = groups * 4 * rows if fast else 0
    used = half - 8

    def do(c, mine):
        out_ref, hout_ref = (keep_ref, hkeep_ref) if mine else (send_ref, hsend_ref)
        for p in range(places):
            r0 = (p * 2 + c) * rows
            for g in range(groups):
                for m in range(4):
                    at = (g * 4 + m) * rows
                    from_ref = dwo_ref if m == 3 else dw_ref
                    c0 = g * cols if m == 3 else m * width + g * cols
                    out_ref[p, at : at + rows, :] = from_ref[
                        r0 : r0 + rows, c0 : c0 + cols
                    ].astype(b16)
            ride = h_ref[c, p]
            if fast:
                k, t = divmod(p * 2 + c, tiles)
                piece = two_ref[k : k + 1, t * SPAN : (t + 1) * SPAN]
                high = piece.astype(b16).astype(f32)
                row = lax.broadcasted_iota(jnp.int32, ride.shape, 0)
                ride = jnp.where(row == used, high, ride)
                ride = jnp.where(row == used + 1, piece - high, ride)
            hout_ref[p, base : base + half, :] = ride.astype(b16)

    each_core(scal_ref[0] % 2, do)


def project_kernel(dqkv_ref, w_ref, dep_ref, out_ref):
    out_ref[0] = mm(dqkv_ref[0], w_ref[:, : dqkv_ref.shape[2]], NT).astype(out_ref.dtype)


def input_kernel(scal_ref, grad_ref, gx2_ref, x_ref, h_ref, ln_ref, out_ref, lng_ref):
    i = pl.program_id(0)
    tok, width = x_ref.shape[1:]
    spans = tok // SPAN
    tiles = width // SPAN

    @pl.when(i == 0)
    def _():
        lng_ref[...] = jnp.zeros_like(lng_ref)

    left = scal_ref[2 + i] - scal_ref[0] * tok
    place = lax.broadcasted_iota(jnp.int32, (tok, 1), 0)
    extra = []
    for s in range(spans):
        part = slice(s * SPAN, (s + 1) * SPAN)
        amount = jnp.clip(left - s * SPAN, 0, SPAN)
        share = jnp.where(place[part] < left, 1.0, 0.0) / jnp.maximum(amount, 1).astype(f32)
        line = jnp.concatenate(
            [h_ref[pl.ds((i * spans + s) * tiles + t, 1), :] for t in range(tiles)], 1
        )
        extra.append(share * line)
    grad = grad_ref[0].astype(f32) + jnp.concatenate(extra, 0)
    normal, inverse = norm_parts(x_ref[0].astype(f32))
    lng_ref[0:1, :] += jnp.sum(grad * normal, 0, keepdims=True)
    lng_ref[1:2, :] += jnp.sum(grad, 0, keepdims=True)
    out_ref[0] = gx2_ref[0].astype(f32) + norm_back(grad, normal, inverse, ln_ref[0:1, :])


def spread_kernel(count, scal_ref, *refs):
    keeps, gets, outs = refs[:count], refs[count : 2 * count], refs[-4:]
    spot = scal_ref[0] // 2
    at = 0
    for keep_ref, get_ref in zip(keeps, gets):
        size = keep_ref.shape[1]
        for move in range(4):
            there = spot ^ move
            total = keep_ref[there].astype(f32) + get_ref[there].astype(f32)
            outs[move][at : at + size, :] = total.astype(outs[move].dtype)
        at += size


def halves_kernel(scal_ref, *refs):
    spot = scal_ref[0] // 2
    for j, far in enumerate((1, 2)):
        keep_ref, get_ref = refs[j], refs[2 + j]
        stay_ref, out_ref = refs[-4 + 2 * j], refs[-3 + 2 * j]
        near = 3 - far
        for k, (ref, move) in enumerate(
            ((stay_ref, 0), (stay_ref, near), (out_ref, far), (out_ref, far ^ near))
        ):
            there = spot ^ move
            total = keep_ref[there].astype(f32) + get_ref[there].astype(f32)
            ref[k % 2] = total.astype(ref.dtype)


def turn_kernel(*refs):
    for j in range(2):
        stay_ref, get_ref = refs[2 * j], refs[2 * j + 1]
        own_ref, out_ref = refs[4 + 2 * j], refs[5 + 2 * j]
        own_ref[...] = stay_ref[0] + get_ref[0].astype(f32)
        out_ref[...] = (stay_ref[1] + get_ref[1].astype(f32)).astype(b16)


def collect_kernel(sizes, count, scal_ref, *refs):
    z = scal_ref[1]
    groups = 4
    outs = refs[len(sizes) * count + 1 :]

    def total(terms, start, size):
        rows = pl.ds(start, size)
        value = terms[0][rows, :].astype(f32)
        for ref in terms[1:]:
            value = value + ref[rows, :].astype(f32)
        return value

    at = 0
    for k, size in enumerate(sizes):
        terms = refs[k * count : (k + 1) * count]
        for by in range(groups):
            start = pl.multiple_of(((z + by) % groups) * size, size)
            outs[by][at : at + size, :] = total(terms, start, size).astype(outs[by].dtype)
        at += size
    if len(outs) > groups:
        outs[groups][...] = total(terms, groups * size, outs[groups].shape[0])


def moments(gradient, first, second):
    corr = 1.0 - decay_rate**STEP
    new_first = decay_rate * first + (1.0 - decay_rate) * gradient
    new_second = decay_rate * second + (1.0 - decay_rate) * gradient * gradient
    return (new_first, new_second, new_first / corr / (jnp.sqrt(new_second / corr) + epsilon))


def lane_line(values):
    lane = lax.broadcasted_iota(jnp.int32, (1, SPAN), 1)
    line = jnp.zeros((1, SPAN), f32)
    for at, value in values.items():
        line = line + jnp.where(lane == at, value, 0.0)
    return line


def square_sum(values):
    return jnp.sum(jnp.sum(values * values, 0, keepdims=True), 1, keepdims=True)


def add_up(refs, rows):
    total = refs[0][rows, :].astype(f32)
    for ref in refs[1:]:
        total = total + ref[rows, :].astype(f32)
    return total


def mlp_step_kernel(dims, count, *refs):
    grads = refs[:count]
    (um_ref, uf_ref, us_ref, dm_ref, df_ref, ds_ref,
     u1_ref, u2_ref, ustep_ref, d1_ref, d2_ref, dstep_ref, line_ref) = refs[count:]
    rows, cols, sub, lanes = dims
    size = sub * rows + cols
    sums = [jnp.zeros((1, 1), f32) for _ in range(4)]
    for j in range(CHUNKS):
        for h in range(sub):
            start = j * size + h * rows
            at = (slice(None), slice((h * CHUNKS + j) * lanes, (h * CHUNKS + j + 1) * lanes))
            first, second, way = moments(
                add_up(grads, slice(start, start + rows)), uf_ref[at], us_ref[at]
            )
            step = way + weight_decay * um_ref[at]
            u1_ref[at], u2_ref[at], ustep_ref[at] = first, second, step
            sums[0] += square_sum(um_ref[at])
            sums[2] += square_sum(step)
        start = j * size + sub * rows
        at = (slice(j * lanes, (j + 1) * lanes), slice(None))
        first, second, way = moments(
            add_up(grads, slice(start, start + cols)).T, df_ref[at], ds_ref[at]
        )
        step = way + weight_decay * dm_ref[at]
        d1_ref[at], d2_ref[at], dstep_ref[at] = first, second, step
        sums[1] += square_sum(dm_ref[at])
        sums[3] += square_sum(step)
    line_ref[...] = lane_line({4: sums[0], 5: sums[1], 10: sums[2], 11: sums[3]})


def attn_step_kernel(count, fast, *refs):
    grads = refs[:count]
    (m_ref, f_ref, s_ref, line_ref, one_ref, h_ref,
     m1_ref, m2_ref, step_ref, out_ref, all_ref) = refs[count:]
    rows = m_ref.shape[1]
    tiles = one_ref.shape[1] // SPAN
    values = {}
    for m in range(4):
        first, second, way = moments(
            add_up(grads, slice(m * rows, (m + 1) * rows)), f_ref[m], s_ref[m]
        )
        step = way + weight_decay * m_ref[m]
        m1_ref[m], m2_ref[m], step_ref[m] = first, second, step
        values[m] = square_sum(m_ref[m])
        values[6 + m] = square_sum(step)
    all_ref[...] = jnp.zeros_like(all_ref)
    for k in range(2):
        for t in range(tiles):
            all_ref[k * tiles + t : k * tiles + t + 1, :] = one_ref[
                k : k + 1, t * SPAN : (t + 1) * SPAN
            ]
    at = 2 * tiles
    if fast:
        used = h_ref.shape[0] - 8
        piece = h_ref[used : used + 1, :] + h_ref[used + 1 : used + 2, :]
        high = piece.astype(b16).astype(f32)
        all_ref[at : at + 1, :] = high
        all_ref[at + 1 : at + 2, :] = piece - high
    line = lane_line(values) + line_ref[...]
    for k in range(3):
        piece = line.astype(b16).astype(f32)
        all_ref[at + 2 + k : at + 3 + k, :] = piece
        line = line - piece
    message = all_ref[...].astype(b16)
    for k in range(out_ref.shape[0]):
        out_ref[k] = message


def final_kernel(
    groups, fast, every_ref, two_ref, am_ref, as_ref, um_ref, us_ref, dm_ref, ds_ref, ln_ref, lf_ref, ls_ref,
    an_ref, ac_ref, un_ref, uc_ref, dn_ref, dc_ref, l1_ref, l2_ref, ln_new_ref, norms_ref,
    all_ref, grad_ref,
):
    width = ln_ref.shape[1]
    tiles = width // SPAN
    at = 2 * tiles
    total = None
    for b in range(every_ref.shape[0] // groups):
        part = every_ref[b * groups].astype(f32)
        for k in range(b * groups + 1, (b + 1) * groups):
            part = part + every_ref[k].astype(f32)
        if fast:
            k, t = divmod(b, tiles)
            grad_ref[2 + k : 3 + k, t * SPAN : (t + 1) * SPAN] = (
                part[at : at + 1, :] + part[at + 1 : at + 2, :]
            )
        total = part if total is None else total + part
    all_ref[...] = total
    for k in range(2):
        for t in range(tiles):
            grad_ref[k : k + 1, t * SPAN : (t + 1) * SPAN] = all_ref[
                k * tiles + t : k * tiles + t + 1, :
            ]
    if not fast:
        grad_ref[2:4, :] = two_ref[0:2, :]
    line = all_ref[at + 2 : at + 3, :] + all_ref[at + 3 : at + 4, :] + all_ref[at + 4 : at + 5, :]
    roots = jnp.sqrt(line)
    norms_ref[0:1, :] = roots[:, 0:6]
    norms_ref[1:2, :] = roots[:, 6:12]
    lane = lax.broadcasted_iota(jnp.int32, line.shape, 1)

    def rate(k):
        weight = jnp.sum(jnp.where(lane == k, roots, 0.0), 1, keepdims=True)
        square = jnp.sum(jnp.where(lane == 6 + k, line, 0.0), 1, keepdims=True)
        return matrix_rate * (weight / jnp.sqrt(square + epsilon))

    for m in range(4):
        new = am_ref[m] - rate(m) * as_ref[m]
        an_ref[m] = new
        ac_ref[m] = new.astype(b16)
    new = um_ref[...] - rate(4) * us_ref[...]
    un_ref[...] = new
    uc_ref[...] = new.astype(b16)
    new = dm_ref[...] - rate(5) * ds_ref[...]
    dn_ref[...] = new
    dc_ref[...] = new.astype(b16)
    first, second, way = moments(grad_ref[...], lf_ref[...], ls_ref[...])
    l1_ref[...], l2_ref[...] = first, second
    ln_new_ref[...] = ln_ref[...] - vector_rate * way


def fast_mesh(nb, ng, width):
    return nb == 8 and ng == 4 and width // ng == SPAN


def shift(values, by, ng):
    return lax.ppermute(values, "group", [(j, (j + by) % ng) for j in range(ng)])


def cross(values, bit, nb):
    return lax.ppermute(values, "blk", [(j, j ^ bit) for j in range(nb)])


def put(buffer, piece, at):
    return lax.dynamic_update_slice(buffer, piece[None], (at,) + (0,) * piece.ndim)


def take(buffer, at):
    return lax.dynamic_index_in_dim(buffer, at, 0, keepdims=False)


def gather_group(piece, z, ng):
    out = put(jnp.zeros((ng,) + piece.shape, piece.dtype), piece, z)
    for by in range(1, ng):
        out = put(out, shift(piece, by, ng), (z - by) % ng)
    return out.reshape((-1,) + piece.shape[1:])


def gather_plane(piece, nb):
    return [piece] + [cross(piece, 2 * move, nb) for move in range(1, nb // 2)]


def gather_cut(piece, cuts, z, ng):
    near, far = shift(piece, 1, ng), shift(piece, ng - 1, ng)
    came = [
        (piece, z), (near, (z - 1) % ng), (far, (z + 1) % ng), (shift(near, 1, ng), (z - 2) % ng)
    ]
    outs = []
    for start, stop in cuts:
        out = jnp.zeros((ng, stop - start, piece.shape[1]), piece.dtype)
        for part, at in came:
            out = put(out, part[start:stop], at)
        outs.append(out.reshape(-1, piece.shape[1]))
    return outs


def other_core(pieces, nb):
    return [cross(piece, 1, nb) for piece in pieces]


def body(
    tokens, cotangent, lengths, ln_params, attn_master, attn_first, attn_second,
    up_master, up_first, up_second, down_master, down_first, down_second, ln_first, ln_second,
    *, nb, ng,
):
    seqs, tok, width = tokens.shape
    spans = tok // SPAN
    tiles = width // SPAN
    amount = nb * spans
    rows, cols = attn_master.shape[1:]
    ff_rows = down_master.shape[0]
    sub = nb // ng
    lanes = ff_rows // CHUNKS
    inner = nb * lanes
    places = nb // 2
    size = sub * rows + cols
    attn_rows = ng * 4 * rows
    half = -(-(seqs * spans * tiles + 8) // 16) * 16
    b, z = lax.axis_index("blk").astype(jnp.int32), lax.axis_index("group").astype(jnp.int32)
    core = b % 2
    fast = fast_mesh(nb, ng, width)
    scal = jnp.concatenate([jnp.stack([b, z]), lengths.astype(jnp.int32)])
    shape = jax.ShapeDtypeStruct

    def like(dtype, *tail):
        return shape((seqs,) + tail, dtype)

    def gather_any(piece, over=("blk", "group")):
        every = lax.all_gather(piece, over)
        every = every.reshape((places, 2, -1) + piece.shape[1:])
        every = jnp.swapaxes(every, 0, 1)
        own, other = take(every, core), take(every, 1 - core)
        return [own[p] for p in range(places)], [other[p] for p in range(places)]

    def reduce_any(keep, send, blocks):
        both = jnp.stack([jnp.where(core == 0, keep, send), jnp.where(core == 0, send, keep)])
        both = jnp.swapaxes(both, 0, 1).reshape((nb,) + keep.shape[1:])
        mine = lax.psum_scatter(both, "blk", scatter_dimension=0)
        if not blocks:
            return mine.astype(f32)
        mine = mine.reshape((ng, -1) + mine.shape[1:])
        return lax.psum_scatter(mine, "group", scatter_dimension=0).astype(f32)

    def flat(call, name, outs, scratch, work, *args, scalar=False):
        return pl.pallas_call(
            call,
            in_specs=[scalars()] * scalar + [whole()] * (len(args) - scalar),
            out_specs=[whole()] * len(outs),
            out_shape=outs,
            scratch_shapes=scratch,
            compiler_params=pltpu.CompilerParams(vmem_limit_bytes=16 * MIB),
            cost_estimate=work,
            name=name,
        )(*args)

    pack_dims = (rows, cols, sub, lanes)

    attn_piece = attn_master[:3].astype(b16).reshape(3 * rows, cols)
    if fast:
        attn_z = gather_group(attn_piece, z, ng)
    normed, rider = pl.pallas_call(
        prep_kernel,
        grid=(seqs,),
        in_specs=[scalars(), per_step(tok, width), fixed(4, width)],
        out_specs=[per_step(tok, width), fixed(2 * half, SPAN)],
        out_shape=[like(b16, tok, width), shape((2 * half, SPAN), b16)],
        scratch_shapes=[pltpu.VMEM((half, SPAN), f32)],
        compiler_params=params(16),
        cost_estimate=cost(4e7, 2 * seqs * tok * width * 2),
        name="prep",
    )(scal, tokens, ln_params)

    def gate(pieces, *deps):
        return flat(
            functools.partial(gate_kernel, len(pieces)), "gate",
            [shape(piece.shape, b16) for piece in pieces], [], cost(1e6, 1e6), *pieces, *deps,
        )

    def everywhere(piece):
        return lax.all_gather(piece, ("blk", "group"))

    if fast:
        message = jnp.concatenate([attn_z, rider], 0)
        attn_own = gather_plane(message, nb)
        attn_bufs = attn_own + other_core(attn_own, nb)
        pack_out = shape((rows + CHUNKS * size, lanes), b16)
        piece = pl.pallas_call(
            functools.partial(pack_kernel, pack_dims),
            grid=(1,),
            in_specs=[
                pl.BlockSpec((1, rows, cols), lambda i: (3, 0, 0)), fixed(*up_master.shape),
                fixed(*down_master.shape), whole(),
            ],
            out_specs=fixed(*pack_out.shape),
            out_shape=pack_out,
            cost_estimate=cost(1e6, 1e6),
            name="pack",
        )(attn_master, up_master, down_master, attn_piece)
        mlp_z, late_z = gather_cut(piece, [(0, rows + size), (rows + size, rows + 2 * size)], z, ng)
        mlp_own = gather_plane(mlp_z, nb)
        dep = mlp_z
    else:
        out_piece = attn_master[3].astype(b16)
        up_low = up_master.astype(b16).reshape(rows, sub, CHUNKS, lanes)
        down_low = down_master.astype(b16).T.reshape(cols, CHUNKS, lanes)
        attn_own, attn_other = gather_any(attn_piece)
        ride_own, ride_other = gather_any(rider, "blk")
        attn_bufs = attn_own + attn_other + ride_own + ride_other
        mlp_bufs = []
        for j in range(CHUNKS):
            piece = [jnp.swapaxes(up_low[:, :, j], 0, 1).reshape(sub * rows, lanes), down_low[:, j]]
            mlp_bufs.append([everywhere(jnp.concatenate(piece, 0))])
        mlp_bufs[0].append(everywhere(out_piece))
        dep = ln_params

    dims = (ng, rows, cols, width)
    act_bytes = seqs * tok * width
    q, k, v, ks, vs, nsum, lse, mixed, w_attn, token = pl.pallas_call(
        functools.partial(forward_kernel, dims, fast, places),
        grid=(seqs,),
        in_specs=[scalars(), per_step(tok, width)] + [whole()] * (len(attn_bufs) + 1),
        out_specs=[
            per_step(tok, width), per_step(tok, width), per_step(tok, width),
            per_step(amount, width), per_step(amount, width), per_step(amount, width),
            per_step(spans, tiles, 2 * SPAN),
            pl.BlockSpec((width, tok), lambda i: (0, i)),
            whole(), fixed(8, SPAN),
        ],
        out_shape=[
            like(b16, tok, width), like(b16, tok, width), like(b16, tok, width),
            like(b16, amount, width), like(b16, amount, width), like(b16, amount, width),
            like(f32, spans, tiles, 2 * SPAN),
            shape((width, seqs * tok), b16),
            shape((width, 3 * width), b16), shape((8, SPAN), f32),
        ],
        scratch_shapes=[
            pltpu.VMEM((2, places, half, SPAN), f32), pltpu.VMEM((amount, width), f32)
        ],
        compiler_params=params(16),
        cost_estimate=cost(8e9, act_bytes * 14),
        name="forward",
    )(scal, normed, *attn_bufs, dep)

    if fast:
        mlp_own[1:] = gate(mlp_own[1:], token)
        late_own = gather_plane(gate([late_z], token)[0], nb)
        mlp_bufs = [mlp_own + other_core(mlp_own, nb)]
        dep = late_own[0]
    mlp_dims = (ng, rows, cols, sub, lanes)
    mlp_out = shape((places, ng * size, lanes), b16)
    every_row = seqs * tok
    tile = every_row // ROW_STEPS
    flat_tokens, flat_cot = tokens.reshape(-1, width), cotangent.reshape(-1, width)
    by_rows = pl.BlockSpec((tile, width), lambda i: (i, 0))
    rows_out = shape((every_row, width), b16)
    keeps, sends = [], []
    y = gm = x2 = mid = wo = None
    for j in range(CHUNKS):
        first, last = j == 0, j == CHUNKS - 1
        if fast and not first:
            late_own[1:] = gate(late_own[1:], token)
            mlp_bufs.append(late_own + other_core(late_own, nb))
        if first:
            args = [scal, mixed, flat_tokens, ln_params, flat_cot]
            in_specs = [
                scalars(), pl.BlockSpec((width, tile), lambda i: (0, i)), by_rows, fixed(4, width),
                by_rows,
            ]
        else:
            args, in_specs = [scal, mid, flat_cot], [scalars(), by_rows, by_rows]
        args += [*mlp_bufs[j], dep]
        in_specs += [whole()] * (len(mlp_bufs[j]) + 1)
        outs = [(by_rows, rows_out), (by_rows, rows_out), (whole(), mlp_out), (whole(), mlp_out)]
        if first:
            outs = [
                (by_rows, rows_out), (by_rows, rows_out), (whole(), shape((width, width), b16)),
                (fixed(8, SPAN), shape((8, SPAN), f32)),
            ] + outs
        if last:
            args += [x2, y, gm]
            in_specs += [by_rows] * 3
        *more, y, gm, keep, send = pl.pallas_call(
            functools.partial(mlp_kernel, mlp_dims, fast, places, first, last),
            grid=(ROW_STEPS,),
            in_specs=in_specs,
            out_specs=[spec for spec, _ in outs],
            out_shape=[out for _, out in outs],
            scratch_shapes=[
                pltpu.VMEM((width, inner), b16), pltpu.VMEM((width, inner), b16),
                pltpu.VMEM((width, inner), f32), pltpu.VMEM((width, inner), f32),
            ],
            compiler_params=params(24),
            cost_estimate=cost(9e9, act_bytes * 20),
            name="mlp",
        )(*args)
        if first:
            x2, mid, wo, token = more
        keeps.append(keep)
        sends.append(send)
    block_out = y.reshape(tokens.shape)
    if fast:
        gets = [cross(send, 1, nb) for send in sends]

    def middle(k, *more):
        rows_k = pl.BlockSpec((every_row // 2, width), lambda i: (k, 0))
        return pl.pallas_call(
            functools.partial(middle_kernel, bool(more)),
            grid=(1,),
            in_specs=[
                rows_k, rows_k, rows_k, pl.BlockSpec((width, every_row // 2), lambda i: (0, k)),
                whole(), fixed(4, width),
            ]
            + [anywhere(), anywhere(), fixed(width, width), fixed(8, width), anywhere()][: len(more)],
            out_specs=[rows_k, rows_k, fixed(width, width), fixed(8, width)],
            out_shape=[rows_out, rows_out, shape((width, width), f32), shape((8, width), f32)],
            input_output_aliases={6: 0, 7: 1} if more else {},
            compiler_params=params(24),
            cost_estimate=cost(3e9, act_bytes * 14),
            name="middle",
        )(gm, flat_cot, x2, mixed, wo, ln_params, *more)

    halfway = middle(0)

    block = shape((ng * size, lanes), f32)
    block_low = shape((ng * size, lanes), b16)
    two, two_low = shape((2,) + block.shape, f32), shape((2,) + block.shape, b16)
    if fast:
        stay_a, out_a, stay_b, out_b = flat(
            halves_kernel, "halves", [two, two_low, two, two_low], [], cost(2e6, 16e6),
            scal, *keeps, *gets, halfway[3], scalar=True,
        )
        get_a, get_b = cross(out_a, 2, nb), cross(out_b, 4, nb)
        dep = stay_a
    else:
        dep = ln_params
    gx2, grad_mixed, dwo, ln_two = middle(1, *halfway, dep)
    gx2, grad_mixed = gx2.reshape(tokens.shape), grad_mixed.reshape(tokens.shape)

    dqkv, key_part, value_part, h_part = pl.pallas_call(
        functools.partial(backward_kernel, places),
        grid=(seqs,),
        in_specs=[
            scalars(), per_step(tok, width),
            per_step(tok, width), per_step(tok, width), per_step(tok, width),
            per_step(spans, tiles, 2 * SPAN), per_step(amount, width), per_step(amount, width),
            whole(), anywhere(),
        ],
        out_specs=[
            per_step(tok, 3 * width), per_step(amount, width), per_step(amount, width), whole()
        ],
        out_shape=[
            like(b16, tok, 3 * width), like(b16, amount, width), like(b16, amount, width),
            shape((2, places, half, SPAN), f32),
        ],
        scratch_shapes=[pltpu.VMEM((width, tok), b16)],
        compiler_params=params(16),
        cost_estimate=cost(14e9, act_bytes * 24),
        name="backward",
    )(scal, grad_mixed, q, k, v, lse, ks, vs, w_attn, dep)

    if fast:
        own_a, out_a, own_b, out_b = flat(
            turn_kernel, "turn", [block, block_low] * 2, [], cost(1e6, 10e6),
            stay_a, get_a, stay_b, get_b,
        )
        mlp_parts = [own_a, cross(out_a, 4, nb), own_b, cross(out_b, 2, nb)]
        dep = own_a
    tail = half if fast else 0
    outs = [shape((places, attn_rows + tail, cols), b16)] * 2
    if not fast:
        outs += [shape((places, half, SPAN), b16)] * 2
    (dw,) = flat(
        grads_kernel, "grads", [shape((width, 3 * width), f32)],
        [pltpu.VMEM((width, seqs * tok), b16)], cost(1e6, 1e5),
        normed.reshape(-1, width), dqkv.reshape(-1, 3 * width), nsum.reshape(-1, width),
        key_part.reshape(-1, width), value_part.reshape(-1, width),
    )
    parts = flat(
        functools.partial(cut_kernel, dims, fast), "cut", outs, [], cost(1e6, 1e5),
        scal, dw, dwo, h_part, ln_two, dep, scalar=True,
    )

    def collect(terms, sizes, count, tail):
        outs = [shape((sum(sizes), SPAN), f32)] + [shape((sum(sizes), SPAN), b16)] * 3
        if tail:
            outs.append(shape((tail, SPAN), f32))
        return flat(
            functools.partial(collect_kernel, sizes, count), "collect", outs, [], cost(1e6, 4e6),
            scal, *terms, scalar=True,
        )

    if fast:
        attn_low = shape((attn_rows + tail, cols), b16)
        attn_parts = flat(
            functools.partial(spread_kernel, 1), "spread",
            [shape(attn_low.shape, f32)] + [attn_low] * 3, [], cost(1e6, 4e6),
            scal, parts[0], cross(parts[1], 1, nb), scalar=True,
        )
        dep = attn_parts[0]
        attn_parts = [dep] + [cross(attn_parts[m], 2 * m, nb) for m in range(1, 4)]
    else:
        dep = parts[2]

    grad_in = pl.pallas_call(
        project_kernel,
        grid=(seqs,),
        in_specs=[per_step(tok, 3 * width), whole(), anywhere()],
        out_specs=per_step(tok, width),
        out_shape=like(b16, tok, width),
        compiler_params=params(16),
        cost_estimate=cost(3e9, act_bytes * 8),
        name="project",
    )(dqkv, w_attn, dep)

    if fast:
        mlp_sums = collect(mlp_parts + [grad_in], (size,) * CHUNKS, 2, 0)
        mlp_sums = [mlp_sums[0]] + [shift(mlp_sums[by], by, ng) for by in range(1, ng)]
        *attn_sums, own = collect(attn_parts + [grad_in], (4 * rows,), 4, half)
        attn_sums = [attn_sums[0]] + [shift(attn_sums[by], by, ng) for by in range(1, ng)]
    else:
        own = reduce_any(parts[2], parts[3], False)
        attn_sums = [reduce_any(parts[0], parts[1], True)]
        mlp_sums = [
            jnp.concatenate([reduce_any(keep, send, True) for keep, send in zip(keeps, sends)], 0)
        ]
        ln_two = lax.psum(ln_two, ("blk", "group"))

    input_grad, ln_one = pl.pallas_call(
        input_kernel,
        grid=(seqs,),
        in_specs=[
            scalars(), per_step(tok, width), per_step(tok, width), per_step(tok, width),
            whole(), fixed(4, width),
        ],
        out_specs=[per_step(tok, width), fixed(8, width)],
        out_shape=[like(f32, tok, width), shape((8, width), f32)],
        compiler_params=params(16),
        cost_estimate=cost(1e8, act_bytes * 10),
        name="input",
    )(scal, grad_in, gx2, tokens, own, ln_params)

    attn_shape = shape(attn_master.shape, f32)
    up_shape, down_shape = shape(up_master.shape, f32), shape(down_master.shape, f32)
    up_moment1, up_moment2, up_step, down_moment1, down_moment2, down_step, line = flat(
        functools.partial(mlp_step_kernel, (rows, cols, sub, lanes), len(mlp_sums)),
        "mlp_step",
        [up_shape] * 3 + [down_shape] * 3 + [shape((1, SPAN), f32)],
        [],
        cost(1e6, 2e6),
        *mlp_sums, up_master, up_first, up_second, down_master, down_first, down_second,
    )
    lines = -(-(2 * tiles + 5) // 16) * 16
    attn_moment1, attn_moment2, attn_step, message = flat(
        functools.partial(attn_step_kernel, len(attn_sums), fast),
        "attn_step",
        [attn_shape] * 3 + [shape((nb * ng, lines, SPAN), b16)],
        [pltpu.VMEM((lines, SPAN), f32)],
        cost(1e6, 2e6),
        *attn_sums, attn_master, attn_first, attn_second, line, ln_one, own,
    )
    every = lax.all_to_all(message, ("blk", "group"), 0, 0, tiled=True)

    def low(like_this):
        return shape(like_this.shape, b16)

    ln_shape = shape(ln_params.shape, f32)
    (attn_new, attn_copy, up_new, up_copy, down_new, down_copy,
     ln_moment1, ln_moment2, ln_new, norms) = flat(
        functools.partial(final_kernel, ng, fast),
        "final",
        [attn_shape, low(attn_master), up_shape, low(up_master), down_shape, low(down_master)]
        + [ln_shape] * 3 + [shape((2, 6), f32)],
        [pltpu.VMEM((lines, SPAN), f32), pltpu.VMEM((4, width), f32)],
        cost(1e6, 2e6),
        every, ln_two, attn_master, attn_step, up_master, up_step, down_master, down_step,
        ln_params, ln_first, ln_second,
    )
    return (
        block_out, input_grad,
        attn_moment1, attn_moment2, attn_new, attn_copy,
        up_moment1, up_moment2, up_new, up_copy,
        down_moment1, down_moment2, down_new, down_copy,
        ln_moment1, ln_moment2, ln_new, norms,
    )


def solution(mesh):
    seq_spec = P("group", "blk", None)
    attn_spec = P(None, "blk", "group")
    flat_spec = P("blk", "group")
    return jax.shard_map(
        functools.partial(body, nb=mesh.shape["blk"], ng=mesh.shape["group"]),
        mesh=mesh,
        in_specs=(seq_spec, seq_spec, P("group"), P())
        + (attn_spec,) * 3
        + (flat_spec,) * 6
        + (P(), P()),
        out_specs=(seq_spec, seq_spec)
        + (attn_spec,) * 4
        + (flat_spec,) * 8
        + (P(),) * 4,
        check_vma=False,
    )
```

```python
import functools

import jax
import jax.numpy as jnp
from jax import lax
from jax.experimental import pallas as pl
from jax.experimental.pallas import tpu as pltpu
from jax.sharding import PartitionSpec as P

HEADS = 8
SPAN = 128
STEP = 5
CHUNKS = 2
ROW_STEPS = 5
BATCH = 4

masked_value = -1e30
decay_rate = 0.5
matrix_rate = 0.3
vector_rate = 0.5
weight_decay = 0.01
epsilon = 1e-06
gelu_a = 0.7978845608028654
gelu_b = 0.044715

f32 = jnp.float32
b16 = jnp.bfloat16
MIB = 1 << 20
NN = (((1,), (0,)), ((), ()))
NT = (((1,), (1,)), ((), ()))
TN = (((0,), (0,)), ((), ()))


def mm(a, b, dims=NN):
    return lax.dot_general(a, b, dims, preferred_element_type=f32)


def whole():
    return pl.BlockSpec(memory_space=pltpu.VMEM)


def scalars():
    return pl.BlockSpec(memory_space=pltpu.SMEM)


def per_step(*tail):
    zeros = (0,) * len(tail)
    return pl.BlockSpec((1,) + tail, lambda i: (i,) + zeros)


def fixed(*shape):
    zeros = (0,) * len(shape)
    return pl.BlockSpec(shape, lambda i: zeros)


def anywhere():
    return pl.BlockSpec(memory_space=pl.ANY)


def params(mib, steps=1):
    return pltpu.CompilerParams(
        dimension_semantics=("arbitrary",) * steps, vmem_limit_bytes=mib * MIB
    )


def cost(flops, nbytes, trans=0):
    return pl.CostEstimate(flops=int(flops * 0.03), bytes_accessed=int(nbytes * 0.03), transcendentals=int(trans))


def norm_parts(values):
    center = values - jnp.mean(values, -1, keepdims=True)
    spread = jnp.mean(center * center, -1, keepdims=True)
    inverse = lax.rsqrt(spread + 1e-05)
    return center * inverse, inverse


def norm_back(gradient, normal, inverse, gain):
    scaled = gradient * gain
    inner = jnp.mean(scaled, -1, keepdims=True)
    cross = jnp.mean(scaled * normal, -1, keepdims=True)
    return inverse * (scaled - inner - normal * cross)


def each_core(core, do):
    @pl.when(core == 0)
    def _():
        do(0, True)
        do(1, False)

    @pl.when(core != 0)
    def _():
        do(0, False)
        do(1, True)


def block(start, size):
    if isinstance(start, int):
        return slice(start, start + size)
    return pl.ds(pl.multiple_of(start, size), size)


def over_seqs(step, moving, unrolled, *refs):
    count = next(ref.shape[0] for ref, moves in zip(refs, moving) if moves)

    def one(i):
        step(i, *(ref.at[pl.ds(i, 1)] if moves else ref for ref, moves in zip(refs, moving)))

    if unrolled:
        for i in range(count):
            one(i)
    else:
        pl.loop(0, count)(one)


def copy_attn(w_ref, own_refs, other_refs, spot, core, dims):
    groups, rows, cols, width = dims

    def do(c, mine):
        for move, buf_ref in enumerate(own_refs if mine else other_refs):
            place = move if spot is None else spot ^ move
            here = block((place * 2 + c) * rows, rows)
            for g in range(groups):
                for m in range(3):
                    at = (g * 3 + m) * rows
                    w_ref[here, m * width + g * cols : m * width + (g + 1) * cols] = buf_ref[
                        at : at + rows, :
                    ]

    each_core(core, do)


def prep_kernel(seqs, i, scal_ref, x_ref, ln_ref, normed_ref, rider_ref, sum_ref):
    tok, width = x_ref.shape[1:]
    spans = tok // SPAN
    tiles = width // SPAN
    half = sum_ref.shape[0]
    normal, _ = norm_parts(x_ref[0].astype(f32))
    normed = (normal * ln_ref[0:1, :] + ln_ref[1:2, :]).astype(b16)
    normed_ref[0] = normed
    left = scal_ref[2 + i] - scal_ref[0] * tok
    row = lax.broadcasted_iota(jnp.int32, (16, tok), 0)
    col = lax.broadcasted_iota(jnp.int32, (16, tok), 1)
    chosen = jnp.where((col // SPAN == row) & (col < left), 1.0, 0.0)
    amount = jnp.maximum(jnp.sum(chosen, 1, keepdims=True), 1.0)
    total = mm(chosen.astype(b16), normed) / amount

    if i == 0:
        sum_ref[...] = jnp.zeros_like(sum_ref)

    for s in range(spans):
        for t in range(tiles):
            sum_ref[(i * spans + s) * tiles + t : (i * spans + s) * tiles + t + 1, :] = total[
                s : s + 1, t * SPAN : (t + 1) * SPAN
            ]

    if i == seqs - 1:
        every = sum_ref[...]
        high = every.astype(b16)
        rider_ref[:half] = high
        rider_ref[half:] = (every - high.astype(f32)).astype(b16)


def pack_kernel(dims, in_ref, up_ref, down_ref, dep_ref, out_ref):
    rows, cols, sub, lanes = dims
    out_ref[:rows, :] = in_ref[0].astype(b16)
    at = rows
    for j in range(CHUNKS):
        for h in range(sub):
            c0 = (h * CHUNKS + j) * lanes
            out_ref[at : at + rows, :] = up_ref[:, c0 : c0 + lanes].astype(b16)
            at += rows
        out_ref[at : at + cols, :] = down_ref[j * lanes : (j + 1) * lanes, :].T.astype(b16)
        at += cols


def heads_apart(values):
    first = lax.broadcasted_iota(jnp.int32, values.shape, 1) < SPAN // 2
    zero = jnp.zeros_like(values)
    return jnp.concatenate([jnp.where(first, values, zero), jnp.where(first, zero, values)], 0)


def score_masks(scal_ref, i, span, spans, amount):
    length = scal_ref[2 + i]
    mine = scal_ref[0] * spans + span
    key = lax.broadcasted_iota(jnp.int32, (SPAN, 2 * SPAN), 0)
    query = lax.broadcasted_iota(jnp.int32, (SPAN, 2 * SPAN), 1) % SPAN
    local = (key <= query) & (key < length - mine * SPAN)
    index = lax.broadcasted_iota(jnp.int32, (amount, 2 * SPAN), 0)
    summary = (index < mine) & (index * SPAN < length)
    return local, summary


def own_heads(both):
    half = SPAN // 2
    return jnp.concatenate([both[:half, :SPAN], both[half:, SPAN:]], 0)


def gate_kernel(count, *refs):
    for in_ref, out_ref in zip(refs[:count], refs[-count:]):
        out_ref[...] = in_ref[...]


def forward_kernel(dims, fast, places, scal_ref, normed_ref, *refs):
    own_refs, refs = refs[:places], refs[places:]
    other_refs, refs = refs[:places], refs[places:]
    if fast:
        rown_refs, rother_refs = own_refs, other_refs
    else:
        rown_refs, refs = refs[:places], refs[places:]
        rother_refs, refs = refs[:places], refs[places:]
    (dep_ref, q_ref, k_ref, v_ref, ks_ref, vs_ref, nsum_ref, lse_ref, mixed_ref,
     w_ref, token_ref, sums_ref, line_ref) = refs
    i = pl.program_id(0)
    groups, rows, cols, width = dims
    tok = normed_ref.shape[1]
    spans = tok // SPAN
    tiles = width // SPAN
    amount = ks_ref.shape[1]
    factor = (width // HEADS) ** (-0.5)
    half = sums_ref.shape[2]
    base = groups * 3 * rows if fast else 0

    @pl.when(i == 0)
    def _():
        core = scal_ref[0] % 2
        spot = scal_ref[0] // 2 if fast else None
        copy_attn(w_ref, own_refs, other_refs, spot, core, dims)

        def do(c, mine):
            for move, buf_ref in enumerate(rown_refs if mine else rother_refs):
                place = spot ^ move if fast else move
                sums_ref[c, place] = buf_ref[base : base + half, :].astype(f32) + buf_ref[
                    base + half : base + 2 * half, :
                ].astype(f32)

        each_core(core, do)
        token_ref[...] = jnp.zeros_like(token_ref)

    for p in range(places):
        for c in range(2):
            for s in range(spans):
                for t in range(tiles):
                    r = (p * 2 + c) * spans + s
                    line_ref[r : r + 1, t * SPAN : (t + 1) * SPAN] = sums_ref[
                        c, p, pl.ds((i * spans + s) * tiles + t, 1), :
                    ]
    lines = line_ref[...]
    high = lines.astype(b16)
    low = (lines - high.astype(f32)).astype(b16)
    nsum_ref[0] = high
    normed = normed_ref[0]
    q_ref[0] = mm(normed, w_ref[:, :width]).astype(b16)
    k_ref[0] = mm(normed, w_ref[:, width : 2 * width]).astype(b16)
    v_ref[0] = mm(normed, w_ref[:, 2 * width : 3 * width]).astype(b16)
    sums = mm(high, w_ref[:, width : 3 * width]) + mm(low, w_ref[:, width : 3 * width])
    ks_ref[0] = sums[:, :width].astype(b16)
    vs_ref[0] = sums[:, width:].astype(b16)
    units = [(span, pair) for span in range(spans) for pair in range(tiles)]
    masks = [score_masks(scal_ref, i, span, spans, amount) for span in range(spans)]

    def places(span, pair):
        return slice(span * SPAN, (span + 1) * SPAN), slice(pair * SPAN, (pair + 1) * SPAN)

    scores = []
    for unit in units:
        part, lanes = places(*unit)
        query = heads_apart(q_ref[0, part, lanes] * b16(factor))
        keys = jnp.concatenate([k_ref[0, part, lanes], ks_ref[0, :, lanes]], 0)
        scores.append(mm(keys, query, NT))
    probs = []
    for (span, pair), score in zip(units, scores):
        local, summary = masks[span]
        here = jnp.where(local, score[:SPAN], masked_value)
        there = jnp.where(summary, score[SPAN:], masked_value)
        top = jnp.maximum(jnp.max(here, 0, keepdims=True), jnp.max(there, 0, keepdims=True))
        here, there = jnp.exp(here - top), jnp.exp(there - top)
        total = jnp.sum(here, 0, keepdims=True) + jnp.sum(there, 0, keepdims=True)
        lse_ref[0, span, pair : pair + 1, :] = top + jnp.log(total)
        probs.append((jnp.concatenate([here.astype(b16), there.astype(b16)], 0), 1.0 / total))
    for unit, (prob, inverse) in zip(units, probs):
        part, lanes = places(*unit)
        values = jnp.concatenate([v_ref[0, part, lanes], vs_ref[0, :, lanes]], 0)
        mixed_ref[lanes, part] = own_heads(mm(values, prob, TN) * inverse).astype(b16)


def mlp_kernel(dims, near, places, first, last, scal_ref, *refs):
    if first:
        mixed_ref, x_ref, ln_ref, *refs = refs
    else:
        mid_ref, *refs = refs
    g_ref, *refs = refs
    if near:
        own_refs, refs = refs[:places], refs[places:]
        other_refs, refs = refs[:places], refs[places:]
    else:
        full_ref, *refs = refs
        if first:
            out_ref, *refs = refs
    dep_ref, *refs = refs
    if last:
        x2_ref, y_in_ref, gm_in_ref, *refs = refs
    if first:
        x2_ref, mid_ref, wo_ref, token_ref, *refs = refs
    y_ref, gm_ref, keep_ref, send_ref, wu_ref, wd_ref, du_ref, dd_ref = refs
    groups, rows, cols, sub, lanes = dims
    size = sub * rows + cols
    extra = rows if first and near else 0
    i = pl.program_id(0)
    core = scal_ref[0] % 2

    def pieces(place, c, skip=0):
        b = place * 2 + c
        here = block(b * rows, rows)
        there = block(b * lanes, lanes)
        for g in range(groups):
            at = g * (size + skip)
            if skip:
                yield slice(at, at + rows), (here, slice(g * cols, (g + 1) * cols)), 2
                at += skip
            for h in range(sub):
                yield (
                    slice(at + h * rows, at + (h + 1) * rows),
                    (here, slice((g * sub + h) * lanes, (g * sub + h + 1) * lanes)),
                    0,
                )
            at += sub * rows
            yield slice(at, at + cols), (slice(g * cols, (g + 1) * cols), there), 1

    @pl.when(i == 0)
    def _():
        def fill(buf, there, here, kind):
            to_ref = wu_ref if kind == 0 else wd_ref if kind == 1 else wo_ref
            to_ref[here] = buf[there, :]

        def do(c, mine):
            for move, buf_ref in enumerate(own_refs if mine else other_refs):
                for there, here, kind in pieces((scal_ref[0] // 2) ^ move, c, extra):
                    fill(buf_ref, there, here, kind)

        if near:
            each_core(core, do)
        else:
            for b in range(2 * places):
                for k, (there, here, kind) in enumerate(pieces(b // 2, b % 2)):
                    g = k // (sub + 1)
                    there = slice(there.start - g * size, there.stop - g * size)
                    fill(full_ref.at[b * groups + g], there, here, kind)
                if first:
                    for g in range(groups):
                        wo_ref[b * rows : (b + 1) * rows, g * cols : (g + 1) * cols] = out_ref[
                            b * groups + g
                        ]
        du_ref[...] = jnp.zeros_like(du_ref)
        dd_ref[...] = jnp.zeros_like(dd_ref)
        if first:
            token_ref[...] = jnp.zeros_like(token_ref)

    if first:
        x2 = x_ref[...].astype(f32) + mm(mixed_ref[...], wo_ref[...], TN)
        x2_ref[...] = x2.astype(b16)
        normal, _ = norm_parts(x2)
        mid = (normal * ln_ref[2:3, :] + ln_ref[3:4, :]).astype(b16)
        mid_ref[...] = mid
    else:
        mid = mid_ref[...]
    g = g_ref[...]
    up = mm(mid, wu_ref[...])
    grad_act = mm(g, wd_ref[...])
    square = up * up
    half = 0.5 + 0.5 * jnp.tanh(up * (gelu_a + gelu_a * gelu_b * square))
    act = (up * half).astype(b16)
    slope = half + (up * half * (1.0 - half)) * (2.0 * gelu_a + 6.0 * gelu_a * gelu_b * square)
    grad_up = (slope * grad_act).astype(b16)
    y = mm(act, wd_ref[...], NT)
    gm = mm(grad_up, wu_ref[...], NT)
    if last:
        y_ref[...] = (x2_ref[...].astype(f32) + y_in_ref[...].astype(f32) + y).astype(b16)
        gm_ref[...] = (gm_in_ref[...].astype(f32) + gm).astype(b16)
    else:
        y_ref[...] = y.astype(b16)
        gm_ref[...] = gm.astype(b16)
    dd_ref[...] += mm(g, act, TN)
    du_ref[...] += mm(mid, grad_up, TN)

    @pl.when(i == pl.num_programs(0) - 1)
    def _():
        def do(c, mine):
            to_ref = keep_ref if mine else send_ref
            for place in range(places):
                for there, here, kind in pieces(place, c):
                    to_ref[place, there, :] = (dd_ref if kind else du_ref)[here].astype(b16)

        each_core(core, do)


def middle_kernel(
    second, gm_ref, g_ref, x2_ref, mixed_ref, w_ref, ln_ref, *refs
):
    gx2_ref, do_ref, dwo_ref, lng_ref = refs[-4:]
    gm = gm_ref[...].astype(f32)
    normal, inverse = norm_parts(x2_ref[...].astype(f32))
    lng_ref[...] = refs[3][...] if second else jnp.zeros_like(lng_ref)
    lng_ref[0:1, :] += jnp.sum(gm * normal, 0, keepdims=True)
    lng_ref[1:2, :] += jnp.sum(gm, 0, keepdims=True)
    gx2 = g_ref[...].astype(f32) + norm_back(gm, normal, inverse, ln_ref[2:3, :])
    branch = gx2.astype(b16)
    gx2_ref[...] = branch
    grad = mm(mixed_ref[...], branch)
    dwo_ref[...] = grad + refs[2][...] if second else grad
    do_ref[...] = mm(branch, w_ref[...], NT).astype(b16)


def backward_kernel(
    places, scal_ref, do_ref, q_ref, k_ref, v_ref, lse_ref, ks_ref, vs_ref, w_ref, dep_ref,
    dqkv_ref, key_ref, value_ref, h_ref, dqt_ref,
):
    i = pl.program_id(0)
    tok, width = do_ref.shape[1:]
    spans = tok // SPAN
    tiles = width // SPAN
    amount = ks_ref.shape[1]
    factor = (width // HEADS) ** (-0.5)

    @pl.when(i == 0)
    def _():
        h_ref[...] = jnp.zeros_like(h_ref)

    key_parts, value_parts = [], []
    for span in range(spans):
        part = slice(span * SPAN, (span + 1) * SPAN)
        local, summary = score_masks(scal_ref, i, span, spans, amount)
        pairs = [slice(pair * SPAN, (pair + 1) * SPAN) for pair in range(tiles)]
        for two in range(0, tiles, BATCH):
            batch = pairs[two : two + BATCH]
            queries = [heads_apart(q_ref[0, part, lanes] * b16(factor)) for lanes in batch]
            grads = [heads_apart(do_ref[0, part, lanes]) for lanes in batch]
            keys = [
                jnp.concatenate([k_ref[0, part, lanes], ks_ref[0, :, lanes]], 0) for lanes in batch
            ]
            scores = [mm(key, query, NT) for key, query in zip(keys, queries)]
            changes = [
                mm(jnp.concatenate([v_ref[0, part, lanes], vs_ref[0, :, lanes]], 0), grad, NT)
                for lanes, grad in zip(batch, grads)
            ]
            lows, backs = [], []
            for k, (score, change) in enumerate(zip(scores, changes)):
                total = lse_ref[0, span, two + k : two + k + 1, :]
                here = jnp.exp(jnp.where(local, score[:SPAN], masked_value) - total)
                there = jnp.exp(jnp.where(summary, score[SPAN:], masked_value) - total)
                here_grad, there_grad = here * change[:SPAN], there * change[SPAN:]
                dot = jnp.sum(here_grad, 0, keepdims=True) + jnp.sum(there_grad, 0, keepdims=True)
                lows.append(jnp.concatenate([here.astype(b16), there.astype(b16)], 0))
                backs.append(
                    jnp.concatenate(
                        [
                            (here_grad - here * dot).astype(b16),
                            (there_grad - there * dot).astype(b16),
                        ],
                        0,
                    )
                )
            for k, lanes in enumerate(batch):
                grad_value = mm(lows[k], grads[k])
                grad_key = mm(backs[k], queries[k])
                dqt_ref[lanes, part] = (own_heads(mm(keys[k], backs[k], TN)) * factor).astype(b16)
                c0 = width + (two + k) * SPAN
                dqkv_ref[0, part, c0 : c0 + SPAN] = grad_key[:SPAN].astype(b16)
                dqkv_ref[0, part, c0 + width : c0 + width + SPAN] = grad_value[:SPAN].astype(b16)
                key_parts.append(grad_key[SPAN:])
                value_parts.append(grad_value[SPAN:])
    dqkv_ref[0, :, :width] = dqt_ref[...].T

    def joined(parts):
        return jnp.concatenate(
            [sum(parts[s * tiles + p] for s in range(spans)) for p in range(tiles)], 1
        ).astype(b16)

    key_part, value_part = joined(key_parts), joined(value_parts)
    key_ref[0], value_ref[0] = key_part, value_part
    extra = mm(key_part, w_ref[:, width : 2 * width], NT) + mm(
        value_part, w_ref[:, 2 * width : 3 * width], NT
    )
    for p in range(places):
        for c in range(2):
            for s in range(spans):
                for t in range(tiles):
                    r = (p * 2 + c) * spans + s
                    h_ref[c, p, pl.ds((i * spans + s) * tiles + t, 1), :] = extra[
                        r : r + 1, t * SPAN : (t + 1) * SPAN
                    ]


def grads_kernel(normed_ref, dqkv_ref, nsum_ref, key_ref, value_ref, dw_ref, nt_ref):
    width = normed_ref.shape[1]
    nt_ref[...] = normed_ref[...].T
    dw_ref[:, :width] = mm(nt_ref[...], dqkv_ref[:, :width])
    dw_ref[:, width : 2 * width] = mm(nt_ref[...], dqkv_ref[:, width : 2 * width]) + mm(
        nsum_ref[...], key_ref[...], TN
    )
    dw_ref[:, 2 * width :] = mm(nt_ref[...], dqkv_ref[:, 2 * width :]) + mm(
        nsum_ref[...], value_ref[...], TN
    )


def cut_kernel(dims, fast, scal_ref, dw_ref, dwo_ref, h_ref, two_ref, dep_ref, *refs):
    if fast:
        keep_ref, send_ref = refs
        hkeep_ref, hsend_ref = keep_ref, send_ref
    else:
        keep_ref, send_ref, hkeep_ref, hsend_ref = refs
    groups, rows, cols, width = dims
    places, half = h_ref.shape[1:3]
    tiles = width // SPAN
    base = groups * 4 * rows if fast else 0
    used = half - 8

    def do(c, mine):
        out_ref, hout_ref = (keep_ref, hkeep_ref) if mine else (send_ref, hsend_ref)
        for p in range(places):
            r0 = (p * 2 + c) * rows
            for g in range(groups):
                for m in range(4):
                    at = (g * 4 + m) * rows
                    from_ref = dwo_ref if m == 3 else dw_ref
                    c0 = g * cols if m == 3 else m * width + g * cols
                    out_ref[p, at : at + rows, :] = from_ref[
                        r0 : r0 + rows, c0 : c0 + cols
                    ].astype(b16)
            ride = h_ref[c, p]
            if fast:
                k, t = divmod(p * 2 + c, tiles)
                piece = two_ref[k : k + 1, t * SPAN : (t + 1) * SPAN]
                high = piece.astype(b16).astype(f32)
                row = lax.broadcasted_iota(jnp.int32, ride.shape, 0)
                ride = jnp.where(row == used, high, ride)
                ride = jnp.where(row == used + 1, piece - high, ride)
            hout_ref[p, base : base + half, :] = ride.astype(b16)

    each_core(scal_ref[0] % 2, do)


def project_kernel(dqkv_ref, w_ref, dep_ref, out_ref):
    out_ref[0] = mm(dqkv_ref[0], w_ref[:, : dqkv_ref.shape[2]], NT).astype(out_ref.dtype)


def input_kernel(scal_ref, grad_ref, gx2_ref, x_ref, h_ref, ln_ref, out_ref, lng_ref):
    i = pl.program_id(0)
    tok, width = x_ref.shape[1:]
    spans = tok // SPAN
    tiles = width // SPAN

    @pl.when(i == 0)
    def _():
        lng_ref[...] = jnp.zeros_like(lng_ref)

    left = scal_ref[2 + i] - scal_ref[0] * tok
    place = lax.broadcasted_iota(jnp.int32, (tok, 1), 0)
    extra = []
    for s in range(spans):
        part = slice(s * SPAN, (s + 1) * SPAN)
        amount = jnp.clip(left - s * SPAN, 0, SPAN)
        share = jnp.where(place[part] < left, 1.0, 0.0) / jnp.maximum(amount, 1).astype(f32)
        line = jnp.concatenate(
            [h_ref[pl.ds((i * spans + s) * tiles + t, 1), :] for t in range(tiles)], 1
        )
        extra.append(share * line)
    grad = grad_ref[0].astype(f32) + jnp.concatenate(extra, 0)
    normal, inverse = norm_parts(x_ref[0].astype(f32))
    lng_ref[0:1, :] += jnp.sum(grad * normal, 0, keepdims=True)
    lng_ref[1:2, :] += jnp.sum(grad, 0, keepdims=True)
    out_ref[0] = gx2_ref[0].astype(f32) + norm_back(grad, normal, inverse, ln_ref[0:1, :])


def spread_kernel(count, scal_ref, *refs):
    keeps, gets, outs = refs[:count], refs[count : 2 * count], refs[-4:]
    spot = scal_ref[0] // 2
    at = 0
    for keep_ref, get_ref in zip(keeps, gets):
        size = keep_ref.shape[1]
        for move in range(4):
            there = spot ^ move
            total = keep_ref[there].astype(f32) + get_ref[there].astype(f32)
            outs[move][at : at + size, :] = total.astype(outs[move].dtype)
        at += size


def halves_kernel(scal_ref, *refs):
    spot = scal_ref[0] // 2
    for j, far in enumerate((1, 2)):
        keep_ref, get_ref = refs[j], refs[2 + j]
        stay_ref, out_ref = refs[-4 + 2 * j], refs[-3 + 2 * j]
        near = 3 - far
        for k, (ref, move) in enumerate(
            ((stay_ref, 0), (stay_ref, near), (out_ref, far), (out_ref, far ^ near))
        ):
            there = spot ^ move
            total = keep_ref[there].astype(f32) + get_ref[there].astype(f32)
            ref[k % 2] = total.astype(ref.dtype)


def turn_kernel(*refs):
    for j in range(2):
        stay_ref, get_ref = refs[2 * j], refs[2 * j + 1]
        own_ref, out_ref = refs[4 + 2 * j], refs[5 + 2 * j]
        own_ref[...] = stay_ref[0] + get_ref[0].astype(f32)
        out_ref[...] = (stay_ref[1] + get_ref[1].astype(f32)).astype(b16)


def collect_kernel(sizes, count, scal_ref, *refs):
    z = scal_ref[1]
    groups = 4
    outs = refs[len(sizes) * count + 1 :]

    def total(terms, start, size):
        rows = pl.ds(start, size)
        value = terms[0][rows, :].astype(f32)
        for ref in terms[1:]:
            value = value + ref[rows, :].astype(f32)
        return value

    at = 0
    for k, size in enumerate(sizes):
        terms = refs[k * count : (k + 1) * count]
        for by in range(groups):
            start = pl.multiple_of(((z + by) % groups) * size, size)
            outs[by][at : at + size, :] = total(terms, start, size).astype(outs[by].dtype)
        at += size
    if len(outs) > groups:
        outs[groups][...] = total(terms, groups * size, outs[groups].shape[0])


def moments(gradient, first, second):
    corr = 1.0 - decay_rate**STEP
    new_first = decay_rate * first + (1.0 - decay_rate) * gradient
    new_second = decay_rate * second + (1.0 - decay_rate) * gradient * gradient
    return (new_first, new_second, new_first / corr / (jnp.sqrt(new_second / corr) + epsilon))


def lane_line(values):
    lane = lax.broadcasted_iota(jnp.int32, (1, SPAN), 1)
    line = jnp.zeros((1, SPAN), f32)
    for at, value in values.items():
        line = line + jnp.where(lane == at, value, 0.0)
    return line


def square_sum(values):
    return jnp.sum(jnp.sum(values * values, 0, keepdims=True), 1, keepdims=True)


def add_up(refs, rows):
    total = refs[0][rows, :].astype(f32)
    for ref in refs[1:]:
        total = total + ref[rows, :].astype(f32)
    return total


def mlp_step_kernel(dims, count, *refs):
    grads = refs[:count]
    (um_ref, uf_ref, us_ref, dm_ref, df_ref, ds_ref,
     u1_ref, u2_ref, ustep_ref, d1_ref, d2_ref, dstep_ref, line_ref) = refs[count:]
    rows, cols, sub, lanes = dims
    size = sub * rows + cols
    sums = [jnp.zeros((1, 1), f32) for _ in range(4)]
    for j in range(CHUNKS):
        for h in range(sub):
            start = j * size + h * rows
            at = (slice(None), slice((h * CHUNKS + j) * lanes, (h * CHUNKS + j + 1) * lanes))
            first, second, way = moments(
                add_up(grads, slice(start, start + rows)), uf_ref[at], us_ref[at]
            )
            step = way + weight_decay * um_ref[at]
            u1_ref[at], u2_ref[at], ustep_ref[at] = first, second, step
            sums[0] += square_sum(um_ref[at])
            sums[2] += square_sum(step)
        start = j * size + sub * rows
        at = (slice(j * lanes, (j + 1) * lanes), slice(None))
        first, second, way = moments(
            add_up(grads, slice(start, start + cols)).T, df_ref[at], ds_ref[at]
        )
        step = way + weight_decay * dm_ref[at]
        d1_ref[at], d2_ref[at], dstep_ref[at] = first, second, step
        sums[1] += square_sum(dm_ref[at])
        sums[3] += square_sum(step)
    line_ref[...] = lane_line({4: sums[0], 5: sums[1], 10: sums[2], 11: sums[3]})


def attn_step_kernel(count, fast, *refs):
    grads = refs[:count]
    (m_ref, f_ref, s_ref, line_ref, one_ref, h_ref,
     m1_ref, m2_ref, step_ref, out_ref, all_ref) = refs[count:]
    rows = m_ref.shape[1]
    tiles = one_ref.shape[1] // SPAN
    values = {}
    for m in range(4):
        first, second, way = moments(
            add_up(grads, slice(m * rows, (m + 1) * rows)), f_ref[m], s_ref[m]
        )
        step = way + weight_decay * m_ref[m]
        m1_ref[m], m2_ref[m], step_ref[m] = first, second, step
        values[m] = square_sum(m_ref[m])
        values[6 + m] = square_sum(step)
    all_ref[...] = jnp.zeros_like(all_ref)
    for k in range(2):
        for t in range(tiles):
            all_ref[k * tiles + t : k * tiles + t + 1, :] = one_ref[
                k : k + 1, t * SPAN : (t + 1) * SPAN
            ]
    at = 2 * tiles
    if fast:
        used = h_ref.shape[0] - 8
        piece = h_ref[used : used + 1, :] + h_ref[used + 1 : used + 2, :]
        high = piece.astype(b16).astype(f32)
        all_ref[at : at + 1, :] = high
        all_ref[at + 1 : at + 2, :] = piece - high
    line = lane_line(values) + line_ref[...]
    for k in range(3):
        piece = line.astype(b16).astype(f32)
        all_ref[at + 2 + k : at + 3 + k, :] = piece
        line = line - piece
    message = all_ref[...].astype(b16)
    for k in range(out_ref.shape[0]):
        out_ref[k] = message


def final_kernel(
    groups, fast, every_ref, two_ref, am_ref, as_ref, um_ref, us_ref, dm_ref, ds_ref, ln_ref, lf_ref, ls_ref,
    an_ref, ac_ref, un_ref, uc_ref, dn_ref, dc_ref, l1_ref, l2_ref, ln_new_ref, norms_ref,
    all_ref, grad_ref,
):
    width = ln_ref.shape[1]
    tiles = width // SPAN
    at = 2 * tiles
    total = None
    for b in range(every_ref.shape[0] // groups):
        part = every_ref[b * groups].astype(f32)
        for k in range(b * groups + 1, (b + 1) * groups):
            part = part + every_ref[k].astype(f32)
        if fast:
            k, t = divmod(b, tiles)
            grad_ref[2 + k : 3 + k, t * SPAN : (t + 1) * SPAN] = (
                part[at : at + 1, :] + part[at + 1 : at + 2, :]
            )
        total = part if total is None else total + part
    all_ref[...] = total
    for k in range(2):
        for t in range(tiles):
            grad_ref[k : k + 1, t * SPAN : (t + 1) * SPAN] = all_ref[
                k * tiles + t : k * tiles + t + 1, :
            ]
    if not fast:
        grad_ref[2:4, :] = two_ref[0:2, :]
    line = all_ref[at + 2 : at + 3, :] + all_ref[at + 3 : at + 4, :] + all_ref[at + 4 : at + 5, :]
    roots = jnp.sqrt(line)
    norms_ref[0:1, :] = roots[:, 0:6]
    norms_ref[1:2, :] = roots[:, 6:12]
    lane = lax.broadcasted_iota(jnp.int32, line.shape, 1)

    def rate(k):
        weight = jnp.sum(jnp.where(lane == k, roots, 0.0), 1, keepdims=True)
        square = jnp.sum(jnp.where(lane == 6 + k, line, 0.0), 1, keepdims=True)
        return matrix_rate * (weight / jnp.sqrt(square + epsilon))

    for m in range(4):
        new = am_ref[m] - rate(m) * as_ref[m]
        an_ref[m] = new
        ac_ref[m] = new.astype(b16)
    new = um_ref[...] - rate(4) * us_ref[...]
    un_ref[...] = new
    uc_ref[...] = new.astype(b16)
    new = dm_ref[...] - rate(5) * ds_ref[...]
    dn_ref[...] = new
    dc_ref[...] = new.astype(b16)
    first, second, way = moments(grad_ref[...], lf_ref[...], ls_ref[...])
    l1_ref[...], l2_ref[...] = first, second
    ln_new_ref[...] = ln_ref[...] - vector_rate * way


def fast_mesh(nb, ng, width):
    return nb == 8 and ng == 4 and width // ng == SPAN


def shift(values, by, ng):
    return lax.ppermute(values, "group", [(j, (j + by) % ng) for j in range(ng)])


def cross(values, bit, nb):
    return lax.ppermute(values, "blk", [(j, j ^ bit) for j in range(nb)])


def put(buffer, piece, at):
    return lax.dynamic_update_slice(buffer, piece[None], (at,) + (0,) * piece.ndim)


def take(buffer, at):
    return lax.dynamic_index_in_dim(buffer, at, 0, keepdims=False)


def gather_group(piece, z, ng):
    out = put(jnp.zeros((ng,) + piece.shape, piece.dtype), piece, z)
    for by in range(1, ng):
        out = put(out, shift(piece, by, ng), (z - by) % ng)
    return out.reshape((-1,) + piece.shape[1:])


def gather_plane(piece, nb):
    return [piece] + [cross(piece, 2 * move, nb) for move in range(1, nb // 2)]


def gather_cut(piece, cuts, z, ng):
    near, far = shift(piece, 1, ng), shift(piece, ng - 1, ng)
    came = [
        (piece, z), (near, (z - 1) % ng), (far, (z + 1) % ng), (shift(near, 1, ng), (z - 2) % ng)
    ]
    outs = []
    for start, stop in cuts:
        out = jnp.zeros((ng, stop - start, piece.shape[1]), piece.dtype)
        for part, at in came:
            out = put(out, part[start:stop], at)
        outs.append(out.reshape(-1, piece.shape[1]))
    return outs


def other_core(pieces, nb):
    return [cross(piece, 1, nb) for piece in pieces]


def body(
    tokens, cotangent, lengths, ln_params, attn_master, attn_first, attn_second,
    up_master, up_first, up_second, down_master, down_first, down_second, ln_first, ln_second,
    *, nb, ng,
):
    seqs, tok, width = tokens.shape
    spans = tok // SPAN
    tiles = width // SPAN
    amount = nb * spans
    rows, cols = attn_master.shape[1:]
    ff_rows = down_master.shape[0]
    sub = nb // ng
    lanes = ff_rows // CHUNKS
    inner = nb * lanes
    places = nb // 2
    size = sub * rows + cols
    attn_rows = ng * 4 * rows
    half = -(-(seqs * spans * tiles + 8) // 16) * 16
    b, z = lax.axis_index("blk").astype(jnp.int32), lax.axis_index("group").astype(jnp.int32)
    core = b % 2
    fast = fast_mesh(nb, ng, width)
    scal = jnp.concatenate([jnp.stack([b, z]), lengths.astype(jnp.int32)])
    shape = jax.ShapeDtypeStruct

    def like(dtype, *tail):
        return shape((seqs,) + tail, dtype)

    def gather_any(piece, over=("blk", "group")):
        every = lax.all_gather(piece, over)
        every = every.reshape((places, 2, -1) + piece.shape[1:])
        every = jnp.swapaxes(every, 0, 1)
        own, other = take(every, core), take(every, 1 - core)
        return [own[p] for p in range(places)], [other[p] for p in range(places)]

    def reduce_any(keep, send, blocks):
        both = jnp.stack([jnp.where(core == 0, keep, send), jnp.where(core == 0, send, keep)])
        both = jnp.swapaxes(both, 0, 1).reshape((nb,) + keep.shape[1:])
        mine = lax.psum_scatter(both, "blk", scatter_dimension=0)
        if not blocks:
            return mine.astype(f32)
        mine = mine.reshape((ng, -1) + mine.shape[1:])
        return lax.psum_scatter(mine, "group", scatter_dimension=0).astype(f32)

    def flat(call, name, outs, scratch, work, *args, scalar=False):
        return pl.pallas_call(
            call,
            in_specs=[scalars()] * scalar + [whole()] * (len(args) - scalar),
            out_specs=[whole()] * len(outs),
            out_shape=outs,
            scratch_shapes=scratch,
            compiler_params=pltpu.CompilerParams(vmem_limit_bytes=16 * MIB),
            cost_estimate=work,
            name=name,
        )(*args)

    pack_dims = (rows, cols, sub, lanes)

    attn_piece = attn_master[:3].astype(b16).reshape(3 * rows, cols)
    if fast:
        attn_z = gather_group(attn_piece, z, ng)
    normed, rider = flat(
        functools.partial(
            over_seqs, functools.partial(prep_kernel, seqs), (False, True, False, True, False, False), True
        ),
        "prep", [like(b16, tok, width), shape((2 * half, SPAN), b16)],
        [pltpu.VMEM((half, SPAN), f32)], cost(4e7, 2 * seqs * tok * width * 2),
        scal, tokens, ln_params, scalar=True,
    )

    def gate(pieces, *deps):
        return flat(
            functools.partial(gate_kernel, len(pieces)), "gate",
            [shape(piece.shape, b16) for piece in pieces], [], cost(1e6, 1e6), *pieces, *deps,
        )

    def everywhere(piece):
        return lax.all_gather(piece, ("blk", "group"))

    if fast:
        message = jnp.concatenate([attn_z, rider], 0)
        attn_own = gather_plane(message, nb)
        attn_bufs = attn_own + other_core(attn_own, nb)
        pack_out = shape((rows + CHUNKS * size, lanes), b16)
        piece = pl.pallas_call(
            functools.partial(pack_kernel, pack_dims),
            grid=(1,),
            in_specs=[
                pl.BlockSpec((1, rows, cols), lambda i: (3, 0, 0)), fixed(*up_master.shape),
                fixed(*down_master.shape), whole(),
            ],
            out_specs=fixed(*pack_out.shape),
            out_shape=pack_out,
            cost_estimate=cost(1e6, 1e6),
            name="pack",
        )(attn_master, up_master, down_master, attn_piece)
        mlp_z, late_z = gather_cut(piece, [(0, rows + size), (rows + size, rows + 2 * size)], z, ng)
        mlp_own = gather_plane(mlp_z, nb)
        dep = mlp_z
    else:
        out_piece = attn_master[3].astype(b16)
        up_low = up_master.astype(b16).reshape(rows, sub, CHUNKS, lanes)
        down_low = down_master.astype(b16).T.reshape(cols, CHUNKS, lanes)
        attn_own, attn_other = gather_any(attn_piece)
        ride_own, ride_other = gather_any(rider, "blk")
        attn_bufs = attn_own + attn_other + ride_own + ride_other
        mlp_bufs = []
        for j in range(CHUNKS):
            piece = [jnp.swapaxes(up_low[:, :, j], 0, 1).reshape(sub * rows, lanes), down_low[:, j]]
            mlp_bufs.append([everywhere(jnp.concatenate(piece, 0))])
        mlp_bufs[0].append(everywhere(out_piece))
        dep = ln_params

    dims = (ng, rows, cols, width)
    act_bytes = seqs * tok * width
    q, k, v, ks, vs, nsum, lse, mixed, w_attn, token = pl.pallas_call(
        functools.partial(forward_kernel, dims, fast, places),
        grid=(seqs,),
        in_specs=[scalars(), per_step(tok, width)] + [whole()] * (len(attn_bufs) + 1),
        out_specs=[
            per_step(tok, width), per_step(tok, width), per_step(tok, width),
            per_step(amount, width), per_step(amount, width), per_step(amount, width),
            per_step(spans, tiles, 2 * SPAN),
            pl.BlockSpec((width, tok), lambda i: (0, i)),
            whole(), fixed(8, SPAN),
        ],
        out_shape=[
            like(b16, tok, width), like(b16, tok, width), like(b16, tok, width),
            like(b16, amount, width), like(b16, amount, width), like(b16, amount, width),
            like(f32, spans, tiles, 2 * SPAN),
            shape((width, seqs * tok), b16),
            shape((width, 3 * width), b16), shape((8, SPAN), f32),
        ],
        scratch_shapes=[
            pltpu.VMEM((2, places, half, SPAN), f32), pltpu.VMEM((amount, width), f32)
        ],
        compiler_params=params(16),
        cost_estimate=cost(8e9, act_bytes * 14),
        name="forward",
    )(scal, normed, *attn_bufs, dep)

    if fast:
        mlp_own[1:] = gate(mlp_own[1:], token)
        late_own = gather_plane(gate([late_z], token)[0], nb)
        mlp_bufs = [mlp_own + other_core(mlp_own, nb)]
        dep = late_own[0]
    mlp_dims = (ng, rows, cols, sub, lanes)
    mlp_out = shape((places, ng * size, lanes), b16)
    every_row = seqs * tok
    tile = every_row // ROW_STEPS
    flat_tokens, flat_cot = tokens.reshape(-1, width), cotangent.reshape(-1, width)
    by_rows = pl.BlockSpec((tile, width), lambda i: (i, 0))
    rows_out = shape((every_row, width), b16)
    keeps, sends = [], []
    y = gm = x2 = mid = wo = None
    for j in range(CHUNKS):
        first, last = j == 0, j == CHUNKS - 1
        if fast and not first:
            late_own[1:] = gate(late_own[1:], token)
            mlp_bufs.append(late_own + other_core(late_own, nb))
        if first:
            args = [scal, mixed, flat_tokens, ln_params, flat_cot]
            in_specs = [
                scalars(), pl.BlockSpec((width, tile), lambda i: (0, i)), by_rows, fixed(4, width),
                by_rows,
            ]
        else:
            args, in_specs = [scal, mid, flat_cot], [scalars(), by_rows, by_rows]
        args += [*mlp_bufs[j], dep]
        in_specs += [whole()] * (len(mlp_bufs[j]) + 1)
        outs = [(by_rows, rows_out), (by_rows, rows_out), (whole(), mlp_out), (whole(), mlp_out)]
        if first:
            outs = [
                (by_rows, rows_out), (by_rows, rows_out), (whole(), shape((width, width), b16)),
                (fixed(8, SPAN), shape((8, SPAN), f32)),
            ] + outs
        if last:
            args += [x2, y, gm]
            in_specs += [by_rows] * 3
        *more, y, gm, keep, send = pl.pallas_call(
            functools.partial(mlp_kernel, mlp_dims, fast, places, first, last),
            grid=(ROW_STEPS,),
            in_specs=in_specs,
            out_specs=[spec for spec, _ in outs],
            out_shape=[out for _, out in outs],
            scratch_shapes=[
                pltpu.VMEM((width, inner), b16), pltpu.VMEM((width, inner), b16),
                pltpu.VMEM((width, inner), f32), pltpu.VMEM((width, inner), f32),
            ],
            compiler_params=params(24),
            cost_estimate=cost(9e9, act_bytes * 20),
            name="mlp",
        )(*args)
        if first:
            x2, mid, wo, token = more
        keeps.append(keep)
        sends.append(send)
    block_out = y.reshape(tokens.shape)
    if fast:
        gets = [cross(send, 1, nb) for send in sends]

    def middle(k, *more):
        rows_k = pl.BlockSpec((every_row // 2, width), lambda i: (k, 0))
        return pl.pallas_call(
            functools.partial(middle_kernel, bool(more)),
            grid=(1,),
            in_specs=[
                rows_k, rows_k, rows_k, pl.BlockSpec((width, every_row // 2), lambda i: (0, k)),
                whole(), fixed(4, width),
            ]
            + [anywhere(), anywhere(), fixed(width, width), fixed(8, width), anywhere()][: len(more)],
            out_specs=[rows_k, rows_k, fixed(width, width), fixed(8, width)],
            out_shape=[rows_out, rows_out, shape((width, width), f32), shape((8, width), f32)],
            input_output_aliases={6: 0, 7: 1} if more else {},
            compiler_params=params(24),
            cost_estimate=cost(3e9, act_bytes * 14),
            name="middle",
        )(gm, flat_cot, x2, mixed, wo, ln_params, *more)

    halfway = middle(0)

    block = shape((ng * size, lanes), f32)
    block_low = shape((ng * size, lanes), b16)
    two, two_low = shape((2,) + block.shape, f32), shape((2,) + block.shape, b16)
    if fast:
        stay_a, out_a, stay_b, out_b = flat(
            halves_kernel, "halves", [two, two_low, two, two_low], [], cost(2e6, 16e6),
            scal, *keeps, *gets, halfway[3], scalar=True,
        )
        get_a, get_b = cross(out_a, 2, nb), cross(out_b, 4, nb)
        dep = stay_a
    else:
        dep = ln_params
    gx2, grad_mixed, dwo, ln_two = middle(1, *halfway, dep)
    gx2, grad_mixed = gx2.reshape(tokens.shape), grad_mixed.reshape(tokens.shape)

    dqkv, key_part, value_part, h_part = pl.pallas_call(
        functools.partial(backward_kernel, places),
        grid=(seqs,),
        in_specs=[
            scalars(), per_step(tok, width),
            per_step(tok, width), per_step(tok, width), per_step(tok, width),
            per_step(spans, tiles, 2 * SPAN), per_step(amount, width), per_step(amount, width),
            whole(), anywhere(),
        ],
        out_specs=[
            per_step(tok, 3 * width), per_step(amount, width), per_step(amount, width), whole()
        ],
        out_shape=[
            like(b16, tok, 3 * width), like(b16, amount, width), like(b16, amount, width),
            shape((2, places, half, SPAN), f32),
        ],
        scratch_shapes=[pltpu.VMEM((width, tok), b16)],
        compiler_params=params(16),
        cost_estimate=cost(14e9, act_bytes * 24),
        name="backward",
    )(scal, grad_mixed, q, k, v, lse, ks, vs, w_attn, dep)

    if fast:
        own_a, out_a, own_b, out_b = flat(
            turn_kernel, "turn", [block, block_low] * 2, [], cost(1e6, 10e6),
            stay_a, get_a, stay_b, get_b,
        )
        mlp_parts = [own_a, cross(out_a, 4, nb), own_b, cross(out_b, 2, nb)]
        dep = own_a
    tail = half if fast else 0
    outs = [shape((places, attn_rows + tail, cols), b16)] * 2
    if not fast:
        outs += [shape((places, half, SPAN), b16)] * 2
    (dw,) = flat(
        grads_kernel, "grads", [shape((width, 3 * width), f32)],
        [pltpu.VMEM((width, seqs * tok), b16)], cost(1e6, 1e5),
        normed.reshape(-1, width), dqkv.reshape(-1, 3 * width), nsum.reshape(-1, width),
        key_part.reshape(-1, width), value_part.reshape(-1, width),
    )
    parts = flat(
        functools.partial(cut_kernel, dims, fast), "cut", outs, [], cost(1e6, 1e5),
        scal, dw, dwo, h_part, ln_two, dep, scalar=True,
    )

    def collect(terms, sizes, count, tail):
        outs = [shape((sum(sizes), SPAN), f32)] + [shape((sum(sizes), SPAN), b16)] * 3
        if tail:
            outs.append(shape((tail, SPAN), f32))
        return flat(
            functools.partial(collect_kernel, sizes, count), "collect", outs, [], cost(1e6, 4e6),
            scal, *terms, scalar=True,
        )

    if fast:
        attn_low = shape((attn_rows + tail, cols), b16)
        attn_parts = flat(
            functools.partial(spread_kernel, 1), "spread",
            [shape(attn_low.shape, f32)] + [attn_low] * 3, [], cost(1e6, 4e6),
            scal, parts[0], cross(parts[1], 1, nb), scalar=True,
        )
        dep = attn_parts[0]
        attn_parts = [dep] + [cross(attn_parts[m], 2 * m, nb) for m in range(1, 4)]
    else:
        dep = parts[2]

    grad_in = pl.pallas_call(
        project_kernel,
        grid=(seqs,),
        in_specs=[per_step(tok, 3 * width), whole(), anywhere()],
        out_specs=per_step(tok, width),
        out_shape=like(b16, tok, width),
        compiler_params=params(16),
        cost_estimate=cost(3e9, act_bytes * 8),
        name="project",
    )(dqkv, w_attn, dep)

    if fast:
        mlp_sums = collect(mlp_parts + [grad_in], (size,) * CHUNKS, 2, 0)
        mlp_sums = [mlp_sums[0]] + [shift(mlp_sums[by], by, ng) for by in range(1, ng)]
        *attn_sums, own = collect(attn_parts + [grad_in], (4 * rows,), 4, half)
        attn_sums = [attn_sums[0]] + [shift(attn_sums[by], by, ng) for by in range(1, ng)]
    else:
        own = reduce_any(parts[2], parts[3], False)
        attn_sums = [reduce_any(parts[0], parts[1], True)]
        mlp_sums = [
            jnp.concatenate([reduce_any(keep, send, True) for keep, send in zip(keeps, sends)], 0)
        ]
        ln_two = lax.psum(ln_two, ("blk", "group"))

    input_grad, ln_one = pl.pallas_call(
        input_kernel,
        grid=(seqs,),
        in_specs=[
            scalars(), per_step(tok, width), per_step(tok, width), per_step(tok, width),
            whole(), fixed(4, width),
        ],
        out_specs=[per_step(tok, width), fixed(8, width)],
        out_shape=[like(f32, tok, width), shape((8, width), f32)],
        compiler_params=params(16),
        cost_estimate=cost(1e8, act_bytes * 10),
        name="input",
    )(scal, grad_in, gx2, tokens, own, ln_params)

    attn_shape = shape(attn_master.shape, f32)
    up_shape, down_shape = shape(up_master.shape, f32), shape(down_master.shape, f32)
    up_moment1, up_moment2, up_step, down_moment1, down_moment2, down_step, line = flat(
        functools.partial(mlp_step_kernel, (rows, cols, sub, lanes), len(mlp_sums)),
        "mlp_step",
        [up_shape] * 3 + [down_shape] * 3 + [shape((1, SPAN), f32)],
        [],
        cost(1e6, 2e6),
        *mlp_sums, up_master, up_first, up_second, down_master, down_first, down_second,
    )
    lines = -(-(2 * tiles + 5) // 16) * 16
    attn_moment1, attn_moment2, attn_step, message = flat(
        functools.partial(attn_step_kernel, len(attn_sums), fast),
        "attn_step",
        [attn_shape] * 3 + [shape((nb * ng, lines, SPAN), b16)],
        [pltpu.VMEM((lines, SPAN), f32)],
        cost(1e6, 2e6),
        *attn_sums, attn_master, attn_first, attn_second, line, ln_one, own,
    )
    every = lax.all_to_all(message, ("blk", "group"), 0, 0, tiled=True)

    def low(like_this):
        return shape(like_this.shape, b16)

    ln_shape = shape(ln_params.shape, f32)
    (attn_new, attn_copy, up_new, up_copy, down_new, down_copy,
     ln_moment1, ln_moment2, ln_new, norms) = flat(
        functools.partial(final_kernel, ng, fast),
        "final",
        [attn_shape, low(attn_master), up_shape, low(up_master), down_shape, low(down_master)]
        + [ln_shape] * 3 + [shape((2, 6), f32)],
        [pltpu.VMEM((lines, SPAN), f32), pltpu.VMEM((4, width), f32)],
        cost(1e6, 2e6),
        every, ln_two, attn_master, attn_step, up_master, up_step, down_master, down_step,
        ln_params, ln_first, ln_second,
    )
    return (
        block_out, input_grad,
        attn_moment1, attn_moment2, attn_new, attn_copy,
        up_moment1, up_moment2, up_new, up_copy,
        down_moment1, down_moment2, down_new, down_copy,
        ln_moment1, ln_moment2, ln_new, norms,
    )


def solution(mesh):
    seq_spec = P("group", "blk", None)
    attn_spec = P(None, "blk", "group")
    flat_spec = P("blk", "group")
    return jax.shard_map(
        functools.partial(body, nb=mesh.shape["blk"], ng=mesh.shape["group"]),
        mesh=mesh,
        in_specs=(seq_spec, seq_spec, P("group"), P())
        + (attn_spec,) * 3
        + (flat_spec,) * 6
        + (P(), P()),
        out_specs=(seq_spec, seq_spec)
        + (attn_spec,) * 4
        + (flat_spec,) * 8
        + (P(),) * 4,
        check_vma=False,
    )
```
